32 devices in a mesh: pipe: 2 (over x), dp: 4 (over z), tensor: 4 (over y, core).
Axes of the slice: x: 2, y: 2, z: 4, core: 2. Of those that a mesh axis runs over, the one named last changes fastest.
Arguments:
- image_side: bfloat16 [2, 32, 197, 768], P('pipe', 'dp'), may hold values from -6 to 6
- text_side: bfloat16 [2, 8, 512, 768], P('pipe', 'dp'), may hold values from -6 to 6
- caption_lengths: int32 [8, 8], P('dp'), may hold values from 1 to 128, 512 in all within a row
- norm_gains: float32 [2, 2, 768], P('pipe'), may hold values from 0.25 to 1.75
- norm_shifts: float32 [2, 2, 768], P('pipe'), may hold values from -1.8 to 1.8
- w_qkv: bfloat16 [2, 768, 3, 768], P('pipe', None, None, 'tensor'), may hold values from -0.21875 to 0.21875
- bias_qv: float32 [2, 2, 768], P('pipe', None, 'tensor'), may hold values from -3 to 3
- w_proj: bfloat16 [2, 768, 768], P('pipe', 'tensor'), may hold values from -0.625 to 0.625
- out_bias: float32 [2, 2, 768], P('pipe'), may hold values from -1.8 to 1.8
- w_up: bfloat16 [2, 768, 3072], P('pipe', None, 'tensor'), may hold values from -0.21875 to 0.21875
- bias_up: float32 [2, 3072], P('pipe', 'tensor'), may hold values from -3 to 3
- w_down: bfloat16 [2, 3072, 768], P('pipe', 'tensor'), may hold values from -0.109375 to 0.109375
Outputs:
- image_result: bfloat16 [2, 32, 197, 768], P('pipe', 'dp')
- text_result: bfloat16 [2, 8, 512, 768], P('pipe', 'dp')
- gains_grad: float32 [2, 2, 768], P('pipe')
- shifts_grad: float32 [2, 2, 768], P('pipe')
- qkv_grad: float32 [2, 768, 3, 768], P('pipe', 'dp', None, 'tensor')
- bias_qv_grad: float32 [2, 2, 768], P('pipe', None, 'tensor')
- proj_grad: float32 [2, 768, 768], P('pipe', 'tensor', 'dp')
- out_bias_grad: float32 [2, 2, 768], P('pipe')
- up_grad: float32 [2, 768, 3072], P('pipe', 'dp', 'tensor')
- bias_up_grad: float32 [2, 3072], P('pipe', 'tensor')
- down_grad: float32 [2, 3072, 768], P('pipe', 'tensor', 'dp')
The draws below stay inside these ranges and needn't reach their ends.
Inputs may be any that keep to these rules, and one draw needn't show every extreme that they name: `caption_lengths`: each row holds the lengths of the 8 captions packed into one text block; they sum to 512 and the largest is exactly 128.
All inputs are finite; a program needn't handle non-finite values.
Results may differ from the reference program's by a relative error of at most 0.014.
Values may be sent and summed in bfloat16 or wider, within the bound.
A program may use at most 192 MiB of HBM per device.

```python
import math
import jax
import jax.numpy as jnp
import numpy as np
from jax import lax

D = 768
HEADS = 12
HEAD_DIM = 64
FF = 3072
IMG_LEN = 197
TXT_LEN = 512
CAPS = 8
SECTIONS = 2
CAP_MOST = 128
IMAGES = 32
BLOCKS = 8


def level_of(own_key, extent, split, least, top_value):
    def one(axis_at, shards_of):
        draws = jax.random.uniform(jax.random.fold_in(jax.random.fold_in(own_key, 6), axis_at), (shards_of,), jnp.float32, least / len(split), top_value / len(split))
        return jnp.repeat(jnp.exp(draws), extent[axis_at] // shards_of).reshape((-1,) + (1,) * (len(extent) - axis_at - 1))

    loudness = one(*split[0])
    for cut in split[1:]:
        loudness = loudness * one(*cut)
    return loudness


def profile(amount, total, limit, slope):
    portions = [(1 << 20) // math.isqrt(grade ** slope) + 1 for grade in range(2, amount + 1)]
    surplus, holding = total - limit - (amount - 1), [1] * (amount - 1)
    while surplus > 0:
        candidates = [i for i in range(amount - 1) if holding[i] < limit]
        pool, budget = sum([portions[i] for i in candidates]), surplus
        for i in candidates:
            more = min(limit - holding[i], max(1, budget * portions[i] // pool), surplus)
            holding[i] = holding[i] + more
            surplus = surplus - more
    return np.array([limit] + holding)


def uneven(stream_key, count, total, limit, slope):
    if count == 2:
        one = jax.random.randint(stream_key, (), max(1, total - limit), min(limit, total - 1) + 1)
        return jnp.stack([one, total - one])
    sizes = jnp.asarray(profile(count, total, limit, slope), jnp.int32)
    couples = (count - 1) // 2
    source_of, sink = sizes[1:1 + 2 * couples:2], sizes[2:2 + 2 * couples:2]
    room = jnp.minimum(source_of - 1, limit - sink)
    moved = jax.random.randint(jax.random.fold_in(stream_key, 1), (couples,), 0, 1 << 20) % (room + 1)
    sizes = sizes.at[1:1 + 2 * couples:2].set(source_of - moved).at[2:2 + 2 * couples:2].set(sink + moved)
    return sizes[jax.random.permutation(jax.random.fold_in(stream_key, 2), count)]


def bell_draw(rng, dims, scale, reach, pieces=(), kind=jnp.bfloat16):
    entries = jax.random.normal(rng, dims, jnp.float32) * scale
    if len(pieces) > 0:
        entries = level_of(rng, dims, pieces, -0.22, 0.18) * entries
    return jnp.clip(entries, min=-reach, max=reach).astype(kind)


def setup_inputs(seed: int = 0) -> dict:
    streams_of = jax.random.split(jax.random.key(seed), 13)
    return {
        "image_side": bell_draw(streams_of[0], (SECTIONS, IMAGES, IMG_LEN, D), 1.0, 6.0, ((0, 2), (1, 4))),
        "text_side": bell_draw(streams_of[1], (SECTIONS, BLOCKS, TXT_LEN, D), 1.0, 6.0, ((0, 2), (1, 4))),
        "caption_lengths": jax.vmap(lambda own: uneven(own, CAPS, TXT_LEN, CAP_MOST, 2))(jax.random.split(streams_of[2], BLOCKS)).reshape((BLOCKS, CAPS)).astype(jnp.int32),
        "norm_gains": jnp.clip(1.0 + 0.15 * jax.random.normal(streams_of[3], (SECTIONS, 2, D), jnp.float32), 0.25, 1.75),
        "norm_shifts": bell_draw(streams_of[4], (SECTIONS, 2, D), 0.3, 1.8, ((0, 2),), jnp.float32),
        "w_qkv": bell_draw(streams_of[5], (SECTIONS, D, 3, D), D ** -0.5, 0.21875, ((0, 2), (3, 4))),
        "bias_qv": bell_draw(streams_of[6], (SECTIONS, 2, D), 0.5, 3.0, ((0, 2), (2, 4)), jnp.float32),
        "w_proj": bell_draw(streams_of[7], (SECTIONS, D, D), (D // 8) ** -0.5, 0.625, ((0, 2), (1, 4))),
        "out_bias": bell_draw(streams_of[8], (SECTIONS, 2, D), 0.3, 1.8, ((0, 2),), jnp.float32),
        "w_up": bell_draw(streams_of[9], (SECTIONS, D, FF), D ** -0.5, 0.21875, ((0, 2), (2, 4))),
        "bias_up": bell_draw(streams_of[10], (SECTIONS, FF), 0.5, 3.0, ((0, 2), (1, 4)), jnp.float32),
        "w_down": bell_draw(streams_of[11], (SECTIONS, FF, D), FF ** -0.5, 0.109375, ((0, 2), (1, 4))),
    }


@jax.custom_vjp
def low(v):
    return lax.optimization_barrier(v.astype(jnp.bfloat16)).astype(jnp.float32)

@jax.custom_vjp
def low_back(v):
    return v

def low_keep(v):
    return (low(v), None)

def low_pass(kept, grad):
    return (grad,)

def back_keep(v):
    return (v, None)

def back_low(kept, grad):
    return (low(grad),)
low.defvjp(low_keep, low_pass)
low_back.defvjp(back_keep, back_low)

def to_wide(array_in):
    return array_in.astype(jnp.float32)

def both_ways(array_in):
    return low_back(low(array_in))

def product(left_op, right_op):
    return jnp.dot(left_op, right_op, precision=lax.Precision.HIGHEST)

def norm_rows(rows_in, gain_row, shift_row):
    centre = rows_in - lax.optimization_barrier(jnp.mean(rows_in, axis=-1, keepdims=True))
    spread = lax.optimization_barrier(jnp.mean(centre * centre, axis=-1, keepdims=True))
    return centre * lax.rsqrt(spread + 1e-06) * gain_row + shift_row

def caption_mask(lengths, length):
    bounds = jnp.cumsum(lengths, axis=-1)
    places = jnp.arange(length, dtype=jnp.int32)
    segment = lax.optimization_barrier(jnp.sum((places[None, :, None] >= bounds[:, None, :]).astype(jnp.int32), axis=-1))
    return segment[:, :, None] == segment[:, None, :]

def attend_item(parts):
    queries, key_rows, value_rows, allowed = parts
    scores = low_back(jnp.einsum('qhe,khe->hqk', queries, key_rows, precision=lax.Precision.HIGHEST))
    scores = jnp.where(allowed[None], scores, -1000000000.0)
    attn_weights = low(jax.nn.softmax(scores, axis=-1))
    return jnp.einsum('hqk,khe->qhe', attn_weights, value_rows, precision=lax.Precision.HIGHEST)

def layer_pass(layer_params, stream, allowed):
    gain_pair, shift_pair, w_qkv, bias_qv, w_proj, out_bias, w_up, bias_up, w_down = layer_params
    number, length, model_width = stream.shape
    flat_rows = stream.reshape(number * length, model_width)
    normed = low(norm_rows(flat_rows, gain_pair[0], shift_pair[0]))
    queries = both_ways((product(normed, w_qkv[:, 0, :]) + bias_qv[0]) * HEAD_DIM ** (-0.5))
    key_rows = both_ways(product(normed, w_qkv[:, 1, :]))
    value_rows = both_ways(product(normed, w_qkv[:, 2, :]) + bias_qv[1])
    head_shape = (number, length, HEADS, HEAD_DIM)
    mixture = lax.map(jax.checkpoint(attend_item), (queries.reshape(head_shape), key_rows.reshape(head_shape), value_rows.reshape(head_shape), allowed))
    mixture = both_ways(mixture.reshape(number * length, model_width))
    residual = flat_rows + low_back(product(mixture, w_proj)) + out_bias[0]
    normed_two = low(norm_rows(residual, gain_pair[1], shift_pair[1]))
    up_part = low_back(product(normed_two, w_up) + bias_up)
    hidden = low(jax.nn.gelu(up_part, approximate=False))
    result = residual + low_back(product(hidden, w_down)) + out_bias[1]
    return result.reshape(number, length, model_width)

def reference(image_side, text_side, caption_lengths, norm_gains, norm_shifts, w_qkv, bias_qv, w_proj, out_bias, w_up, bias_up, w_down):
    params = (to_wide(norm_gains), to_wide(norm_shifts), to_wide(w_qkv), to_wide(bias_qv), to_wide(w_proj), to_wide(out_bias), to_wide(w_up), to_wide(bias_up), to_wide(w_down))
    image_in = to_wide(image_side[0])
    text_in = to_wide(text_side[0])
    image_allow = jnp.ones((image_in.shape[0], IMG_LEN, IMG_LEN), dtype=jnp.bool_)
    text_allow = caption_mask(caption_lengths, TXT_LEN)

    def forward(layer_params, image_stream, text_stream):
        image_params = tuple((member[0] for member in layer_params))
        text_params = tuple((member[1] for member in layer_params))
        return (layer_pass(image_params, image_stream, image_allow), layer_pass(text_params, text_stream, text_allow))
    (image_out, text_out), pullback = jax.vjp(forward, params, image_in, text_in)
    param_grads, image_grad, text_grad = pullback((to_wide(image_side[1]), to_wide(text_side[1])))
    image_result = jnp.stack([image_grad, image_out]).astype(jnp.bfloat16)
    text_result = jnp.stack([text_grad, text_out]).astype(jnp.bfloat16)
    return (image_result, text_result, param_grads[0], param_grads[1], param_grads[2], param_grads[3], param_grads[4], param_grads[5], param_grads[6], param_grads[7], param_grads[8])
```

```python
from functools import partial

import jax
import jax.numpy as jnp
from jax import lax
from jax.experimental import pallas as pl
from jax.experimental.pallas import tpu as pltpu
from jax.sharding import PartitionSpec as P

F32 = jnp.float32
BF16 = jnp.bfloat16
BY_MESH = pl.DeviceIdType.MESH
HEAD = 64
HALF = 3
HEADS = 2 * HALF
WIDE = HALF * HEAD
EPSILON = 1e-06
MASKED = -1000000000.0
CHUNKS = 4
STRIP = 16
QKV = 640
MIX = 256
TILE = 256

K_IN, K_A, K_B, K_C, K_Y1, K_Y2, K_YT, K_OI, K_OT, K_T1, K_T2, K_W, K_S, K_G, K_Z = range(15)
N_KINDS = K_Z + 5


def dot(a, b):
    return lax.dot_general(a, b, (((1,), (0,)), ((), ())), preferred_element_type=F32)


def dot_nt(a, b):
    return lax.dot_general(a, b, (((1,), (1,)), ((), ())), preferred_element_type=F32)


def dot_tn(a, b):
    return lax.dot_general(a, b, (((0,), (0,)), ((), ())), preferred_element_type=F32)


def loop(count, body):
    def step(j, carry):
        body(j)
        return carry

    lax.fori_loop(0, count, step, 0)


def unit_of(rows):
    centre = rows - jnp.mean(rows, axis=-1, keepdims=True)
    inverse = lax.rsqrt(jnp.mean(centre * centre, axis=-1, keepdims=True) + EPSILON)
    return centre * inverse, inverse


def norm_back(grad, unit, inverse, gain):
    scaled = grad * gain
    first = jnp.mean(scaled, axis=-1, keepdims=True)
    second = jnp.mean(scaled * unit, axis=-1, keepdims=True)
    return inverse * (scaled - first - unit * second)


def gelu_pair(u):
    cdf = 0.5 * (1.0 + lax.erf(u * (0.5**0.5)))
    pdf = jnp.exp(u * u * -0.5) * 0.3989422804014327
    return u * cdf, cdf + u * pdf


def fold(rows):
    return jnp.sum(rows.reshape(rows.shape[0] // 8, 8, rows.shape[1]), axis=0)


def layers_kernel(
    rows_i, rows_t, keys_i, dp_size, z_inside,
    img_own, txt_own, w_qkv, w_proj, w_up, w_down, small, gains, shifts, outb, seg_col, seg_row,
    img_out, txt_out, g_qkv, g_proj, g_up, g_down, vec_out,
    x_s, dy_s, wq_s, wp_s, wu_s, wd_s, small_s, a1_s, qkv_s, o_s, r_s, a2_s, gb_s, du_s, p_s, dkv_s, do_s,
    send_s, ra_s, rb_s, rc_s, ys_s, yt_s, y1_s, y2_s, fin_s, acc_s, vec_s, vrec_s, vall_s,
    gs_q, gs_p, gs_u, gs_d, gr_q, gr_p, gr_u, gr_d, *rest,
):
    if z_inside:
        zr_q, zr_p, zr_u, zr_d, zf_q, zf_p, zf_u, zf_d, ssem, rsem, lsem = rest
    else:
        ssem, rsem, lsem = rest
    width = x_s.shape[1]
    p, d, t = lax.axis_index("pipe"), lax.axis_index("dp"), lax.axis_index("tensor")
    core = lax.rem(t, 2)
    sib_t = t + 1 - 2 * core
    peer_t = lax.rem(t + 2, 4)
    other = 1 - p
    sib, peer = (p, d, sib_t), (p, d, peer_t)
    across, across_peer, across_sib = (other, d, t), (other, d, peer_t), (other, d, sib_t)
    offsets = range(1, dp_size) if z_inside else range(0)
    partners = [sib, peer, across, across_peer, across_sib]
    partners += [(p, lax.rem(d + k, dp_size), t) for k in offsets]

    def remote(src, dst, kind, slot, to):
        at = kind * 4 + slot
        return pltpu.make_async_remote_copy(
            src_ref=src, dst_ref=dst, send_sem=ssem.at[at], recv_sem=rsem.at[at],
            device_id=to, device_id_type=BY_MESH,
        )

    def local(src, dst, slot):
        return pltpu.make_async_copy(src, dst, lsem.at[slot])

    image_here = p == 0
    n_img = rows_i * CHUNKS
    n_txt = rows_t * CHUNKS

    wq_own = local(w_qkv, wq_s.at[:, 0:QKV], 0)
    wp_own = local(w_proj, wp_s.at[0:WIDE], 1)
    wu_own = local(w_up, wu_s.at[:, 0:width], 2)
    wd_own = local(w_down, wd_s.at[0:width], 3)
    sm_own = local(small, small_s.at[0], 4)
    img_in = local(img_own, x_s, 5)
    txt_in = local(txt_own, dy_s.at[0:n_txt], 6)
    sm_own.start()
    wq_own.start()

    @pl.when(image_here)
    def _():
        img_in.start()

    @pl.when(jnp.logical_not(image_here))
    def _():
        txt_in.start()

    wp_own.start()
    wu_own.start()
    wd_own.start()
    zero_rows = jnp.zeros((MIX - WIDE, width), BF16)
    wp_s[WIDE:MIX, :] = zero_rows
    wp_s[MIX + WIDE :, :] = zero_rows
    acc_s[...] = jnp.zeros_like(acc_s)

    barrier = pltpu.get_barrier_semaphore()
    for to in partners:
        pl.semaphore_signal(barrier, inc=1, device_id=to, device_id_type=BY_MESH)
    pl.semaphore_wait(barrier, len(partners))

    sm_sib = remote(small, small_s.at[1], K_S, 0, sib)
    wq_sib = remote(w_qkv, wq_s.at[:, QKV:], K_W, 0, sib)
    wp_sib = remote(w_proj, wp_s.at[MIX : MIX + WIDE], K_W, 1, sib)
    wu_sib = remote(w_up, wu_s.at[:, width:], K_W, 2, sib)
    wd_sib = remote(w_down, wd_s.at[width:], K_W, 3, sib)

    def x_to_text(i):
        rows = pl.ds(pl.multiple_of(i * rows_t, 16), rows_t)
        return remote(txt_own.at[rows], x_s.at[rows], K_IN, i, across)

    def dy_to_image(i):
        rows = pl.ds(pl.multiple_of(i * rows_i, 16), rows_i)
        return remote(img_own.at[rows], dy_s.at[rows], K_IN, i, across)

    @pl.when(image_here)
    def _():
        loop(CHUNKS, lambda i: x_to_text(i).start())

    sm_sib.start()
    wq_sib.start()

    @pl.when(jnp.logical_not(image_here))
    def _():
        loop(CHUNKS, lambda i: dy_to_image(i).start())

    wp_sib.start()
    wu_sib.start()
    wd_sib.start()

    own_gain = [gains[0:1, :], gains[1:2, :]]
    own_shift = [shifts[0:1, :], shifts[1:2, :]]

    g_arrays = [(gs_q, gr_q), (gs_p, gr_p), (gs_u, gr_u), (gs_d, gr_d)]

    def g_exchange(a):
        return remote(g_arrays[a][0], g_arrays[a][1], K_G, a, sib)

    def grads_pair(a, left, right, n, own_cols, sib_cols):
        mine, theirs = g_arrays[a]
        tiles = width // TILE

        def part(cols):
            def body(m):
                at = pl.ds(pl.multiple_of(m * TILE, TILE), TILE)
                return at, dot_tn(left[0:n, at], right[0:n, cols[0] : cols[1]])

            return body

        first, second = part(sib_cols), part(own_cols)

        def send_half(m):
            at, value = first(m)
            mine[at, :] = value.astype(BF16)

        loop(tiles, send_half)
        g_exchange(a).start()

        def finish():
            g_exchange(a).wait()

            def own_half(m):
                at, value = second(m)
                mine[at, :] = (value + theirs[at, :].astype(F32)).astype(BF16)

            loop(tiles, own_half)

        return finish

    z_sets = [(gs_q, zr_q, zf_q, g_qkv), (gs_p, zr_p, zf_p, g_proj), (gs_u, zr_u, zf_u, g_up), (gs_d, zr_d, zf_d, g_down)] if z_inside else []
    share = width // dp_size

    def z_copy(a, k):
        whole, landing = z_sets[a][0:2]
        to = lax.rem(d + k, dp_size)
        rows = pl.ds(pl.multiple_of(to * share, 16), share)
        return remote(whole.at[rows], landing.at[k - 1], K_Z + a, k - 1, (p, to, t))

    out_plain = [(gs_q, g_qkv), (gs_p, g_proj), (gs_u, g_up), (gs_d, g_down)]

    def z_start(a):
        if z_inside:
            for k in offsets:
                z_copy(a, k).start()
        else:
            local(out_plain[a][0], out_plain[a][1], 20 + a).start()

    def z_finish(a):
        if z_inside:
            whole, landing, final, result = z_sets[a]
            for k in offsets:
                z_copy(a, k).wait()

            def body(j):
                at = pl.ds(pl.multiple_of(j * STRIP, STRIP), STRIP)
                rows = pl.ds(pl.multiple_of(d * share + j * STRIP, STRIP), STRIP)
                total = whole[rows, :].astype(F32)
                for k in offsets:
                    total = total + landing[k - 1, at, :].astype(F32)
                final[at, :] = total

            loop(share // STRIP, body)
            local(final, result, 20 + a).start()

    def z_end(a):
        if z_inside:
            local(z_sets[a][2], z_sets[a][3], 20 + a).wait()
        else:
            local(out_plain[a][0], out_plain[a][1], 20 + a).wait()

    def one_layer(text):
        rows = rows_t if text else rows_i
        total = rows * CHUNKS
        strips = rows // STRIP
        q_off = rows_t if text else 0

        def at_rows(i):
            return pl.ds(pl.multiple_of(i * rows, 16), rows)

        def q_rows(i):
            return pl.ds(pl.multiple_of(i * rows + q_off, 16), rows)

        def strip_rows(i, j):
            return pl.ds(pl.multiple_of(i * rows + j * STRIP, STRIP), STRIP)

        def swap(i, landing, kind):
            return remote(send_s.at[at_rows(i)], landing.at[at_rows(i)], kind, i, peer)

        incoming = dy_to_image if not text else x_to_text

        def wait_input(i):
            cp = remote(x_s.at[at_rows(i)] if text else dy_s.at[at_rows(i)],
                        x_s.at[at_rows(i)] if text else dy_s.at[at_rows(i)], K_IN, i, across)
            cp.wait_recv()

        wq_own.wait()
        wq_sib.wait()
        sm_own.wait()
        sm_sib.wait()
        if text:
            txt_in.wait()
            pad = jnp.zeros((rows_t, 2 * QKV), BF16)
            qkv_s[0:rows_t, :] = pad
            qkv_s[rows_t + total : 2 * rows_t + total, :] = pad
            dkv_s[...] = jnp.zeros_like(dkv_s)
        else:
            img_in.wait()
        for s in range(2):
            o_s[0:total, s * MIX + WIDE : (s + 1) * MIX] = jnp.zeros((total, MIX - WIDE), BF16)

        def project(i):
            if text:
                wait_input(i)

            def first_norm(j):
                at = strip_rows(i, j)
                unit, _ = unit_of(x_s[at, :].astype(F32))
                a1_s[at, :] = (unit * own_gain[0] + own_shift[0]).astype(BF16)

            loop(strips, first_norm)
            left = a1_s[at_rows(i), :]
            lanes = lax.broadcasted_iota(jnp.int32, (1, QKV), 1)
            factor = jnp.where(lanes < WIDE, HEAD**-0.5, 1.0).astype(F32)
            for s in range(2):
                value = dot(left, wq_s[:, s * QKV : (s + 1) * QKV])
                value = (value + small_s[s, 0:1, width : width + QKV]) * factor
                qkv_s[q_rows(i), s * QKV : (s + 1) * QKV] = value.astype(BF16)

        def head_at(h):
            s, hh = h // HALF, h % HALF
            base = s * QKV + hh * HEAD
            return slice(base, base + HEAD), slice(base + WIDE, base + WIDE + HEAD), slice(base + 2 * WIDE, base + 2 * WIDE + HEAD), slice(s * MIX + hh * HEAD, s * MIX + hh * HEAD + HEAD)

        span = 3 * rows_t if text else rows_i

        def key_rows(i):
            return pl.ds(pl.multiple_of(i * rows, 16), span)

        def allowed(i):
            if text:
                mine = seg_col[at_rows(i), 0:1]
                keys = seg_row[0:1, pl.ds(pl.multiple_of(i * rows_t, 128), span)]
                return mine == keys
            return lax.broadcasted_iota(jnp.int32, (1, span), 1) < keys_i

        def attend(i):
            ok = allowed(i)
            for h in range(HEADS):
                qc, kc, vc, oc = head_at(h)
                scores = dot_nt(qkv_s[q_rows(i), qc], qkv_s[key_rows(i), kc])
                scores = jnp.where(ok, scores, MASKED)
                raised = jnp.exp(scores - jnp.max(scores, axis=-1, keepdims=True))
                weights = raised * (1.0 / jnp.sum(raised, axis=-1, keepdims=True))
                p_s[i * HEADS + h, 0:rows, 0:span] = weights
                mixed = dot(weights.astype(BF16), qkv_s[key_rows(i), vc])
                o_s[at_rows(i), oc] = mixed.astype(BF16)

        def send_a(i):
            send_s[at_rows(i), :] = dot(o_s[at_rows(i), :], wp_s[...]).astype(BF16)
            swap(i, ra_s, K_A).start()

        if text:
            loop(CHUNKS, project)
            wp_own.wait()
            wp_sib.wait()

            def forward(i):
                attend(i)
                send_a(i)

            loop(CHUNKS, forward)
        else:

            def forward(i):
                project(i)
                attend(i)

                @pl.when(i == 0)
                def _():
                    wp_own.wait()
                    wp_sib.wait()

                send_a(i)

            loop(CHUNKS, forward)
        wu_own.wait()
        wu_sib.wait()
        wd_own.wait()
        wd_sib.wait()

        def y_copies(i):
            at = at_rows(i)
            if text:
                return [remote(ys_s.at[at], yt_s.at[at], K_YT, i, peer)]
            return [
                remote(ys_s.at[at], y1_s.at[at], K_Y1, i, across),
                remote(ys_s.at[at], y2_s.at[at], K_Y2, i, across_peer),
            ]

        def middle(i):
            if not text:
                wait_input(i)
            swap(i, ra_s, K_A).wait()

            def second_norm(j):
                at = strip_rows(i, j)
                r = x_s[at, :].astype(F32) + (send_s[at, :].astype(F32) + ra_s[at, :].astype(F32)) + outb[0:1, :]
                r_s[at, :] = r
                unit, _ = unit_of(r)
                a2_s[at, :] = (unit * own_gain[1] + own_shift[1]).astype(BF16)
                acc_s[5] += fold(dy_s[at, :].astype(F32))

            loop(strips, second_norm)
            left = a2_s[at_rows(i), :]
            grad = dy_s[at_rows(i), :]
            for n in range(2 * width // TILE):
                cols = slice(n * TILE, (n + 1) * TILE)
                s, inner = (n * TILE) // width, (n * TILE) % width
                u = dot(left, wu_s[:, cols]) + small_s[s, 0:1, inner : inner + TILE]
                g, slope = gelu_pair(u)
                gb_s[at_rows(i), cols] = g.astype(BF16)
                du = (dot_nt(grad, wd_s[cols, :]) * slope).astype(BF16)
                du_s[at_rows(i), cols] = du
                acc_s[6 + s, :, inner : inner + TILE] += fold(du.astype(F32))
            send_s[at_rows(i), :] = dot_nt(du_s[at_rows(i), :], wu_s[...]).astype(BF16)
            swap(i, rb_s, K_B).start()
            lower = dot(gb_s[at_rows(i), :], wd_s[...])
            ys_s[at_rows(i), :] = (lower + 0.5 * (r_s[at_rows(i), :] + outb[1:2, :])).astype(BF16)
            for cp in y_copies(i):
                cp.start()

        loop(CHUNKS, middle)
        end_d = grads_pair(3, dy_s, gb_s, total, (0, width), (width, 2 * width))
        end_u = grads_pair(2, a2_s, du_s, total, (0, width), (width, 2 * width))
        end_d()
        z_start(3)
        end_u()
        z_start(2)

        dq_s, drb_s = gb_s, a2_s
        for s in range(2):
            dq_s[0:total, s * QKV + 3 * WIDE : (s + 1) * QKV] = jnp.zeros((total, QKV - 3 * WIDE), BF16)

        def attend_back(i):
            swap(i, rb_s, K_B).wait()

            def back_norm(j):
                at = strip_rows(i, j)
                grad = send_s[at, :].astype(F32) + rb_s[at, :].astype(F32)
                unit, inverse = unit_of(r_s[at, :])
                dr = dy_s[at, :].astype(F32) + norm_back(grad, unit, inverse, own_gain[1])
                r_s[at, :] = dr
                drb_s[at, :] = dr.astype(BF16)
                acc_s[1] += fold(grad * unit)
                acc_s[3] += fold(grad)
                acc_s[4] += fold(dr)

            loop(strips, back_norm)
            do_s[0:rows, :] = dot_nt(drb_s[at_rows(i), :], wp_s[...]).astype(BF16)
            for h in range(HEADS):
                qc, kc, vc, oc = head_at(h)
                weights = p_s[i * HEADS + h, 0:rows, 0:span]
                grad_o = do_s[0:rows, oc]
                keys = qkv_s[key_rows(i), kc]
                slope = dot_nt(grad_o, qkv_s[key_rows(i), vc])
                ds = (weights * (slope - jnp.sum(slope * weights, axis=-1, keepdims=True))).astype(BF16)
                dq = dot(ds, keys).astype(BF16) * (HEAD**-0.5)
                dk = dot_tn(ds, qkv_s[q_rows(i), qc])
                dv = dot_tn(weights.astype(BF16), grad_o)
                dq_s[at_rows(i), qc] = dq.astype(BF16)
                if text:
                    hc = slice(h * HEAD, (h + 1) * HEAD)
                    hv = slice((HEADS + h) * HEAD, (HEADS + h + 1) * HEAD)
                    dkv_s[key_rows(i), hc] += dk
                    dkv_s[key_rows(i), hv] += dv
                else:
                    dq_s[at_rows(i), kc] = dk.astype(BF16)
                    dq_s[at_rows(i), vc] = dv.astype(BF16)

        def send_c(i):
            if text:
                for s in range(2):
                    k0 = s * QKV + WIDE
                    dq_s[at_rows(i), k0 : k0 + WIDE] = dkv_s[q_rows(i), s * WIDE : (s + 1) * WIDE].astype(BF16)
                    v0 = 2 * WIDE + s * WIDE
                    dq_s[at_rows(i), k0 + WIDE : k0 + 2 * WIDE] = dkv_s[q_rows(i), v0 : v0 + WIDE].astype(BF16)
            grad = dq_s[at_rows(i), 0 : 2 * QKV]
            send_s[at_rows(i), :] = dot_nt(grad, wq_s[...]).astype(BF16)
            swap(i, rc_s, K_C).start()
            for s in range(2):
                acc_s[8 + s, :, 0:QKV] += fold(grad[:, s * QKV : (s + 1) * QKV].astype(F32))

        if text:

            def backward(i):
                @pl.when(i < CHUNKS)
                def _():
                    attend_back(i)

                @pl.when(i > 0)
                def _():
                    send_c(i - 1)

            loop(CHUNKS + 1, backward)
        else:

            def backward(i):
                attend_back(i)
                send_c(i)

            loop(CHUNKS, backward)
        end_q = grads_pair(0, a1_s, dq_s, total, (0, QKV), (QKV, 2 * QKV))
        end_p = grads_pair(1, drb_s, o_s, total, (0, MIX), (MIX, 2 * MIX))
        end_q()
        z_start(0)
        end_p()
        z_start(1)

        def own_img(i):
            return img_out.at[pl.ds(pl.multiple_of(core * n_img + i * rows_i, 16), rows_i)]

        def own_txt(i):
            return txt_out.at[pl.ds(pl.multiple_of(core * n_txt + i * rows_t, 16), rows_t)]

        def img_copies(i):
            src = fin_s.at[pl.ds(pl.multiple_of(i * rows_i, 16), rows_i)]
            return local(src, own_img(i), 8 + i), remote(src, own_img(i), K_OI, i, sib)

        def txt_copies(i):
            src = ys_s.at[pl.ds(pl.multiple_of(i * rows_t, 16), rows_t)]
            return local(src, own_txt(i), 12 + i), remote(src, own_txt(i), K_OT, i, sib)

        def dx_copies(i):
            src = rb_s.at[pl.ds(pl.multiple_of(i * rows_t, 16), rows_t)]
            return remote(src, own_txt(i), K_T1, i, across), remote(src, own_txt(i), K_T2, i, across_sib)

        if text:

            def own_y(i):
                y_copies(i)[0].wait()
                at = at_rows(i)
                ys_s[at, :] = (ys_s[at, :].astype(F32) + yt_s[at, :].astype(F32)).astype(BF16)
                for cp in txt_copies(i):
                    cp.start()

            def image_y(i):
                at = pl.ds(pl.multiple_of(i * rows_i, 16), rows_i)
                remote(y1_s.at[at], y1_s.at[at], K_Y1, i, across).wait_recv()
                remote(y2_s.at[at], y2_s.at[at], K_Y2, i, across_peer).wait_recv()
                fin_s[at, :] = (y1_s[at, :].astype(F32) + y2_s[at, :].astype(F32)).astype(BF16)
                for cp in img_copies(i):
                    cp.start()

        def last(i):
            swap(i, rc_s, K_C).wait()

            def body(j):
                at = strip_rows(i, j)
                grad = send_s[at, :].astype(F32) + rc_s[at, :].astype(F32)
                unit, inverse = unit_of(x_s[at, :].astype(F32))
                dx = (r_s[at, :] + norm_back(grad, unit, inverse, own_gain[0])).astype(BF16)
                if text:
                    rb_s[at, :] = dx
                else:
                    fin_s[at, :] = dx
                acc_s[0] += fold(grad * unit)
                acc_s[2] += fold(grad)

            loop(strips, body)
            for cp in dx_copies(i) if text else img_copies(i):
                cp.start()

        if text:
            loop(CHUNKS, own_y)
        loop(CHUNKS, last)

        order = (0, 1, 2, 3, 4, 5, 7, 6, 9, 8, 10, 11, 12, 13, 14, 15)
        sums = jnp.sum(acc_s[...], axis=1)
        vec_s[0] = sums
        for row, src in enumerate(order):
            vec_s[1, row : row + 1, :] = sums[src : src + 1, :]
        v_sib = remote(vec_s.at[1], vrec_s, K_S, 1, sib)
        v_sib.start()
        z_finish(3)
        z_finish(2)
        v_sib.wait()
        vec_s[0] = vec_s[0] + vrec_s[...]
        if z_inside:
            vall_s[d] = vec_s[0]

            def v_copy(k):
                to = lax.rem(d + k, dp_size)
                return remote(vec_s.at[0], vall_s.at[d], K_Z + 4, k - 1, (p, to, t))

            for k in offsets:
                v_copy(k).start()
        if text:
            loop(CHUNKS, image_y)
        z_finish(0)
        z_finish(1)
        if z_inside:
            for k in offsets:
                v_copy(k).wait_send()
            for k in offsets:
                back = lax.rem(d + dp_size - k, dp_size)
                remote(vall_s.at[back], vall_s.at[back], K_Z + 4, k - 1, (p, back, t)).wait_recv()
            totals = vall_s[0]
            for k in range(1, dp_size):
                totals = totals + vall_s[k]
            vec_out[...] = totals
        else:
            vec_out[...] = vec_s[0]

        def finish(i):
            if text:
                dy_to_image(i).wait_send()
                for cp in dx_copies(i):
                    cp.wait_send()
                here, there = txt_copies(i)
                here.wait()
                there.wait()
            else:
                x_to_text(i).wait_send()
                for cp in y_copies(i):
                    cp.wait_send()
                for cp in dx_copies(i):
                    cp.wait_recv()
            here, there = img_copies(i)
            here.wait()
            there.wait()

        loop(CHUNKS, finish)
        for a in range(4):
            z_end(a)

    @pl.when(image_here)
    def _():
        one_layer(False)

    @pl.when(jnp.logical_not(image_here))
    def _():
        one_layer(True)


def per_device(
    image_side, text_side, caption_lengths, norm_gains, norm_shifts, w_qkv, bias_qv, w_proj, out_bias, w_up, bias_up, w_down,
):
    dp_size = lax.axis_size("dp")
    core = lax.rem(lax.axis_index("tensor"), 2)
    images, keys_i, width = image_side.shape[1:]
    blocks, length = text_side.shape[1:3]
    per_core = images // 2
    rows_i = -(-(per_core // CHUNKS * keys_i) // 16) * 16
    rows_t = length * (blocks // 2) // CHUNKS
    share = width // dp_size
    z_inside = 1 < dp_size <= 4 and share % 16 == 0

    img = lax.dynamic_slice_in_dim(image_side[0], core * per_core, per_core, 0)
    img = jnp.pad(img, ((0, 0), (0, rows_i - keys_i), (0, 0))).reshape(per_core * rows_i, width)
    txt = lax.dynamic_slice_in_dim(text_side[0], core, 1, 0)[0]
    bounds = jnp.cumsum(lax.dynamic_slice_in_dim(caption_lengths, core, 1, 0)[0])
    places = jnp.arange(length, dtype=jnp.int32)
    segment = jnp.sum((places[:, None] >= bounds[None, :]).astype(jnp.int32), axis=1)
    seg_col = segment[:, None]
    seg_row = jnp.pad(segment, (rows_t, rows_t), constant_values=-1)[None]
    wq = jnp.pad(w_qkv[0].reshape(width, 3 * WIDE), ((0, 0), (0, QKV - 3 * WIDE)))
    lane = jnp.zeros((WIDE,), F32)
    small = jnp.concatenate([bias_up[0], bias_qv[0, 0], lane, bias_qv[0, 1], jnp.zeros((QKV - 3 * WIDE,), F32)])
    small = jnp.broadcast_to(small[None], (8, small.shape[0]))

    n_i, n_t = rows_i * CHUNKS, rows_t * CHUNKS
    columns = (QKV, MIX, width, width)
    sds = jax.ShapeDtypeStruct
    grad_type = (lambda w: sds((share, w), F32)) if z_inside else (lambda w: sds((width, w), BF16))
    outs = [sds((2 * n_i, width), BF16), sds((2 * n_t, width), BF16)]
    outs += [grad_type(w) for w in columns] + [sds((16, width), F32)]
    any_spec, vmem_spec = pl.BlockSpec(memory_space=pl.ANY), pl.BlockSpec(memory_space=pltpu.VMEM)
    v = pltpu.VMEM
    scratch = [
        v((n_i, width), BF16), v((n_i, width), BF16),
        v((width, 2 * QKV), BF16), v((2 * MIX, width), BF16), v((width, 2 * width), BF16), v((2 * width, width), BF16),
        v((2, 8, width + QKV), F32),
        v((n_i, width), BF16), v((max(n_i, n_t + 2 * rows_t), 2 * QKV), BF16), v((n_i, 2 * MIX), BF16), v((n_i, width), F32),
        v((n_i, width), BF16), v((n_i, 2 * width), BF16), v((n_i, 2 * width), BF16),
        v((CHUNKS * HEADS, max(rows_i, rows_t), max(-(-rows_i // 128) * 128, 3 * rows_t)), F32),
        v((n_t + 2 * rows_t, 2 * HEADS * HEAD), F32), v((max(rows_i, rows_t), 2 * MIX), BF16),
        v((n_i, width), BF16), v((n_i, width), BF16), v((n_i, width), BF16), v((n_i, width), BF16),
        v((n_i, width), BF16), v((n_t, width), BF16), v((n_i, width), BF16), v((n_i, width), BF16), v((n_i, width), BF16),
        v((16, 8, width), F32), v((2, 16, width), F32), v((16, width), F32), v((dp_size if z_inside else 1, 16, width), F32),
    ]
    scratch += [v((width, w), BF16) for w in columns] + [v((width, w), BF16) for w in columns]
    if z_inside:
        scratch += [v((dp_size - 1, share, w), BF16) for w in columns] + [v((share, w), F32) for w in columns]
    dma = pltpu.SemaphoreType.DMA
    scratch += [dma((4 * N_KINDS,)), dma((4 * N_KINDS,)), dma((24,))]
    img_out, txt_out, g_q, g_p, g_u, g_d, vec = pl.pallas_call(
        partial(layers_kernel, rows_i, rows_t, keys_i, dp_size, z_inside),
        out_shape=outs,
        in_specs=[any_spec] * 7 + [vmem_spec] * 5,
        out_specs=[any_spec] * 6 + [vmem_spec],
        scratch_shapes=scratch,
        compiler_params=pltpu.CompilerParams(collective_id=0, has_side_effects=True, vmem_limit_bytes=60 << 20),
    )(
        img, txt, wq, w_proj[0], w_up[0], w_down[0], small, norm_gains[0], norm_shifts[0], out_bias[0], seg_col, seg_row,
    )
    if not z_inside:
        def scatter(grad):
            return lax.psum_scatter(grad, "dp", scatter_dimension=0, tiled=True).astype(F32)

        g_q, g_p, g_u, g_d = (scatter(g) for g in (g_q[:, : 3 * WIDE], g_p[:, :WIDE], g_u, g_d))
        vec = lax.psum(vec, "dp")
    image_result = img_out.reshape(images, rows_i, width)[:, :keys_i][None]
    text_result = txt_out.reshape(blocks, length, width)[None]
    return (
        image_result,
        text_result,
        vec[0:2][None],
        vec[2:4][None],
        g_q[:, : 3 * WIDE].reshape(share, 3, WIDE)[None],
        jnp.stack([vec[8, 0:WIDE], vec[8, 2 * WIDE : 3 * WIDE]])[None],
        g_p[:, :WIDE].T[None],
        vec[4:6][None],
        g_u[None],
        vec[6][None],
        g_d.T[None],
    )


def solution(mesh):
    placed = (
        P("pipe", "dp", None, None),
        P("pipe", "dp", None, None),
        P("dp", None),
        P("pipe", None, None),
        P("pipe", None, None),
        P("pipe", None, None, "tensor"),
        P("pipe", None, "tensor"),
        P("pipe", "tensor", None),
        P("pipe", None, None),
        P("pipe", None, "tensor"),
        P("pipe", "tensor"),
        P("pipe", "tensor", None),
    )
    return jax.shard_map(
        per_device,
        mesh=mesh,
        in_specs=placed,
        out_specs=(
            P("pipe", "dp", None, None),
            P("pipe", "dp", None, None),
            P("pipe", None, None),
            P("pipe", None, None),
            P("pipe", "dp", None, "tensor"),
            P("pipe", None, "tensor"),
            P("pipe", "tensor", "dp"),
            P("pipe", None, None),
            P("pipe", "dp", "tensor"),
            P("pipe", "tensor"),
            P("pipe", "tensor", "dp"),
        ),
        check_vma=False,
    )
```

```python
from functools import partial

import jax
import jax.numpy as jnp
from jax import lax
from jax.experimental import pallas as pl
from jax.experimental.pallas import tpu as pltpu
from jax.sharding import PartitionSpec as P

F32 = jnp.float32
BF16 = jnp.bfloat16
BY_MESH = pl.DeviceIdType.MESH
HEAD = 64
HALF = 3
HEADS = 2 * HALF
WIDE = HALF * HEAD
EPSILON = 1e-06
MASKED = -1000000000.0
CHUNKS = 4
STRIP = 16
BLOCK = 208
QKV = 640
MIX = 256
PAD = MIX - WIDE
TILE = 256

K_IN, K_A, K_B, K_C, K_Y1, K_Y2, K_YT, K_OI, K_OT, K_T1, K_W, K_S, K_G, K_V, K_Z = range(15)
N_KINDS = K_Z + 3


def dot(a, b):
    return lax.dot_general(a, b, (((1,), (0,)), ((), ())), preferred_element_type=F32)


def dot_nt(a, b):
    return lax.dot_general(a, b, (((1,), (1,)), ((), ())), preferred_element_type=F32)


def dot_tn(a, b):
    return lax.dot_general(a, b, (((0,), (0,)), ((), ())), preferred_element_type=F32)


def loop(count, body):
    def step(j, carry):
        body(j)
        return carry

    lax.fori_loop(0, count, step, 0)


def unit_of(rows):
    centre = rows - jnp.mean(rows, axis=-1, keepdims=True)
    inverse = lax.rsqrt(jnp.mean(centre * centre, axis=-1, keepdims=True) + EPSILON)
    return centre * inverse, inverse


def norm_back(grad, unit, inverse, gain):
    scaled = grad * gain
    first = jnp.mean(scaled, axis=-1, keepdims=True)
    second = jnp.mean(scaled * unit, axis=-1, keepdims=True)
    return inverse * (scaled - first - unit * second)


def gelu_pair(u):
    cdf = 0.5 * (1.0 + lax.erf(u * (0.5**0.5)))
    pdf = jnp.exp(u * u * -0.5) * 0.3989422804014327
    return u * cdf, cdf + u * pdf


def fold(rows):
    return jnp.sum(rows.reshape(rows.shape[0] // 8, 8, rows.shape[1]), axis=0)


def layers_kernel(
    rows_i, rows_t, keys_i, dp_size, z_inside,
    img_own, txt_own, w_qkv, w_proj, w_up, w_down, small, gains, shifts, outb, seg_col, seg_row,
    img_out, txt_out, g_mix, g_up, g_down, vec_out,
    x_s, dy_s, wq_s, wp_s, wu_s, wd_s, small_s, a1_s, qkv_s, o_s, r_s, a2_s, gb_s, du_s, p_s, dkv_s, do_s,
    send_s, ra_s, rb_s, rc_s, ys_s, yt_s, y1_s, y2_s, fin_s, acc_s, vec_s, vrec_s, vall_s,
    gs_x, gs_u, gs_d, gr_x, gr_u, gr_d, *rest,
):
    if z_inside:
        z1_s, z2_s, zf_s, ssem, rsem, lsem = rest
    else:
        ssem, rsem, lsem = rest
    width = x_s.shape[1]
    p, d, t = lax.axis_index("pipe"), lax.axis_index("dp"), lax.axis_index("tensor")
    core = lax.rem(t, 2)
    sib_t = t + 1 - 2 * core
    peer_t = lax.rem(t + 2, 4)
    other = 1 - p
    sib, peer = (p, d, sib_t), (p, d, peer_t)
    across = (other, d, t)
    offsets = range(1, dp_size) if z_inside else range(0)
    partners = [sib, peer, across]
    partners += [(p, lax.rem(d + k, dp_size), t) for k in offsets]

    def remote(src, dst, kind, slot, to):
        at = kind * 4 + slot
        return pltpu.make_async_remote_copy(
            src_ref=src, dst_ref=dst, send_sem=ssem.at[at], recv_sem=rsem.at[at],
            device_id=to, device_id_type=BY_MESH,
        )

    def local(src, dst, slot):
        return pltpu.make_async_copy(src, dst, lsem.at[slot])

    image_here = p == 0
    n_img = rows_i * CHUNKS
    n_txt = rows_t * CHUNKS

    wq_own = local(w_qkv, wq_s.at[:, 0:QKV], 0)
    wp_own = local(w_proj, wp_s.at[PAD:MIX], 1)
    wu_own = local(w_up, wu_s.at[:, 0:width], 2)
    wd_own = local(w_down, wd_s.at[0:width], 3)
    sm_own = local(small, small_s.at[0], 4)
    img_in = local(img_own, x_s, 5)
    txt_in = local(txt_own, dy_s.at[0:n_txt], 6)
    sm_own.start()
    wq_own.start()

    @pl.when(image_here)
    def _():
        img_in.start()

    @pl.when(jnp.logical_not(image_here))
    def _():
        txt_in.start()

    wp_own.start()
    wu_own.start()
    wd_own.start()
    zero_rows = jnp.zeros((PAD, width), BF16)
    wp_s[0:PAD, :] = zero_rows
    wp_s[MIX : MIX + PAD, :] = zero_rows
    acc_s[...] = jnp.zeros_like(acc_s)

    barrier = pltpu.get_barrier_semaphore()
    for to in partners:
        pl.semaphore_signal(barrier, inc=1, device_id=to, device_id_type=BY_MESH)
    pl.semaphore_wait(barrier, len(partners))

    sm_sib = remote(small, small_s.at[1], K_S, 0, sib)
    wq_sib = remote(w_qkv, wq_s.at[:, QKV:], K_W, 0, sib)
    wp_sib = remote(w_proj, wp_s.at[MIX + PAD :], K_W, 1, sib)
    wu_sib = remote(w_up, wu_s.at[:, width:], K_W, 2, sib)
    wd_sib = remote(w_down, wd_s.at[width:], K_W, 3, sib)

    def x_to_text(i):
        rows = pl.ds(pl.multiple_of(i * rows_t, 16), rows_t)
        return remote(txt_own.at[rows], x_s.at[rows], K_IN, i, across)

    def dy_to_image(i):
        rows = pl.ds(pl.multiple_of(i * rows_i, 16), rows_i)
        return remote(img_own.at[rows], dy_s.at[rows], K_IN, i, across)

    @pl.when(image_here)
    def _():
        loop(CHUNKS, lambda i: x_to_text(i).start())

    sm_sib.start()
    wq_sib.start()

    @pl.when(jnp.logical_not(image_here))
    def _():
        loop(CHUNKS, lambda i: dy_to_image(i).start())

    wp_sib.start()
    wu_sib.start()
    wd_sib.start()

    own_gain = [gains[0:1, :], gains[1:2, :]]
    own_shift = [shifts[0:1, :], shifts[1:2, :]]

    g_arrays = [(gs_x, gr_x, g_mix), (gs_u, gr_u, g_up), (gs_d, gr_d, g_down)]

    def g_exchange(a):
        return remote(g_arrays[a][0], g_arrays[a][1], K_G, a, sib)

    def grads_pair(a, product):
        mine, theirs = g_arrays[a][0:2]
        tiles = width // TILE

        def send_half(m):
            at = pl.ds(pl.multiple_of(m * TILE, TILE), TILE)
            mine[at, :] = product(at, 1).astype(BF16)

        loop(tiles, send_half)
        g_exchange(a).start()

        def finish():
            g_exchange(a).wait()

            def own_half(m):
                at = pl.ds(pl.multiple_of(m * TILE, TILE), TILE)
                mine[at, :] = (product(at, 0) + theirs[at, :].astype(F32)).astype(BF16)

            loop(tiles, own_half)

        return finish

    share = width // dp_size
    parity = lax.rem(d, 2)
    upper = d // 2
    near = d + 1 - 2 * parity
    far = d + 2 - 4 * upper if z_inside else d

    def share_rows(at):
        return pl.ds(pl.multiple_of(at * share, 16), share)

    def z_near(a, k):
        src = g_arrays[a][0].at[share_rows(1 - parity + 2 * k)]
        return remote(src, z1_s.at[a, k], K_Z, 3 * k + a, (p, near, t))

    def z_far(a):
        return remote(g_arrays[a][0].at[share_rows(far)], z2_s.at[a], K_Z, 6 + a, (p, far, t))

    def z_start(a):
        if z_inside:
            for k in range(2):
                z_near(a, k).start()
        else:
            local(g_arrays[a][0], g_arrays[a][2], 20 + a).start()

    def z_middle(a):
        if z_inside:
            for k in range(2):
                z_near(a, k).wait()
            mine = g_arrays[a][0]
            rows = share_rows(far)
            mine[rows, :] = (mine[rows, :].astype(F32) + z1_s[a, 1 - upper].astype(F32)).astype(BF16)
            z_far(a).start()

    def z_finish(a):
        if z_inside:
            z_far(a).wait()
            total = g_arrays[a][0][share_rows(d), :].astype(F32) + z1_s[a, upper].astype(F32)
            zf_s[a] = total + z2_s[a].astype(F32)
            local(zf_s.at[a], g_arrays[a][2], 20 + a).start()

    def z_end(a):
        if z_inside:
            local(zf_s.at[a], g_arrays[a][2], 20 + a).wait()
        else:
            local(g_arrays[a][0], g_arrays[a][2], 20 + a).wait()

    def one_layer(text):
        rows = rows_t if text else rows_i
        total = rows * CHUNKS
        cuts = [(o, min(BLOCK, rows - o)) for o in range(0, rows, BLOCK)]
        q_off = rows_t if text else 0

        def at_rows(i):
            return pl.ds(pl.multiple_of(i * rows, 16), rows)

        def q_rows(i):
            return pl.ds(pl.multiple_of(i * rows + q_off, 16), rows)

        def by_strips(i, body):
            for o, size in cuts:
                body(pl.ds(pl.multiple_of(i * rows + o, STRIP), size))

        def swap(i, landing, kind):
            return remote(send_s.at[at_rows(i)], landing.at[at_rows(i)], kind, i, peer)

        incoming = dy_to_image if not text else x_to_text

        def wait_input(i):
            cp = remote(x_s.at[at_rows(i)] if text else dy_s.at[at_rows(i)],
                        x_s.at[at_rows(i)] if text else dy_s.at[at_rows(i)], K_IN, i, across)
            cp.wait_recv()

        wq_own.wait()
        wq_sib.wait()
        sm_own.wait()
        sm_sib.wait()
        if text:
            txt_in.wait()
            pad = jnp.zeros((rows_t, 2 * QKV), BF16)
            qkv_s[0:rows_t, :] = pad
            qkv_s[rows_t + total : 2 * rows_t + total, :] = pad
            dkv_s[...] = jnp.zeros_like(dkv_s)
        else:
            img_in.wait()
        for s in range(2):
            o_s[0:total, s * MIX : s * MIX + PAD] = jnp.zeros((total, PAD), BF16)

        def project(i):
            if text:
                wait_input(i)

            def first_norm(at):
                unit, _ = unit_of(x_s[at, :].astype(F32))
                a1_s[at, :] = (unit * own_gain[0] + own_shift[0]).astype(BF16)

            by_strips(i, first_norm)
            left = a1_s[at_rows(i), :]
            lanes = lax.broadcasted_iota(jnp.int32, (1, QKV), 1)
            factor = jnp.where(lanes < WIDE, HEAD**-0.5, 1.0).astype(F32)
            for s in range(2):
                value = dot(left, wq_s[:, s * QKV : (s + 1) * QKV])
                value = (value + small_s[s, 0:1, width : width + QKV]) * factor
                qkv_s[q_rows(i), s * QKV : (s + 1) * QKV] = value.astype(BF16)

        def head_at(h):
            s, hh = h // HALF, h % HALF
            base = s * QKV + hh * HEAD
            return slice(base, base + HEAD), slice(base + WIDE, base + WIDE + HEAD), slice(base + 2 * WIDE, base + 2 * WIDE + HEAD), slice(s * MIX + PAD + hh * HEAD, s * MIX + PAD + hh * HEAD + HEAD)

        span = 3 * rows_t if text else rows_i

        def key_rows(i):
            return pl.ds(pl.multiple_of(i * rows, 16), span)

        def allowed(i):
            if text:
                mine = seg_col[at_rows(i), 0:1]
                keys = seg_row[0:1, pl.ds(pl.multiple_of(i * rows_t, 128), span)]
                return mine == keys
            return lax.broadcasted_iota(jnp.int32, (1, span), 1) < keys_i

        def attend(i):
            ok = allowed(i)
            for h in range(HEADS):
                qc, kc, vc, oc = head_at(h)
                scores = dot_nt(qkv_s[q_rows(i), qc], qkv_s[key_rows(i), kc])
                scores = jnp.where(ok, scores, MASKED)
                raised = jnp.exp(scores - jnp.max(scores, axis=-1, keepdims=True))
                weights = raised * (1.0 / jnp.sum(raised, axis=-1, keepdims=True))
                p_s[i * HEADS + h, 0:rows, 0:span] = weights
                mixed = dot(weights.astype(BF16), qkv_s[key_rows(i), vc])
                o_s[at_rows(i), oc] = mixed.astype(BF16)

        def send_a(i):
            send_s[at_rows(i), :] = dot(o_s[at_rows(i), :], wp_s[...]).astype(BF16)
            swap(i, ra_s, K_A).start()

        if text:

            def forward(i):
                @pl.when(i < CHUNKS)
                def _():
                    project(i)

                @pl.when(i == 1)
                def _():
                    wp_own.wait()
                    wp_sib.wait()

                @pl.when(i > 0)
                def _():
                    attend(i - 1)
                    send_a(i - 1)

            loop(CHUNKS + 1, forward)
        else:

            def forward(i):
                project(i)
                attend(i)

                @pl.when(i == 0)
                def _():
                    wp_own.wait()
                    wp_sib.wait()

                send_a(i)

            loop(CHUNKS, forward)
        wu_own.wait()
        wu_sib.wait()
        wd_own.wait()
        wd_sib.wait()

        def y_copies(i):
            at = at_rows(i)
            if text:
                return [remote(ys_s.at[at], yt_s.at[at], K_YT, i, peer)]
            return [remote(ys_s.at[at], y1_s.at[at], K_Y1, i, across)]

        def y_relay(i):
            at = pl.ds(pl.multiple_of(i * rows_i, 16), rows_i)
            return remote(y1_s.at[at], y2_s.at[at], K_Y2, i, peer)

        def hand_on(i):
            at = pl.ds(pl.multiple_of(i * rows_i, 16), rows_i)
            remote(y1_s.at[at], y1_s.at[at], K_Y1, i, across).wait_recv()
            y_relay(i).start()

        def middle(i):
            if not text:
                wait_input(i)
            swap(i, ra_s, K_A).wait()

            def second_norm(at):
                r = x_s[at, :].astype(F32) + (send_s[at, :].astype(F32) + ra_s[at, :].astype(F32)) + outb[0:1, :]
                r_s[at, :] = r
                unit, _ = unit_of(r)
                a2_s[at, :] = (unit * own_gain[1] + own_shift[1]).astype(BF16)
                acc_s[5] += fold(dy_s[at, :].astype(F32))

            by_strips(i, second_norm)
            left = a2_s[at_rows(i), :]
            grad = dy_s[at_rows(i), :]
            for n in range(2 * width // TILE):
                cols = slice(n * TILE, (n + 1) * TILE)
                s, inner = (n * TILE) // width, (n * TILE) % width
                u = dot(left, wu_s[:, cols]) + small_s[s, 0:1, inner : inner + TILE]
                g, slope = gelu_pair(u)
                gb_s[at_rows(i), cols] = g.astype(BF16)
                du = (dot_nt(grad, wd_s[cols, :]) * slope).astype(BF16)
                du_s[at_rows(i), cols] = du
                acc_s[6 + s, :, inner : inner + TILE] += fold(du.astype(F32))
            send_s[at_rows(i), :] = dot_nt(du_s[at_rows(i), :], wu_s[...]).astype(BF16)
            swap(i, rb_s, K_B).start()
            lower = dot(gb_s[at_rows(i), :], wd_s[...])
            ys_s[at_rows(i), :] = (lower + 0.5 * (r_s[at_rows(i), :] + outb[1:2, :])).astype(BF16)
            if not text:
                for cp in y_copies(i):
                    cp.start()

        loop(CHUNKS, middle)
        end_d = grads_pair(2, lambda at, s: dot_tn(dy_s[0:total, at], gb_s[0:total, s * width : (s + 1) * width]))
        end_u = grads_pair(1, lambda at, s: dot_tn(a2_s[0:total, at], du_s[0:total, s * width : (s + 1) * width]))
        end_d()
        z_start(2)
        end_u()
        z_start(1)

        dq_s, drb_s = gb_s, a2_s
        for s in range(2):
            dq_s[0:total, s * QKV + 3 * WIDE : (s + 1) * QKV] = jnp.zeros((total, QKV - 3 * WIDE), BF16)

        def attend_back(i):
            swap(i, rb_s, K_B).wait()

            def back_norm(at):
                grad = send_s[at, :].astype(F32) + rb_s[at, :].astype(F32)
                unit, inverse = unit_of(r_s[at, :])
                dr = dy_s[at, :].astype(F32) + norm_back(grad, unit, inverse, own_gain[1])
                r_s[at, :] = dr
                drb_s[at, :] = dr.astype(BF16)
                acc_s[1] += fold(grad * unit)
                acc_s[3] += fold(grad)
                acc_s[4] += fold(dr)

            by_strips(i, back_norm)
            do_s[0:rows, :] = dot_nt(drb_s[at_rows(i), :], wp_s[...]).astype(BF16)
            for h in range(HEADS):
                qc, kc, vc, oc = head_at(h)
                weights = p_s[i * HEADS + h, 0:rows, 0:span]
                grad_o = do_s[0:rows, oc]
                keys = qkv_s[key_rows(i), kc]
                slope = dot_nt(grad_o, qkv_s[key_rows(i), vc])
                ds = (weights * (slope - jnp.sum(slope * weights, axis=-1, keepdims=True))).astype(BF16)
                dq = dot(ds, keys).astype(BF16) * (HEAD**-0.5)
                dk = dot_tn(ds, qkv_s[q_rows(i), qc])
                dv = dot_tn(weights.astype(BF16), grad_o)
                dq_s[at_rows(i), qc] = dq.astype(BF16)
                if text:
                    hc = slice(h * HEAD, (h + 1) * HEAD)
                    hv = slice((HEADS + h) * HEAD, (HEADS + h + 1) * HEAD)
                    dkv_s[key_rows(i), hc] += dk
                    dkv_s[key_rows(i), hv] += dv
                else:
                    dq_s[at_rows(i), kc] = dk.astype(BF16)
                    dq_s[at_rows(i), vc] = dv.astype(BF16)

        def send_c(i):
            if text:
                for s in range(2):
                    k0 = s * QKV + WIDE
                    dq_s[at_rows(i), k0 : k0 + WIDE] = dkv_s[q_rows(i), s * WIDE : (s + 1) * WIDE].astype(BF16)
                    v0 = 2 * WIDE + s * WIDE
                    dq_s[at_rows(i), k0 + WIDE : k0 + 2 * WIDE] = dkv_s[q_rows(i), v0 : v0 + WIDE].astype(BF16)
            grad = dq_s[at_rows(i), 0 : 2 * QKV]
            send_s[at_rows(i), :] = dot_nt(grad, wq_s[...]).astype(BF16)
            swap(i, rc_s, K_C).start()
            for s in range(2):
                acc_s[8 + s, :, 0:QKV] += fold(grad[:, s * QKV : (s + 1) * QKV].astype(F32))

        def own_img(i):
            return img_out.at[pl.ds(pl.multiple_of(core * n_img + i * rows_i, 16), rows_i)]

        def own_txt(i):
            return txt_out.at[pl.ds(pl.multiple_of(core * n_txt + i * rows_t, 16), rows_t)]

        def img_copies(i):
            src = fin_s.at[pl.ds(pl.multiple_of(i * rows_i, 16), rows_i)]
            return local(src, own_img(i), 8 + i), remote(src, own_img(i), K_OI, i, sib)

        def txt_copies(i):
            src = ys_s.at[pl.ds(pl.multiple_of(i * rows_t, 16), rows_t)]
            return local(src, own_txt(i), 12 + i), remote(src, own_txt(i), K_OT, i, sib)

        def dx_copies(i):
            src = rb_s.at[pl.ds(pl.multiple_of(i * rows_t, 16), rows_t)]
            return remote(src, own_txt(i), K_T1, i, across)

        def dx_relay(i):
            return remote(own_txt(i), own_txt(i), K_OT, i, sib)

        if text:

            def own_y(i):
                y_copies(i)[0].wait()
                at = at_rows(i)
                ys_s[at, :] = (ys_s[at, :].astype(F32) + yt_s[at, :].astype(F32)).astype(BF16)
                for cp in txt_copies(i):
                    cp.start()

            def image_y(i):
                at = pl.ds(pl.multiple_of(i * rows_i, 16), rows_i)
                y_relay(i).wait()
                fin_s[at, :] = (y1_s[at, :].astype(F32) + y2_s[at, :].astype(F32)).astype(BF16)
                for cp in img_copies(i):
                    cp.start()

        def last(i):
            swap(i, rc_s, K_C).wait()

            def body(at):
                grad = send_s[at, :].astype(F32) + rc_s[at, :].astype(F32)
                unit, inverse = unit_of(x_s[at, :].astype(F32))
                dx = (r_s[at, :] + norm_back(grad, unit, inverse, own_gain[0])).astype(BF16)
                if text:
                    rb_s[at, :] = dx
                else:
                    fin_s[at, :] = dx
                acc_s[0] += fold(grad * unit)
                acc_s[2] += fold(grad)

            by_strips(i, body)

            for cp in [dx_copies(i)] if text else img_copies(i):
                cp.start()

        if text:
            hand_on(0)
            hand_on(1)
        if text:

            def backward(i):
                @pl.when(i < CHUNKS)
                def _():
                    attend_back(i)

                @pl.when(i == CHUNKS - 1)
                def _():
                    z_middle(2)

                @pl.when(i > 0)
                def _():
                    send_c(i - 1)

                @pl.when(i > 2)
                def _():
                    last(i - 3)

            loop(CHUNKS + 1, backward)
        else:

            def backward(i):
                @pl.when(i == CHUNKS - 1)
                def _():
                    z_middle(2)

                attend_back(i)
                send_c(i)

            loop(CHUNKS, backward)

        def mixed_grads(at, s):
            first = dot_tn(a1_s[0:total, at], dq_s[0:total, s * QKV : (s + 1) * QKV])
            second = dot_tn(drb_s[0:total, at], o_s[0:total, s * MIX : (s + 1) * MIX])
            seam = first[:, MIX * 2 :] + second[:, 0 : QKV - 2 * MIX]
            return jnp.concatenate([first[:, : MIX * 2], seam, second[:, QKV - 2 * MIX :]], axis=1)

        if text:
            loop(CHUNKS, lambda i: y_copies(i)[0].start())
        end_x = grads_pair(0, mixed_grads)
        end_x()
        z_start(0)
        if text:
            last(CHUNKS - 2)
            last(CHUNKS - 1)
            hand_on(2)
            hand_on(3)
            z_middle(1)
            loop(CHUNKS, own_y)
            z_middle(0)
        else:
            z_middle(1)
            loop(CHUNKS - 1, last)
            z_middle(0)
            last(CHUNKS - 1)


        order = (0, 1, 2, 3, 4, 5, 7, 6, 9, 8, 10, 11, 12, 13, 14, 15)
        sums = jnp.sum(acc_s[...], axis=1)
        vec_s[0] = sums
        for row, src in enumerate(order):
            vec_s[1, row : row + 1, :] = sums[src : src + 1, :]
        v_sib = remote(vec_s.at[1], vrec_s, K_S, 1, sib)
        v_sib.start()
        z_finish(2)
        z_finish(1)
        v_sib.wait()
        vec_s[0] = vec_s[0] + vrec_s[...]
        if z_inside:
            vall_s[d] = vec_s[0]

            def v_copy(k):
                to = lax.rem(d + k, dp_size)
                return remote(vec_s.at[0], vall_s.at[d], K_V, k - 1, (p, to, t))

            for k in offsets:
                v_copy(k).start()
        if text:
            loop(CHUNKS, image_y)
        z_finish(0)
        if z_inside:
            for k in offsets:
                v_copy(k).wait_send()
            for k in offsets:
                back = lax.rem(d + dp_size - k, dp_size)
                remote(vall_s.at[back], vall_s.at[back], K_V, k - 1, (p, back, t)).wait_recv()
            totals = vall_s[0]
            for k in range(1, dp_size):
                totals = totals + vall_s[k]
            vec_out[...] = totals
        else:
            vec_out[...] = vec_s[0]

        def finish(i):
            if text:
                dy_to_image(i).wait_send()
                dx_copies(i).wait_send()
                here, there = txt_copies(i)
                here.wait()
                there.wait()
            else:
                x_to_text(i).wait_send()
                for cp in y_copies(i):
                    cp.wait_send()
                dx_copies(i).wait_recv()
                dx_relay(i).start()
            here, there = img_copies(i)
            here.wait()
            there.wait()

        loop(CHUNKS, finish)
        if not text:
            loop(CHUNKS, lambda i: dx_relay(i).wait())
        for a in range(3):
            z_end(a)

    @pl.when(image_here)
    def _():
        one_layer(False)

    @pl.when(jnp.logical_not(image_here))
    def _():
        one_layer(True)


def per_device(
    image_side, text_side, caption_lengths, norm_gains, norm_shifts, w_qkv, bias_qv, w_proj, out_bias, w_up, bias_up, w_down,
):
    dp_size = lax.axis_size("dp")
    core = lax.rem(lax.axis_index("tensor"), 2)
    images, keys_i, width = image_side.shape[1:]
    blocks, length = text_side.shape[1:3]
    per_core = images // 2
    rows_i = -(-(per_core // CHUNKS * keys_i) // 16) * 16
    rows_t = length * (blocks // 2) // CHUNKS
    share = width // dp_size
    z_inside = dp_size == 4 and share % 16 == 0

    img = lax.dynamic_slice_in_dim(image_side[0], core * per_core, per_core, 0)
    img = jnp.pad(img, ((0, 0), (0, rows_i - keys_i), (0, 0))).reshape(per_core * rows_i, width)
    txt = lax.dynamic_slice_in_dim(text_side[0], core, 1, 0)[0]
    bounds = jnp.cumsum(lax.dynamic_slice_in_dim(caption_lengths, core, 1, 0)[0])
    places = jnp.arange(length, dtype=jnp.int32)
    segment = jnp.sum((places[:, None] >= bounds[None, :]).astype(jnp.int32), axis=1)
    seg_col = segment[:, None]
    seg_row = jnp.pad(segment, (rows_t, rows_t), constant_values=-1)[None]
    wq = jnp.pad(w_qkv[0].reshape(width, 3 * WIDE), ((0, 0), (0, QKV - 3 * WIDE)))
    lane = jnp.zeros((WIDE,), F32)
    small = jnp.concatenate([bias_up[0], bias_qv[0, 0], lane, bias_qv[0, 1], jnp.zeros((QKV - 3 * WIDE,), F32)])
    small = jnp.broadcast_to(small[None], (8, small.shape[0]))

    n_i, n_t = rows_i * CHUNKS, rows_t * CHUNKS
    columns = (width, width, width)
    sds = jax.ShapeDtypeStruct
    grad_type = (lambda w: sds((share, w), F32)) if z_inside else (lambda w: sds((width, w), BF16))
    outs = [sds((2 * n_i, width), BF16), sds((2 * n_t, width), BF16)]
    outs += [grad_type(w) for w in columns] + [sds((16, width), F32)]
    any_spec, vmem_spec = pl.BlockSpec(memory_space=pl.ANY), pl.BlockSpec(memory_space=pltpu.VMEM)
    v = pltpu.VMEM
    scratch = [
        v((n_i, width), BF16), v((n_i, width), BF16),
        v((width, 2 * QKV), BF16), v((2 * MIX, width), BF16), v((width, 2 * width), BF16), v((2 * width, width), BF16),
        v((2, 8, width + QKV), F32),
        v((n_i, width), BF16), v((max(n_i, n_t + 2 * rows_t), 2 * QKV), BF16), v((n_i, 2 * MIX), BF16), v((n_i, width), F32),
        v((n_i, width), BF16), v((n_i, 2 * width), BF16), v((n_i, 2 * width), BF16),
        v((CHUNKS * HEADS, max(rows_i, rows_t), max(-(-rows_i // 128) * 128, 3 * rows_t)), F32),
        v((n_t + 2 * rows_t, 2 * HEADS * HEAD), F32), v((max(rows_i, rows_t), 2 * MIX), BF16),
        v((n_i, width), BF16), v((n_i, width), BF16), v((n_i, width), BF16), v((n_i, width), BF16),
        v((n_i, width), BF16), v((n_t, width), BF16), v((n_i, width), BF16), v((n_i, width), BF16), v((n_i, width), BF16),
        v((16, 8, width), F32), v((2, 16, width), F32), v((16, width), F32), v((dp_size if z_inside else 1, 16, width), F32),
    ]
    scratch += [v((width, w), BF16) for w in columns] + [v((width, w), BF16) for w in columns]
    if z_inside:
        scratch += [v((3, 2, share, width), BF16), v((3, share, width), BF16), v((3, share, width), F32)]
    dma = pltpu.SemaphoreType.DMA
    scratch += [dma((4 * N_KINDS,)), dma((4 * N_KINDS,)), dma((24,))]
    img_out, txt_out, g_x, g_u, g_d, vec = pl.pallas_call(
        partial(layers_kernel, rows_i, rows_t, keys_i, dp_size, z_inside),
        out_shape=outs,
        in_specs=[any_spec] * 7 + [vmem_spec] * 5,
        out_specs=[any_spec] * 5 + [vmem_spec],
        scratch_shapes=scratch,
        compiler_params=pltpu.CompilerParams(collective_id=0, has_side_effects=True, vmem_limit_bytes=60 << 20),
    )(
        img, txt, wq, w_proj[0], w_up[0], w_down[0], small, norm_gains[0], norm_shifts[0], out_bias[0], seg_col, seg_row,
    )
    if not z_inside:
        def scatter(grad):
            return lax.psum_scatter(grad, "dp", scatter_dimension=0, tiled=True).astype(F32)

        g_x, g_u, g_d = (scatter(g) for g in (g_x, g_u, g_d))
        vec = lax.psum(vec, "dp")
    image_result = img_out.reshape(images, rows_i, width)[:, :keys_i][None]
    text_result = txt_out.reshape(blocks, length, width)[None]
    return (
        image_result,
        text_result,
        vec[0:2][None],
        vec[2:4][None],
        g_x[:, : 3 * WIDE].reshape(share, 3, WIDE)[None],
        jnp.stack([vec[8, 0:WIDE], vec[8, 2 * WIDE : 3 * WIDE]])[None],
        g_x[:, 3 * WIDE :].T[None],
        vec[4:6][None],
        g_u[None],
        vec[6][None],
        g_d.T[None],
    )


def solution(mesh):
    placed = (
        P("pipe", "dp", None, None),
        P("pipe", "dp", None, None),
        P("dp", None),
        P("pipe", None, None),
        P("pipe", None, None),
        P("pipe", None, None, "tensor"),
        P("pipe", None, "tensor"),
        P("pipe", "tensor", None),
        P("pipe", None, None),
        P("pipe", None, "tensor"),
        P("pipe", "tensor"),
        P("pipe", "tensor", None),
    )
    return jax.shard_map(
        per_device,
        mesh=mesh,
        in_specs=placed,
        out_specs=(
            P("pipe", "dp", None, None),
            P("pipe", "dp", None, None),
            P("pipe", None, None),
            P("pipe", None, None),
            P("pipe", "dp", None, "tensor"),
            P("pipe", None, "tensor"),
            P("pipe", "tensor", "dp"),
            P("pipe", None, None),
            P("pipe", "dp", "tensor"),
            P("pipe", "tensor"),
            P("pipe", "tensor", "dp"),
        ),
        check_vma=False,
    )
```

```python
from functools import partial

import jax
import jax.numpy as jnp
from jax import lax
from jax.experimental import pallas as pl
from jax.experimental.pallas import tpu as pltpu
from jax.sharding import PartitionSpec as P

F32 = jnp.float32
BF16 = jnp.bfloat16
BY_MESH = pl.DeviceIdType.MESH
HEAD = 64
HALF = 3
HEADS = 2 * HALF
WIDE = HALF * HEAD
EPSILON = 1e-06
MASKED = -1000000000.0
CHUNKS = 4
STRIP = 16
STEP = 64
BLOCK = 208
QKV = 640
MIX = 256
PAD = MIX - WIDE
TILE = 256

K_IN, K_A, K_B, K_C, K_Y1, K_Y2, K_YT, K_OI, K_OT, K_T1, K_W, K_S, K_G, K_V, K_Z = range(15)
N_KINDS = K_Z + 3


def dot(a, b):
    return lax.dot_general(a, b, (((1,), (0,)), ((), ())), preferred_element_type=F32)


def dot_nt(a, b):
    return lax.dot_general(a, b, (((1,), (1,)), ((), ())), preferred_element_type=F32)


def dot_tn(a, b):
    return lax.dot_general(a, b, (((0,), (0,)), ((), ())), preferred_element_type=F32)


def loop(count, body):
    def step(j, carry):
        body(j)
        return carry

    lax.fori_loop(0, count, step, 0)


def unit_of(rows):
    centre = rows - jnp.mean(rows, axis=-1, keepdims=True)
    inverse = lax.rsqrt(jnp.mean(centre * centre, axis=-1, keepdims=True) + EPSILON)
    return centre * inverse, inverse


def norm_back(grad, unit, inverse, gain):
    scaled = grad * gain
    first = jnp.mean(scaled, axis=-1, keepdims=True)
    second = jnp.mean(scaled * unit, axis=-1, keepdims=True)
    return inverse * (scaled - first - unit * second)


def gelu_pair(u):
    cdf = 0.5 * (1.0 + lax.erf(u * (0.5**0.5)))
    pdf = jnp.exp(u * u * -0.5) * 0.3989422804014327
    return u * cdf, cdf + u * pdf


def fold(rows):
    return jnp.sum(rows.reshape(rows.shape[0] // 8, 8, rows.shape[1]), axis=0)


def layers_kernel(
    rows_i, rows_t, keys_i, dp_size, z_inside,
    img_own, txt_all, w_qkv, w_proj, w_up, w_down, lengths, gains, shifts, outb, bias_up, bias_qv,
    img_out, txt_out, g_mix, g_up, g_down, vec_out,
    x_s, dy_s, wq_s, wp_s, wu_s, wd_s, small_s, seg_s, a1_s, qkv_s, o_s, r_s, a2_s, gb_s, du_s, p_s, dkv_s, do_s,
    send_s, ra_s, rb_s, rc_s, ys_s, yt_s, y1_s, y2_s, fin_s, acc_s, vec_s, vrec_s, vall_s,
    gs_x, gs_u, gs_d, gr_x, gr_u, gr_d, *rest,
):
    if z_inside:
        z1_s, z2_s, zf_s, ssem, rsem, lsem = rest
    else:
        ssem, rsem, lsem = rest
    width = x_s.shape[1]
    p, d, t = lax.axis_index("pipe"), lax.axis_index("dp"), lax.axis_index("tensor")
    core = lax.rem(t, 2)
    sib_t = t + 1 - 2 * core
    peer_t = lax.rem(t + 2, 4)
    other = 1 - p
    sib, peer = (p, d, sib_t), (p, d, peer_t)
    across = (other, d, t)
    txt_own = txt_all.at[core]
    offsets = range(1, dp_size) if z_inside else range(0)
    partners = [sib, peer, across]
    partners += [(p, lax.rem(d + k, dp_size), t) for k in offsets]

    def remote(src, dst, kind, slot, to):
        at = kind * 4 + slot
        return pltpu.make_async_remote_copy(
            src_ref=src, dst_ref=dst, send_sem=ssem.at[at], recv_sem=rsem.at[at],
            device_id=to, device_id_type=BY_MESH,
        )

    def local(src, dst, slot):
        return pltpu.make_async_copy(src, dst, lsem.at[slot])

    image_here = p == 0
    n_img = rows_i * CHUNKS
    n_txt = rows_t * CHUNKS

    wq_own = local(w_qkv, wq_s.at[0 : 3 * WIDE], 0)
    wp_own = local(w_proj, wp_s.at[PAD:MIX], 1)
    wu_own = local(w_up, wu_s.at[:, 0:width], 2)
    wd_own = local(w_down, wd_s.at[0:width], 3)
    img_in = local(img_own, x_s, 5)
    txt_in = local(txt_own, dy_s.at[0:n_txt], 6)
    wq_own.start()

    @pl.when(image_here)
    def _():
        img_in.start()

    @pl.when(jnp.logical_not(image_here))
    def _():
        txt_in.start()

    wp_own.start()
    wu_own.start()
    wd_own.start()
    zero_rows = jnp.zeros((PAD, width), BF16)
    wp_s[0:PAD, :] = zero_rows
    wp_s[MIX : MIX + PAD, :] = zero_rows
    zero_rows = jnp.zeros((QKV - 3 * WIDE, width), BF16)
    wq_s[3 * WIDE : QKV, :] = zero_rows
    wq_s[QKV + 3 * WIDE :, :] = zero_rows
    acc_s[...] = jnp.zeros_like(acc_s)
    small_s[0] = jnp.zeros_like(small_s[0])
    small_s[0, 0:1, 0:width] = bias_up[...]
    small_s[0, 0:1, width : width + WIDE] = bias_qv[0:1, :]
    small_s[0, 0:1, width + 2 * WIDE : width + 3 * WIDE] = bias_qv[1:2, :]

    barrier = pltpu.get_barrier_semaphore()
    for to in partners:
        pl.semaphore_signal(barrier, inc=1, device_id=to, device_id_type=BY_MESH)
    pl.semaphore_wait(barrier, len(partners))

    sm_sib = remote(small_s.at[0], small_s.at[1], K_S, 0, sib)
    wq_sib = remote(w_qkv, wq_s.at[QKV : QKV + 3 * WIDE], K_W, 0, sib)
    wp_sib = remote(w_proj, wp_s.at[MIX + PAD :], K_W, 1, sib)
    wu_sib = remote(w_up, wu_s.at[:, width:], K_W, 2, sib)
    wd_sib = remote(w_down, wd_s.at[width:], K_W, 3, sib)

    def x_to_text(i):
        rows = pl.ds(pl.multiple_of(i * rows_t, 16), rows_t)
        return remote(txt_own.at[rows], x_s.at[rows], K_IN, i, across)

    def dy_to_image(i):
        rows = pl.ds(pl.multiple_of(i * rows_i, 16), rows_i)
        return remote(img_own.at[rows], dy_s.at[rows], K_IN, i, across)

    @pl.when(image_here)
    def _():
        loop(CHUNKS, lambda i: x_to_text(i).start())

    sm_sib.start()
    wq_sib.start()

    @pl.when(jnp.logical_not(image_here))
    def _():
        loop(CHUNKS, lambda i: dy_to_image(i).start())

    wp_sib.start()
    wu_sib.start()
    wd_sib.start()

    own_gain = [gains[0:1, :], gains[1:2, :]]
    own_shift = [shifts[0:1, :], shifts[1:2, :]]

    g_arrays = [(gs_x, gr_x, g_mix), (gs_u, gr_u, g_up), (gs_d, gr_d, g_down)]

    def g_exchange(a):
        return remote(g_arrays[a][0], g_arrays[a][1], K_G, a, sib)

    def grads_pair(a, product):
        mine, theirs = g_arrays[a][0:2]
        tiles = width // TILE

        def send_half(m):
            at = pl.ds(pl.multiple_of(m * TILE, TILE), TILE)
            mine[at, :] = product(at, 1).astype(BF16)

        loop(tiles, send_half)
        g_exchange(a).start()

        def finish():
            g_exchange(a).wait()

            def own_half(m):
                at = pl.ds(pl.multiple_of(m * TILE, TILE), TILE)
                mine[at, :] = (product(at, 0) + theirs[at, :].astype(F32)).astype(BF16)

            loop(tiles, own_half)

        return finish

    share = width // dp_size
    parity = lax.rem(d, 2)
    upper = d // 2
    near = d + 1 - 2 * parity
    far = d + 2 - 4 * upper if z_inside else d

    def share_rows(at):
        return pl.ds(pl.multiple_of(at * share, 16), share)

    def z_near(a, k):
        src = g_arrays[a][0].at[share_rows(1 - parity + 2 * k)]
        return remote(src, z1_s.at[a, k], K_Z, 3 * k + a, (p, near, t))

    def z_far(a):
        return remote(g_arrays[a][0].at[share_rows(far)], z2_s.at[a], K_Z, 6 + a, (p, far, t))

    def z_start(a):
        if z_inside:
            for k in range(2):
                z_near(a, k).start()
        else:
            local(g_arrays[a][0], g_arrays[a][2], 20 + a).start()

    def z_middle(a):
        if z_inside:
            for k in range(2):
                z_near(a, k).wait()
            mine = g_arrays[a][0]
            rows = share_rows(far)
            mine[rows, :] = (mine[rows, :].astype(F32) + z1_s[a, 1 - upper].astype(F32)).astype(BF16)
            z_far(a).start()

    def z_finish(a):
        if z_inside:
            z_far(a).wait()
            total = g_arrays[a][0][share_rows(d), :].astype(F32) + z1_s[a, upper].astype(F32)
            zf_s[a] = total + z2_s[a].astype(F32)
            local(zf_s.at[a], g_arrays[a][2], 20 + a).start()

    def z_end(a):
        if z_inside:
            local(zf_s.at[a], g_arrays[a][2], 20 + a).wait()
        else:
            local(g_arrays[a][0], g_arrays[a][2], 20 + a).wait()

    def one_layer(text):
        rows = rows_t if text else rows_i
        total = rows * CHUNKS
        cuts = [(o, min(BLOCK, rows - o)) for o in range(0, rows, BLOCK)]
        q_off = rows_t if text else 0

        def at_rows(i):
            return pl.ds(pl.multiple_of(i * rows, 16), rows)

        def q_rows(i):
            return pl.ds(pl.multiple_of(i * rows + q_off, 16), rows)

        def by_strips(i, body):
            for o, size in cuts:
                body(pl.ds(pl.multiple_of(i * rows + o, STRIP), size))

        def swap(i, landing, kind):
            return remote(send_s.at[at_rows(i)], landing.at[at_rows(i)], kind, i, peer)

        incoming = dy_to_image if not text else x_to_text

        def wait_input(i):
            cp = remote(x_s.at[at_rows(i)] if text else dy_s.at[at_rows(i)],
                        x_s.at[at_rows(i)] if text else dy_s.at[at_rows(i)], K_IN, i, across)
            cp.wait_recv()

        wq_own.wait()
        wq_sib.wait()
        sm_sib.wait()
        def caption(places):
            bound = lengths[core, 0]
            segment = (places >= bound).astype(jnp.int32)
            for k in range(1, lengths.shape[1]):
                bound = bound + lengths[core, k]
                segment = segment + (places >= bound).astype(jnp.int32)
            return segment

        if text:
            places = lax.broadcasted_iota(jnp.int32, (8, total + 2 * rows_t), 1) - rows_t
            seg_s[...] = jnp.where(places < 0, -1, caption(places))
            txt_in.wait()
            pad = jnp.zeros((rows_t, 2 * QKV), BF16)
            qkv_s[0:rows_t, :] = pad
            qkv_s[rows_t + total : 2 * rows_t + total, :] = pad
            dkv_s[...] = jnp.zeros_like(dkv_s)
        else:
            img_in.wait()
        for s in range(2):
            o_s[0:total, s * MIX : s * MIX + PAD] = jnp.zeros((total, PAD), BF16)

        def project(i):
            if text:
                wait_input(i)

            def first_norm(at):
                unit, _ = unit_of(x_s[at, :].astype(F32))
                a1_s[at, :] = (unit * own_gain[0] + own_shift[0]).astype(BF16)

            by_strips(i, first_norm)
            left = a1_s[at_rows(i), :]
            lanes = lax.broadcasted_iota(jnp.int32, (1, QKV), 1)
            factor = jnp.where(lanes < WIDE, HEAD**-0.5, 1.0).astype(F32)
            for s in range(2):
                value = dot_nt(left, wq_s[s * QKV : (s + 1) * QKV, :])
                value = (value + small_s[s, 0:1, width : width + QKV]) * factor
                qkv_s[q_rows(i), s * QKV : (s + 1) * QKV] = value.astype(BF16)

        def head_at(h):
            s, hh = h // HALF, h % HALF
            base = s * QKV + hh * HEAD
            return slice(base, base + HEAD), slice(base + WIDE, base + WIDE + HEAD), slice(base + 2 * WIDE, base + 2 * WIDE + HEAD), slice(s * MIX + PAD + hh * HEAD, s * MIX + PAD + hh * HEAD + HEAD)

        span = 3 * rows_t if text else rows_i

        def key_rows(i):
            return pl.ds(pl.multiple_of(i * rows, 16), span)

        def allowed(i):
            if text:
                mine = caption(lax.broadcasted_iota(jnp.int32, (rows, 1), 0) + i * rows)
                keys = seg_s[0:1, pl.ds(pl.multiple_of(i * rows_t, 128), span)]
                return mine == keys
            return lax.broadcasted_iota(jnp.int32, (1, span), 1) < keys_i

        def attend(i):
            ok = allowed(i)
            for h in range(HEADS):
                qc, kc, vc, oc = head_at(h)
                scores = dot_nt(qkv_s[q_rows(i), qc], qkv_s[key_rows(i), kc])
                scores = jnp.where(ok, scores, MASKED)
                raised = jnp.exp(scores - jnp.max(scores, axis=-1, keepdims=True))
                weights = raised * (1.0 / jnp.sum(raised, axis=-1, keepdims=True))
                p_s[i * HEADS + h, 0:rows, 0:span] = weights
                mixed = dot(weights.astype(BF16), qkv_s[key_rows(i), vc])
                o_s[at_rows(i), oc] = mixed.astype(BF16)

        def send_a(i):
            send_s[at_rows(i), :] = dot(o_s[at_rows(i), :], wp_s[...]).astype(BF16)
            swap(i, ra_s, K_A).start()

        if text:

            def forward(i):
                @pl.when(i < CHUNKS)
                def _():
                    project(i)

                @pl.when(i == 1)
                def _():
                    wp_own.wait()
                    wp_sib.wait()

                @pl.when(i > 0)
                def _():
                    attend(i - 1)
                    send_a(i - 1)

            loop(CHUNKS + 1, forward)
        else:

            def forward(i):
                project(i)
                attend(i)

                @pl.when(i == 0)
                def _():
                    wp_own.wait()
                    wp_sib.wait()

                send_a(i)

            loop(CHUNKS, forward)
        wu_own.wait()
        wu_sib.wait()
        wd_own.wait()
        wd_sib.wait()

        def y_copies(i):
            at = at_rows(i)
            if text:
                return [remote(ys_s.at[at], yt_s.at[at], K_YT, i, peer)]
            return [remote(ys_s.at[at], y1_s.at[at], K_Y1, i, across)]

        def y_relay(i):
            at = pl.ds(pl.multiple_of(i * rows_i, 16), rows_i)
            return remote(y1_s.at[at], y2_s.at[at], K_Y2, i, peer)

        def hand_on(i):
            at = pl.ds(pl.multiple_of(i * rows_i, 16), rows_i)
            remote(y1_s.at[at], y1_s.at[at], K_Y1, i, across).wait_recv()
            y_relay(i).start()

        def middle(i):
            if not text:
                wait_input(i)
            swap(i, ra_s, K_A).wait()

            def second_norm(at):
                r = x_s[at, :].astype(F32) + (send_s[at, :].astype(F32) + ra_s[at, :].astype(F32)) + outb[0:1, :]
                r_s[at, :] = r
                unit, _ = unit_of(r)
                a2_s[at, :] = (unit * own_gain[1] + own_shift[1]).astype(BF16)
                acc_s[5] += fold(dy_s[at, :].astype(F32))

            by_strips(i, second_norm)
            left = a2_s[at_rows(i), :]
            grad = dy_s[at_rows(i), :]
            for n in range(2 * width // TILE):
                cols = slice(n * TILE, (n + 1) * TILE)
                s, inner = (n * TILE) // width, (n * TILE) % width
                u = dot(left, wu_s[:, cols]) + small_s[s, 0:1, inner : inner + TILE]
                g, slope = gelu_pair(u)
                gb_s[at_rows(i), cols] = g.astype(BF16)
                du = (dot_nt(grad, wd_s[cols, :]) * slope).astype(BF16)
                du_s[at_rows(i), cols] = du
                acc_s[6 + s, :, inner : inner + TILE] += fold(du.astype(F32))
            send_s[at_rows(i), :] = dot_nt(du_s[at_rows(i), :], wu_s[...]).astype(BF16)
            swap(i, rb_s, K_B).start()
            lower = dot(gb_s[at_rows(i), :], wd_s[...])
            ys_s[at_rows(i), :] = (lower + 0.5 * (r_s[at_rows(i), :] + outb[1:2, :])).astype(BF16)
            if not text:
                for cp in y_copies(i):
                    cp.start()

        loop(CHUNKS, middle)
        end_d = grads_pair(2, lambda at, s: dot_tn(dy_s[0:total, at], gb_s[0:total, s * width : (s + 1) * width]))
        end_u = grads_pair(1, lambda at, s: dot_tn(a2_s[0:total, at], du_s[0:total, s * width : (s + 1) * width]))
        end_d()
        z_start(2)
        end_u()
        z_start(1)

        dq_s, drb_s = gb_s, a2_s
        for s in range(2):
            dq_s[0:total, s * QKV + 3 * WIDE : (s + 1) * QKV] = jnp.zeros((total, QKV - 3 * WIDE), BF16)

        def attend_back(i):
            swap(i, rb_s, K_B).wait()

            def back_norm(at):
                grad = send_s[at, :].astype(F32) + rb_s[at, :].astype(F32)
                unit, inverse = unit_of(r_s[at, :])
                dr = dy_s[at, :].astype(F32) + norm_back(grad, unit, inverse, own_gain[1])
                r_s[at, :] = dr
                drb_s[at, :] = dr.astype(BF16)
                acc_s[1] += fold(grad * unit)
                acc_s[3] += fold(grad)
                acc_s[4] += fold(dr)

            by_strips(i, back_norm)
            do_s[0:rows, :] = dot_nt(drb_s[at_rows(i), :], wp_s[...]).astype(BF16)
            for h in range(HEADS):
                qc, kc, vc, oc = head_at(h)
                weights = p_s[i * HEADS + h, 0:rows, 0:span]
                grad_o = do_s[0:rows, oc]
                keys = qkv_s[key_rows(i), kc]
                slope = dot_nt(grad_o, qkv_s[key_rows(i), vc])
                ds = (weights * (slope - jnp.sum(slope * weights, axis=-1, keepdims=True))).astype(BF16)
                dq = dot(ds, keys).astype(BF16) * (HEAD**-0.5)
                dk = dot_tn(ds, qkv_s[q_rows(i), qc])
                dv = dot_tn(weights.astype(BF16), grad_o)
                dq_s[at_rows(i), qc] = dq.astype(BF16)
                if text:
                    hc = slice(h * HEAD, (h + 1) * HEAD)
                    hv = slice((HEADS + h) * HEAD, (HEADS + h + 1) * HEAD)
                    dkv_s[key_rows(i), hc] += dk
                    dkv_s[key_rows(i), hv] += dv
                else:
                    dq_s[at_rows(i), kc] = dk.astype(BF16)
                    dq_s[at_rows(i), vc] = dv.astype(BF16)

        def send_c(i):
            if text:
                for s in range(2):
                    k0 = s * QKV + WIDE
                    dq_s[at_rows(i), k0 : k0 + WIDE] = dkv_s[q_rows(i), s * WIDE : (s + 1) * WIDE].astype(BF16)
                    v0 = 2 * WIDE + s * WIDE
                    dq_s[at_rows(i), k0 + WIDE : k0 + 2 * WIDE] = dkv_s[q_rows(i), v0 : v0 + WIDE].astype(BF16)
            grad = dq_s[at_rows(i), 0 : 2 * QKV]
            send_s[at_rows(i), :] = dot(grad, wq_s[...]).astype(BF16)
            swap(i, rc_s, K_C).start()
            for s in range(2):
                acc_s[8 + s, :, 0:QKV] += fold(grad[:, s * QKV : (s + 1) * QKV].astype(F32))

        def own_img(i):
            return img_out.at[pl.ds(pl.multiple_of(core * n_img + i * rows_i, 16), rows_i)]

        def own_txt(i):
            return txt_out.at[pl.ds(pl.multiple_of(core * n_txt + i * rows_t, 16), rows_t)]

        def img_copies(i):
            src = fin_s.at[pl.ds(pl.multiple_of(i * rows_i, 16), rows_i)]
            return local(src, own_img(i), 8 + i), remote(src, own_img(i), K_OI, i, sib)

        def txt_copies(i):
            src = ys_s.at[pl.ds(pl.multiple_of(i * rows_t, 16), rows_t)]
            return local(src, own_txt(i), 12 + i), remote(src, own_txt(i), K_OT, i, sib)

        def dx_copies(i):
            src = rb_s.at[pl.ds(pl.multiple_of(i * rows_t, 16), rows_t)]
            return remote(src, own_txt(i), K_T1, i, across)

        def dx_relay(i):
            return remote(own_txt(i), own_txt(i), K_OT, i, sib)

        if text:

            def own_y(i):
                y_copies(i)[0].wait()
                at = at_rows(i)
                ys_s[at, :] = (ys_s[at, :].astype(F32) + yt_s[at, :].astype(F32)).astype(BF16)
                for cp in txt_copies(i):
                    cp.start()

            def image_y(i):
                at = pl.ds(pl.multiple_of(i * rows_i, 16), rows_i)
                y_relay(i).wait()
                fin_s[at, :] = (y1_s[at, :].astype(F32) + y2_s[at, :].astype(F32)).astype(BF16)
                for cp in img_copies(i):
                    cp.start()

        def last(i):
            swap(i, rc_s, K_C).wait()

            def body(at):
                grad = send_s[at, :].astype(F32) + rc_s[at, :].astype(F32)
                unit, inverse = unit_of(x_s[at, :].astype(F32))
                dx = (r_s[at, :] + norm_back(grad, unit, inverse, own_gain[0])).astype(BF16)
                if text:
                    rb_s[at, :] = dx
                else:
                    fin_s[at, :] = dx
                acc_s[0] += fold(grad * unit)
                acc_s[2] += fold(grad)

            by_strips(i, body)

            for cp in [dx_copies(i)] if text else img_copies(i):
                cp.start()

        if text:
            hand_on(0)
            hand_on(1)
        if text:

            def backward(i):
                @pl.when(i < CHUNKS)
                def _():
                    attend_back(i)

                @pl.when(i == CHUNKS - 1)
                def _():
                    z_middle(2)

                @pl.when(i > 0)
                def _():
                    send_c(i - 1)

                @pl.when(i > 2)
                def _():
                    last(i - 3)

            loop(CHUNKS + 1, backward)
        else:

            def backward(i):
                @pl.when(i == CHUNKS - 1)
                def _():
                    z_middle(2)

                attend_back(i)
                send_c(i)

            loop(CHUNKS, backward)

        def mixed_grads(at, s):
            first = dot_tn(a1_s[0:total, at], dq_s[0:total, s * QKV : (s + 1) * QKV])
            second = dot_tn(drb_s[0:total, at], o_s[0:total, s * MIX : (s + 1) * MIX])
            seam = first[:, MIX * 2 :] + second[:, 0 : QKV - 2 * MIX]
            return jnp.concatenate([first[:, : MIX * 2], seam, second[:, QKV - 2 * MIX :]], axis=1)

        if text:
            loop(CHUNKS, lambda i: y_copies(i)[0].start())
        end_x = grads_pair(0, mixed_grads)
        end_x()
        z_start(0)
        if text:
            last(CHUNKS - 2)
            last(CHUNKS - 1)
            hand_on(2)
            hand_on(3)
            z_middle(1)
            loop(CHUNKS, own_y)
            z_middle(0)
        else:
            z_middle(1)
            loop(CHUNKS - 1, last)
            z_middle(0)
            last(CHUNKS - 1)


        order = (0, 1, 2, 3, 4, 5, 7, 6, 9, 8, 10, 11, 12, 13, 14, 15)
        sums = jnp.sum(acc_s[...], axis=1)
        vec_s[0] = sums
        for row, src in enumerate(order):
            vec_s[1, row : row + 1, :] = sums[src : src + 1, :]
        v_sib = remote(vec_s.at[1], vrec_s, K_S, 1, sib)
        v_sib.start()
        z_finish(2)
        z_finish(1)
        v_sib.wait()
        vec_s[0] = vec_s[0] + vrec_s[...]
        if z_inside:
            vall_s[d] = vec_s[0]

            def v_copy(k):
                to = lax.rem(d + k, dp_size)
                return remote(vec_s.at[0], vall_s.at[d], K_V, k - 1, (p, to, t))

            for k in offsets:
                v_copy(k).start()
        if text:
            loop(CHUNKS, image_y)
        z_finish(0)
        if z_inside:
            for k in offsets:
                v_copy(k).wait_send()
            for k in offsets:
                back = lax.rem(d + dp_size - k, dp_size)
                remote(vall_s.at[back], vall_s.at[back], K_V, k - 1, (p, back, t)).wait_recv()
            totals = vall_s[0]
            for k in range(1, dp_size):
                totals = totals + vall_s[k]
            vec_out[...] = totals
        else:
            vec_out[...] = vec_s[0]

        def finish(i):
            if text:
                dy_to_image(i).wait_send()
                dx_copies(i).wait_send()
                here, there = txt_copies(i)
                here.wait()
                there.wait()
            else:
                x_to_text(i).wait_send()
                for cp in y_copies(i):
                    cp.wait_send()
                dx_copies(i).wait_recv()
                dx_relay(i).start()
            here, there = img_copies(i)
            here.wait()
            there.wait()

        loop(CHUNKS, finish)
        if not text:
            loop(CHUNKS, lambda i: dx_relay(i).wait())
        for a in range(3):
            z_end(a)

    @pl.when(image_here)
    def _():
        one_layer(False)

    @pl.when(jnp.logical_not(image_here))
    def _():
        one_layer(True)


def finish_kernel(
    images, keys_i, rows_i, img_in, txt_in, g_x, g_u, g_d, vec,
    img_out, txt_out, gains, shifts, qkv, bias_qv, proj, outb, up, bias_up, down,
    buf, out_s, gx_s, qkv_s, txt_s, gu_s, gd_s, sem,
):
    plain = [(g_u, gu_s, up), (g_d, gd_s, down), (txt_in, txt_s, txt_out)]
    fetch = [pltpu.make_async_copy(src, mid, sem.at[k]) for k, (src, mid, dst) in enumerate(plain)]
    copies = [pltpu.make_async_copy(mid, dst, sem.at[5 + k]) for k, (src, mid, dst) in enumerate(plain)]
    gx_in = pltpu.make_async_copy(g_x, gx_s, sem.at[3])
    gx_in.start()
    blocks = [(o, min(STEP, rows_i - o)) for o in range(0, rows_i, STEP)]
    loads = [
        pltpu.make_async_copy(img_in.at[:, o : o + n], buf.at[:, o : o + n], sem.at[8 + k])
        for k, (o, n) in enumerate(blocks)
    ]
    for cp in loads:
        cp.start()
    for cp in fetch:
        cp.start()
    gains[...] = vec[0:2, :]
    shifts[...] = vec[2:4, :]
    outb[...] = vec[4:6, :]
    bias_up[...] = vec[6:7, :]
    bias_qv[0:1, :] = vec[8:9, 0:WIDE]
    bias_qv[1:2, :] = vec[8:9, 2 * WIDE : 3 * WIDE]
    gx_in.wait()
    proj[...] = gx_s[:, 3 * WIDE :].T
    for k in range(3):
        qkv_s[k] = gx_s[:, k * WIDE : (k + 1) * WIDE]
    q_out = pltpu.make_async_copy(qkv_s, qkv, sem.at[4])
    q_out.start()
    stores = []
    for k, (o, n) in enumerate(blocks):
        loads[k].wait()
        rows = min(n, keys_i - o)
        value = jnp.swapaxes(buf[:, o : o + n, :].astype(F32), 0, 1)
        out_s[o : o + n] = value.astype(BF16)
        cp = pltpu.make_async_copy(out_s.at[o : o + rows], img_out.at[o : o + rows], sem.at[16 + k])
        cp.start()
        stores.append(cp)
        if k < len(fetch):
            fetch[k].wait()
            copies[k].start()
    for cp in copies + [q_out] + stores:
        cp.wait()


def finish_outputs(images, keys_i, rows_i, img_out, txt_out, g_x, g_u, g_d, vec):
    share, width = g_x.shape
    sds, v = jax.ShapeDtypeStruct, pltpu.VMEM
    any_spec, vmem_spec = pl.BlockSpec(memory_space=pl.ANY), pl.BlockSpec(memory_space=pltpu.VMEM)
    outs = [
        (sds((keys_i, images, width), BF16), any_spec),
        (sds(txt_out.shape, BF16), any_spec),
        (sds((2, width), F32), vmem_spec),
        (sds((2, width), F32), vmem_spec),
        (sds((3, share, WIDE), F32), any_spec),
        (sds((2, WIDE), F32), vmem_spec),
        (sds((WIDE, share), F32), vmem_spec),
        (sds((2, width), F32), vmem_spec),
        (sds((share, width), F32), any_spec),
        (sds((1, width), F32), vmem_spec),
        (sds((share, width), F32), any_spec),
    ]
    img, txt, gains, shifts, qkv, bias_qv, proj, outb, up, bias_up, down = pl.pallas_call(
        partial(finish_kernel, images, keys_i, rows_i),
        out_shape=[o[0] for o in outs],
        in_specs=[any_spec] * 5 + [vmem_spec],
        out_specs=[o[1] for o in outs],
        scratch_shapes=[
            v((images, rows_i, width), BF16), v((rows_i, images, width), BF16), v((share, width), F32),
            v((3, share, WIDE), F32), v(txt_out.shape, BF16), v((share, width), F32), v((share, width), F32),
            pltpu.SemaphoreType.DMA((24,)),
        ],
        compiler_params=pltpu.CompilerParams(vmem_limit_bytes=60 << 20),
    )(img_out.reshape(images, rows_i, width), txt_out, g_x, g_u, g_d, vec)
    return (
        jnp.transpose(img, (1, 0, 2))[None], txt.reshape(2, -1, width)[None], gains[None], shifts[None],
        jnp.transpose(qkv, (1, 0, 2))[None], bias_qv[None], proj[None], outb[None], up[None], bias_up, down.T[None],
    )


def per_device(
    image_side, text_side, caption_lengths, norm_gains, norm_shifts, w_qkv, bias_qv, w_proj, out_bias, w_up, bias_up, w_down,
):
    dp_size = lax.axis_size("dp")
    core = lax.rem(lax.axis_index("tensor"), 2)
    images, keys_i, width = image_side.shape[1:]
    blocks, length = text_side.shape[1:3]
    per_core = images // 2
    rows_i = -(-(per_core // CHUNKS * keys_i) // 16) * 16
    rows_t = length * (blocks // 2) // CHUNKS
    share = width // dp_size
    z_inside = dp_size == 4 and share % 16 == 0

    img = lax.dynamic_slice_in_dim(image_side[0], core * per_core, per_core, 0)
    img = jnp.pad(img, ((0, 0), (0, rows_i - keys_i), (0, 0))).reshape(per_core * rows_i, width)
    wq = jnp.transpose(w_qkv[0], (1, 2, 0)).reshape(3 * WIDE, width)
    n_i, n_t = rows_i * CHUNKS, rows_t * CHUNKS
    columns = (width, width, width)
    sds = jax.ShapeDtypeStruct
    grad_type = (lambda w: sds((share, w), F32)) if z_inside else (lambda w: sds((width, w), BF16))
    outs = [sds((2 * n_i, width), BF16), sds((2 * n_t, width), BF16)]
    outs += [grad_type(w) for w in columns] + [sds((16, width), F32)]
    any_spec, vmem_spec = pl.BlockSpec(memory_space=pl.ANY), pl.BlockSpec(memory_space=pltpu.VMEM)
    v = pltpu.VMEM
    scratch = [
        v((n_i, width), BF16), v((n_i, width), BF16),
        v((2 * QKV, width), BF16), v((2 * MIX, width), BF16), v((width, 2 * width), BF16), v((2 * width, width), BF16),
        v((2, 8, width + QKV), F32), v((8, n_t + 2 * rows_t), jnp.int32),
        v((n_i, width), BF16), v((max(n_i, n_t + 2 * rows_t), 2 * QKV), BF16), v((n_i, 2 * MIX), BF16), v((n_i, width), F32),
        v((n_i, width), BF16), v((n_i, 2 * width), BF16), v((n_i, 2 * width), BF16),
        v((CHUNKS * HEADS, max(rows_i, rows_t), max(-(-rows_i // 128) * 128, 3 * rows_t)), F32),
        v((n_t + 2 * rows_t, 2 * HEADS * HEAD), F32), v((max(rows_i, rows_t), 2 * MIX), BF16),
        v((n_i, width), BF16), v((n_i, width), BF16), v((n_i, width), BF16), v((n_i, width), BF16),
        v((n_i, width), BF16), v((n_t, width), BF16), v((n_i, width), BF16), v((n_i, width), BF16), v((n_i, width), BF16),
        v((16, 8, width), F32), v((2, 16, width), F32), v((16, width), F32), v((dp_size if z_inside else 1, 16, width), F32),
    ]
    scratch += [v((width, w), BF16) for w in columns] + [v((width, w), BF16) for w in columns]
    if z_inside:
        scratch += [v((3, 2, share, width), BF16), v((3, share, width), BF16), v((3, share, width), F32)]
    dma = pltpu.SemaphoreType.DMA
    scratch += [dma((4 * N_KINDS,)), dma((4 * N_KINDS,)), dma((24,))]
    img_out, txt_out, g_x, g_u, g_d, vec = pl.pallas_call(
        partial(layers_kernel, rows_i, rows_t, keys_i, dp_size, z_inside),
        out_shape=outs,
        in_specs=[any_spec] * 6 + [pl.BlockSpec(memory_space=pltpu.SMEM)] + [vmem_spec] * 5,
        out_specs=[any_spec] * 5 + [vmem_spec],
        scratch_shapes=scratch,
        compiler_params=pltpu.CompilerParams(collective_id=0, has_side_effects=True, vmem_limit_bytes=60 << 20),
    )(
        img, text_side[0], wq, w_proj[0], w_up[0], w_down[0], caption_lengths,
        norm_gains[0], norm_shifts[0], out_bias[0], bias_up, bias_qv[0],
    )
    if z_inside:
        return finish_outputs(images, keys_i, rows_i, img_out, txt_out, g_x, g_u, g_d, vec)
    else:
        def scatter(grad):
            return lax.psum_scatter(grad, "dp", scatter_dimension=0, tiled=True).astype(F32)

        g_x, g_u, g_d = (scatter(g) for g in (g_x, g_u, g_d))
        vec = lax.psum(vec, "dp")
    image_result = img_out.reshape(images, rows_i, width)[:, :keys_i][None]
    text_result = txt_out.reshape(blocks, length, width)[None]
    return (
        image_result,
        text_result,
        vec[0:2][None],
        vec[2:4][None],
        g_x[:, : 3 * WIDE].reshape(share, 3, WIDE)[None],
        jnp.stack([vec[8, 0:WIDE], vec[8, 2 * WIDE : 3 * WIDE]])[None],
        g_x[:, 3 * WIDE :].T[None],
        vec[4:6][None],
        g_u[None],
        vec[6][None],
        g_d.T[None],
    )


def solution(mesh):
    placed = (
        P("pipe", "dp", None, None),
        P("pipe", "dp", None, None),
        P("dp", None),
        P("pipe", None, None),
        P("pipe", None, None),
        P("pipe", None, None, "tensor"),
        P("pipe", None, "tensor"),
        P("pipe", "tensor", None),
        P("pipe", None, None),
        P("pipe", None, "tensor"),
        P("pipe", "tensor"),
        P("pipe", "tensor", None),
    )
    return jax.shard_map(
        per_device,
        mesh=mesh,
        in_specs=placed,
        out_specs=(
            P("pipe", "dp", None, None),
            P("pipe", "dp", None, None),
            P("pipe", None, None),
            P("pipe", None, None),
            P("pipe", "dp", None, "tensor"),
            P("pipe", None, "tensor"),
            P("pipe", "tensor", "dp"),
            P("pipe", None, None),
            P("pipe", "dp", "tensor"),
            P("pipe", "tensor"),
            P("pipe", "tensor", "dp"),
        ),
        check_vma=False,
    )
```

```python
from functools import partial

import jax
import jax.numpy as jnp
from jax import lax
from jax.experimental import pallas as pl
from jax.experimental.pallas import tpu as pltpu
from jax.sharding import PartitionSpec as P

F32 = jnp.float32
BF16 = jnp.bfloat16
BY_MESH = pl.DeviceIdType.MESH
HEAD = 64
HALF = 3
HEADS = 2 * HALF
WIDE = HALF * HEAD
EPSILON = 1e-06
MASKED = -1000000000.0
CHUNKS = 4
STRIP = 16
TURNS = 4
G_TILE = 256
STEP = 64
BLOCK = 208
QKV = 640
MIX = 256
PAD = MIX - WIDE
TILE = 256

K_IN, K_A, K_B, K_C, K_Y1, K_Y2, K_YT, K_OI, K_OT, K_T1, K_W, K_S, K_G, K_Z = range(14)
K_V = K_Z + 3
K_E = K_V + 2
N_KINDS = K_E + 1


def dot(a, b):
    return lax.dot_general(a, b, (((1,), (0,)), ((), ())), preferred_element_type=F32)


def dot_nt(a, b):
    return lax.dot_general(a, b, (((1,), (1,)), ((), ())), preferred_element_type=F32)


def dot_tn(a, b):
    return lax.dot_general(a, b, (((0,), (0,)), ((), ())), preferred_element_type=F32)


def loop(count, body):
    def step(j, carry):
        body(j)
        return carry

    lax.fori_loop(0, count, step, 0)


def unit_of(rows):
    centre = rows - jnp.mean(rows, axis=-1, keepdims=True)
    inverse = lax.rsqrt(jnp.mean(centre * centre, axis=-1, keepdims=True) + EPSILON)
    return centre * inverse, inverse


def norm_back(grad, unit, inverse, gain):
    scaled = grad * gain
    first = jnp.mean(scaled, axis=-1, keepdims=True)
    second = jnp.mean(scaled * unit, axis=-1, keepdims=True)
    return inverse * (scaled - first - unit * second)


def gelu_pair(u):
    cdf = 0.5 * (1.0 + lax.erf(u * (0.5**0.5)))
    pdf = jnp.exp(u * u * -0.5) * 0.3989422804014327
    return u * cdf, cdf + u * pdf


def fold(rows):
    return jnp.sum(rows.reshape(rows.shape[0] // 8, 8, rows.shape[1]), axis=0)


def layers_kernel(
    rows_i, rows_t, keys_i, dp_size, z_inside,
    img_own, txt_all, w_qkv, w_proj, w_up, w_down, lengths, gains, shifts, outb, bias_up, bias_qv,
    img_out, txt_out, g_mix, g_up, g_down, vec_out,
    x_s, dy_s, wq_s, wp_s, wu_s, wd_s, small_s, seg_s, a1_s, qkv_s, o_s, r_s, a2_s, gb_s, du_s, p_s, dkv_s, do_s,
    send_s, ra_s, rb_s, rc_s, ys_s, yt_s, y1_s, y2_s, fin_s, acc_s, early_s, esib_s, eall_s, late_s, lall_s,
    half_s, gs_x, gs_u, gs_d, gr_x, gr_u, gr_d, *rest,
):
    if z_inside:
        z1_s, z2_s, zf_s, ssem, rsem, lsem = rest
    else:
        ssem, rsem, lsem = rest
    width = x_s.shape[1]
    p, d, t = lax.axis_index("pipe"), lax.axis_index("dp"), lax.axis_index("tensor")
    core = lax.rem(t, 2)
    sib_t = t + 1 - 2 * core
    peer_t = lax.rem(t + 2, 4)
    other = 1 - p
    sib, peer = (p, d, sib_t), (p, d, peer_t)
    across = (other, d, t)
    txt_own = txt_all.at[core]
    groups = dp_size if z_inside else 1
    adders = [(k, j) for k in range(groups) for j in range(2) if k + j > 0]

    def adder(k, j, back=False):
        dist = dp_size - k if back else k
        return (p, lax.rem(d + dist, dp_size) if k else d, sib_t if j else t)

    partners = [peer, across] + [adder(k, j) for k, j in adders]

    def remote(src, dst, kind, slot, to):
        at = kind * 4 + slot
        return pltpu.make_async_remote_copy(
            src_ref=src, dst_ref=dst, send_sem=ssem.at[at], recv_sem=rsem.at[at],
            device_id=to, device_id_type=BY_MESH,
        )

    def local(src, dst, slot):
        return pltpu.make_async_copy(src, dst, lsem.at[slot])

    image_here = p == 0
    n_img = rows_i * CHUNKS
    n_txt = rows_t * CHUNKS

    wq_own = local(w_qkv, wq_s.at[0 : 3 * WIDE], 0)
    wp_own = local(w_proj, wp_s.at[PAD:MIX], 1)
    wu_own = local(w_up, wu_s.at[:, 0:width], 2)
    wd_own = local(w_down, wd_s.at[0:width], 3)
    img_in = local(img_own, x_s, 5)
    txt_in = local(txt_own, dy_s.at[0:n_txt], 6)
    wq_own.start()

    @pl.when(image_here)
    def _():
        img_in.start()

    @pl.when(jnp.logical_not(image_here))
    def _():
        txt_in.start()

    wp_own.start()
    wu_own.start()
    wd_own.start()
    zero_rows = jnp.zeros((PAD, width), BF16)
    wp_s[0:PAD, :] = zero_rows
    wp_s[MIX : MIX + PAD, :] = zero_rows
    zero_rows = jnp.zeros((QKV - 3 * WIDE, width), BF16)
    wq_s[3 * WIDE : QKV, :] = zero_rows
    wq_s[QKV + 3 * WIDE :, :] = zero_rows
    acc_s[...] = jnp.zeros_like(acc_s)
    small_s[0] = jnp.zeros_like(small_s[0])
    small_s[0, 0:1, 0:width] = bias_up[...]
    small_s[0, 0:1, width : width + WIDE] = bias_qv[0:1, :]
    small_s[0, 0:1, width + 2 * WIDE : width + 3 * WIDE] = bias_qv[1:2, :]

    barrier = pltpu.get_barrier_semaphore()
    for to in partners:
        pl.semaphore_signal(barrier, inc=1, device_id=to, device_id_type=BY_MESH)

    @pl.when(image_here)
    def _():
        img_in.wait()

        def first_norm(i):
            at = pl.ds(pl.multiple_of(i * rows_i, 16), rows_i)
            unit, _ = unit_of(x_s[at, :].astype(F32))
            a1_s[at, :] = (unit * gains[0:1, :] + shifts[0:1, :]).astype(BF16)

        loop(CHUNKS, first_norm)

    pl.semaphore_wait(barrier, len(partners))

    sm_sib = remote(small_s.at[0], small_s.at[1], K_S, 0, sib)
    wq_sib = remote(w_qkv, wq_s.at[QKV : QKV + 3 * WIDE], K_W, 0, sib)
    wp_sib = remote(w_proj, wp_s.at[MIX + PAD :], K_W, 1, sib)
    wu_sib = remote(w_up, wu_s.at[:, width:], K_W, 2, sib)
    wd_sib = remote(w_down, wd_s.at[width:], K_W, 3, sib)

    def x_to_text(i):
        rows = pl.ds(pl.multiple_of(i * rows_t, 16), rows_t)
        return remote(txt_own.at[rows], x_s.at[rows], K_IN, i, across)

    def dy_to_image(i):
        rows = pl.ds(pl.multiple_of(i * rows_i, 16), rows_i)
        return remote(img_own.at[rows], dy_s.at[rows], K_IN, i, across)

    @pl.when(image_here)
    def _():
        loop(CHUNKS, lambda i: x_to_text(i).start())

    sm_sib.start()
    wq_sib.start()

    @pl.when(jnp.logical_not(image_here))
    def _():
        loop(CHUNKS, lambda i: dy_to_image(i).start())

    wp_sib.start()
    wu_sib.start()
    wd_sib.start()

    own_gain = [gains[0:1, :], gains[1:2, :]]
    own_shift = [shifts[0:1, :], shifts[1:2, :]]

    g_arrays = [(gs_x, gr_x, g_mix), (gs_u, gr_u, g_up), (gs_d, gr_d, g_down)]

    def g_exchange(a):
        return remote(half_s.at[a % 2], g_arrays[a][1], K_G, a, sib)

    def grads_part(a, product, first):
        mine, theirs = g_arrays[a][0], half_s.at[a % 2]

        def both(m):
            at = pl.ds(pl.multiple_of(m * G_TILE, G_TILE), G_TILE)
            for ref, value in zip((mine, theirs), product(at)):
                ref[at, :] = (value if first else value + ref[at, :].astype(F32)).astype(BF16)

        loop(width // G_TILE, both)
        if not first:
            g_exchange(a).start()

    def grads_sum(a):
        g_exchange(a).wait()
        mine, theirs = g_arrays[a][0:2]

        def body(m):
            at = pl.ds(pl.multiple_of(m * G_TILE, G_TILE), G_TILE)
            mine[at, :] = (mine[at, :].astype(F32) + theirs[at, :].astype(F32)).astype(BF16)

        loop(width // G_TILE, body)

    share = width // dp_size
    parity = lax.rem(d, 2)
    upper = d // 2
    near = d + 1 - 2 * parity
    far = d + 2 - 4 * upper if z_inside else d

    def share_rows(at):
        return pl.ds(pl.multiple_of(at * share, 16), share)

    def z_near(a, k):
        src = g_arrays[a][0].at[share_rows(1 - parity + 2 * k)]
        return remote(src, z1_s.at[a, k], K_Z, 3 * k + a, (p, near, t))

    def z_far(a):
        return remote(g_arrays[a][0].at[share_rows(far)], z2_s.at[a], K_Z, 6 + a, (p, far, t))

    def z_start(a):
        if z_inside:
            z_near(a, 1 - upper).start()
        else:
            local(g_arrays[a][0], g_arrays[a][2], 20 + a).start()

    def z_middle(a):
        if z_inside:
            z_near(a, 1 - upper).wait()
            mine = g_arrays[a][0]
            rows = share_rows(far)
            mine[rows, :] = (mine[rows, :].astype(F32) + z1_s[a, 1 - upper].astype(F32)).astype(BF16)
            z_far(a).start()

    def z_finish(a):
        if z_inside:
            z_near(a, upper).wait()
            z_far(a).wait()
            total = g_arrays[a][0][share_rows(d), :].astype(F32) + z1_s[a, upper].astype(F32)
            zf_s[a] = total + z2_s[a].astype(F32)
            local(zf_s.at[a], g_arrays[a][2], 20 + a).start()

    def z_end(a):
        if z_inside:
            local(zf_s.at[a], g_arrays[a][2], 20 + a).wait()
        else:
            local(g_arrays[a][0], g_arrays[a][2], 20 + a).wait()

    def one_layer(text):
        rows = rows_t if text else rows_i
        total = rows * CHUNKS
        cuts = [(o, min(BLOCK, rows - o)) for o in range(0, rows, BLOCK)]
        q_off = rows_t if text else 0

        def at_rows(i):
            return pl.ds(pl.multiple_of(i * rows, 16), rows)

        def q_rows(i):
            return pl.ds(pl.multiple_of(i * rows + q_off, 16), rows)

        def by_strips(i, body):
            for o, size in cuts:
                body(pl.ds(pl.multiple_of(i * rows + o, STRIP), size))

        def swap(i, landing, kind):
            return remote(send_s.at[at_rows(i)], landing.at[at_rows(i)], kind, i, peer)

        incoming = dy_to_image if not text else x_to_text

        def wait_input(i):
            cp = remote(x_s.at[at_rows(i)] if text else dy_s.at[at_rows(i)],
                        x_s.at[at_rows(i)] if text else dy_s.at[at_rows(i)], K_IN, i, across)
            cp.wait_recv()

        wq_own.wait()
        wq_sib.wait()
        sm_sib.wait()
        def caption(places):
            bound = lengths[core, 0]
            segment = (places >= bound).astype(jnp.int32)
            for k in range(1, lengths.shape[1]):
                bound = bound + lengths[core, k]
                segment = segment + (places >= bound).astype(jnp.int32)
            return segment

        if text:
            places = lax.broadcasted_iota(jnp.int32, (8, total + 2 * rows_t), 1) - rows_t
            seg_s[...] = jnp.where(places < 0, -1, caption(places))
            txt_in.wait()
            pad = jnp.zeros((rows_t, 2 * QKV), BF16)
            qkv_s[0:rows_t, :] = pad
            qkv_s[rows_t + total : 2 * rows_t + total, :] = pad
            dkv_s[...] = jnp.zeros_like(dkv_s)
        for s in range(2):
            o_s[0:total, s * MIX : s * MIX + PAD] = jnp.zeros((total, PAD), BF16)

        def project(i):
            if text:
                wait_input(i)

            def first_norm(at):
                unit, _ = unit_of(x_s[at, :].astype(F32))
                a1_s[at, :] = (unit * own_gain[0] + own_shift[0]).astype(BF16)

            if text:
                by_strips(i, first_norm)
            left = a1_s[at_rows(i), :]
            lanes = lax.broadcasted_iota(jnp.int32, (1, QKV), 1)
            factor = jnp.where(lanes < WIDE, HEAD**-0.5, 1.0).astype(F32)
            for s in range(2):
                value = dot_nt(left, wq_s[s * QKV : (s + 1) * QKV, :])
                value = (value + small_s[s, 0:1, width : width + QKV]) * factor
                qkv_s[q_rows(i), s * QKV : (s + 1) * QKV] = value.astype(BF16)

        def head_at(h):
            s, hh = h // HALF, h % HALF
            base = s * QKV + hh * HEAD
            return slice(base, base + HEAD), slice(base + WIDE, base + WIDE + HEAD), slice(base + 2 * WIDE, base + 2 * WIDE + HEAD), slice(s * MIX + PAD + hh * HEAD, s * MIX + PAD + hh * HEAD + HEAD)

        span = 3 * rows_t if text else rows_i
        pieces = [(o, min(128, span - o)) for o in range(0, span, 128)]

        def keep_weights(at, value):
            for k, (o, n) in enumerate(pieces):
                p_s[at, k * rows : (k + 1) * rows, 0:n] = value[:, o : o + n]

        def kept_weights(at):
            parts = [p_s[at, k * rows : (k + 1) * rows, 0:n] for k, (o, n) in enumerate(pieces)]
            return jnp.concatenate(parts, axis=1)

        def key_rows(i):
            return pl.ds(pl.multiple_of(i * rows, 16), span)

        def allowed(i):
            if text:
                mine = caption(lax.broadcasted_iota(jnp.int32, (rows, 1), 0) + i * rows)
                keys = seg_s[0:1, pl.ds(pl.multiple_of(i * rows_t, 128), span)]
                return mine == keys
            return lax.broadcasted_iota(jnp.int32, (1, span), 1) < keys_i

        def attend(i):
            ok = allowed(i)
            for h in range(HEADS):
                qc, kc, vc, oc = head_at(h)
                scores = dot_nt(qkv_s[q_rows(i), qc], qkv_s[key_rows(i), kc])
                scores = jnp.where(ok, scores, MASKED)
                raised = jnp.exp(scores - jnp.max(scores, axis=-1, keepdims=True))
                weights = raised * (1.0 / jnp.sum(raised, axis=-1, keepdims=True))
                keep_weights(i * HEADS + h, weights)
                mixed = dot(weights.astype(BF16), qkv_s[key_rows(i), vc])
                o_s[at_rows(i), oc] = mixed.astype(BF16)

        def send_a(i):
            send_s[at_rows(i), :] = dot(o_s[at_rows(i), :], wp_s[...]).astype(BF16)
            swap(i, ra_s, K_A).start()

        if text:

            def forward(i):
                @pl.when(i < CHUNKS)
                def _():
                    project(i)

                @pl.when(i == 1)
                def _():
                    wp_own.wait()
                    wp_sib.wait()

                @pl.when(i > 0)
                def _():
                    attend(i - 1)
                    send_a(i - 1)

            loop(CHUNKS + 1, forward)
        else:

            def forward(i):
                project(i)
                attend(i)

                @pl.when(i == 0)
                def _():
                    wp_own.wait()
                    wp_sib.wait()

                send_a(i)

            loop(CHUNKS, forward)
        wu_own.wait()
        wu_sib.wait()
        wd_own.wait()
        wd_sib.wait()

        def y_copies(i):
            at = at_rows(i)
            if text:
                return [remote(ys_s.at[at], yt_s.at[at], K_YT, i, peer)]
            return [remote(ys_s.at[at], y1_s.at[at], K_Y1, i, across)]

        def owned(i):
            return lax.rem(i, 2) == t // 2

        def y_side(i):
            at = pl.ds(pl.multiple_of(i * rows_i, 16), rows_i)
            there = y1_s if text and i < TURNS else y2_s
            return remote((y1_s if text else ys_s).at[at], there.at[at], K_Y2, i, peer)

        def y_share(i):
            @pl.when(jnp.logical_not(owned(i)))
            def _():
                y_side(i).start()

        def y_sum(i):
            @pl.when(owned(i))
            def _():
                y_side(i).wait_recv()
                at = at_rows(i)
                ys_s[at, :] = (ys_s[at, :].astype(F32) + y2_s[at, :].astype(F32)).astype(BF16)
                y_copies(i)[0].start()

        def hand_on(i):
            def go():
                at = pl.ds(pl.multiple_of(i * rows_i, 16), rows_i)
                remote(y1_s.at[at], y1_s.at[at], K_Y1, i, across).wait_recv()
                y_side(i).start()

            if i < TURNS:
                pl.when(owned(i))(go)
            else:
                go()

        def middle(i):
            if not text:
                wait_input(i)
            swap(i, ra_s, K_A).wait()

            def second_norm(at):
                r = x_s[at, :].astype(F32) + (send_s[at, :].astype(F32) + ra_s[at, :].astype(F32)) + outb[0:1, :]
                r_s[at, :] = r
                unit, _ = unit_of(r)
                a2_s[at, :] = (unit * own_gain[1] + own_shift[1]).astype(BF16)
                acc_s[5] += fold(dy_s[at, :].astype(F32))

            by_strips(i, second_norm)
            left = a2_s[at_rows(i), :]
            grad = dy_s[at_rows(i), :]
            for n in range(2 * width // TILE):
                cols = slice(n * TILE, (n + 1) * TILE)
                s, inner = (n * TILE) // width, (n * TILE) % width
                u = dot(left, wu_s[:, cols]) + small_s[s, 0:1, inner : inner + TILE]
                g, slope = gelu_pair(u)
                gb_s[at_rows(i), cols] = g.astype(BF16)
                du = (dot_nt(grad, wd_s[cols, :]) * slope).astype(BF16)
                du_s[at_rows(i), cols] = du
                acc_s[6 + s, :, inner : inner + TILE] += fold(du.astype(F32))
            send_s[at_rows(i), :] = dot_nt(du_s[at_rows(i), :], wu_s[...]).astype(BF16)
            swap(i, rb_s, K_B).start()
            lower = dot(gb_s[at_rows(i), :], wd_s[...])
            ys_s[at_rows(i), :] = (lower + 0.5 * (r_s[at_rows(i), :] + outb[1:2, :])).astype(BF16)
            if not text:

                @pl.when(i >= TURNS)
                def _():
                    y_copies(i)[0].start()
        parts = (slice(0, total // 2), slice(total // 2, total))

        def halves(left, right, part):
            def product(at):
                value = dot_tn(left[part, at], right[part, :])
                return value[:, :width], value[:, width:]

            return product

        def middle_and_grads(i):
            middle(i)

            @pl.when(i == 1)
            def _():
                grads_part(2, halves(dy_s, gb_s, parts[0]), True)

            @pl.when(i == 2)
            def _():
                grads_part(1, halves(a2_s, du_s, parts[0]), True)

        loop(CHUNKS, middle_and_grads)
        grads_part(2, halves(dy_s, gb_s, parts[1]), False)
        grads_part(1, halves(a2_s, du_s, parts[1]), False)
        grads_sum(2)
        z_start(2)
        grads_sum(1)
        z_start(1)
        if z_inside:
            z_near(2, upper).start()
            z_near(1, upper).start()

        dq_s, drb_s = gb_s, a2_s
        for s in range(2):
            dq_s[0:total, s * QKV + 3 * WIDE : (s + 1) * QKV] = jnp.zeros((total, QKV - 3 * WIDE), BF16)

        def attend_back(i):
            swap(i, rb_s, K_B).wait()

            def back_norm(at):
                grad = send_s[at, :].astype(F32) + rb_s[at, :].astype(F32)
                unit, inverse = unit_of(r_s[at, :])
                dr = dy_s[at, :].astype(F32) + norm_back(grad, unit, inverse, own_gain[1])
                r_s[at, :] = dr
                drb_s[at, :] = dr.astype(BF16)
                acc_s[1] += fold(grad * unit)
                acc_s[3] += fold(grad)
                acc_s[4] += fold(dr)

            by_strips(i, back_norm)
            do_s[0:rows, :] = dot_nt(drb_s[at_rows(i), :], wp_s[...]).astype(BF16)
            for h in range(HEADS):
                qc, kc, vc, oc = head_at(h)
                weights = kept_weights(i * HEADS + h)
                grad_o = do_s[0:rows, oc]
                keys = qkv_s[key_rows(i), kc]
                slope = dot_nt(grad_o, qkv_s[key_rows(i), vc])
                ds = (weights * (slope - jnp.sum(slope * weights, axis=-1, keepdims=True))).astype(BF16)
                dq = dot(ds, keys).astype(BF16) * (HEAD**-0.5)
                dk = dot_tn(ds, qkv_s[q_rows(i), qc])
                dv = dot_tn(weights.astype(BF16), grad_o)
                dq_s[at_rows(i), qc] = dq.astype(BF16)
                if text:
                    hc = slice(h * HEAD, (h + 1) * HEAD)
                    hv = slice((HEADS + h) * HEAD, (HEADS + h + 1) * HEAD)
                    dkv_s[key_rows(i), hc] += dk
                    dkv_s[key_rows(i), hv] += dv
                else:
                    dq_s[at_rows(i), kc] = dk.astype(BF16)
                    dq_s[at_rows(i), vc] = dv.astype(BF16)

        def send_c(i):
            if text:
                for s in range(2):
                    k0 = s * QKV + WIDE
                    dq_s[at_rows(i), k0 : k0 + WIDE] = dkv_s[q_rows(i), s * WIDE : (s + 1) * WIDE].astype(BF16)
                    v0 = 2 * WIDE + s * WIDE
                    dq_s[at_rows(i), k0 + WIDE : k0 + 2 * WIDE] = dkv_s[q_rows(i), v0 : v0 + WIDE].astype(BF16)
            grad = dq_s[at_rows(i), 0 : 2 * QKV]
            send_s[at_rows(i), :] = dot(grad, wq_s[...]).astype(BF16)
            swap(i, rc_s, K_C).start()
            for s in range(2):
                acc_s[8 + s, :, 0:QKV] += fold(grad[:, s * QKV : (s + 1) * QKV].astype(F32))

        def own_img(i):
            return img_out.at[pl.ds(pl.multiple_of(core * n_img + i * rows_i, 16), rows_i)]

        def own_txt(i):
            return txt_out.at[pl.ds(pl.multiple_of(core * n_txt + i * rows_t, 16), rows_t)]

        def img_copies(i):
            src = (y1_s if text else fin_s).at[pl.ds(pl.multiple_of(i * rows_i, 16), rows_i)]
            return local(src, own_img(i), 8 + i), remote(src, own_img(i), K_OI, i, sib)

        def txt_copies(i):
            src = ys_s.at[pl.ds(pl.multiple_of(i * rows_t, 16), rows_t)]
            return local(src, own_txt(i), 12 + i), remote(src, own_txt(i), K_OT, i, sib)

        def dx_copies(i):
            src = rb_s.at[pl.ds(pl.multiple_of(i * rows_t, 16), rows_t)]
            return remote(src, own_txt(i), K_T1, i, across)

        def dx_relay(i):
            return remote(own_txt(i), own_txt(i), K_OT, i, sib)

        if text:

            def own_y(i):
                y_copies(i)[0].wait()
                at = at_rows(i)
                ys_s[at, :] = (ys_s[at, :].astype(F32) + yt_s[at, :].astype(F32)).astype(BF16)
                for cp in txt_copies(i):
                    cp.start()

            def image_y(i):
                at = pl.ds(pl.multiple_of(i * rows_i, 16), rows_i)
                if i < TURNS:

                    @pl.when(owned(i))
                    def _():
                        y_side(i).wait_send()

                    @pl.when(jnp.logical_not(owned(i)))
                    def _():
                        y_side(i).wait_recv()

                else:
                    y_side(i).wait()
                    y1_s[at, :] = (y1_s[at, :].astype(F32) + y2_s[at, :].astype(F32)).astype(BF16)
                for cp in img_copies(i):
                    cp.start()

        def last(i):
            swap(i, rc_s, K_C).wait()

            def body(at):
                grad = send_s[at, :].astype(F32) + rc_s[at, :].astype(F32)
                unit, inverse = unit_of(x_s[at, :].astype(F32))
                dx = (r_s[at, :] + norm_back(grad, unit, inverse, own_gain[0])).astype(BF16)
                if text:
                    rb_s[at, :] = dx
                else:
                    fin_s[at, :] = dx
                acc_s[0] += fold(grad * unit)
                acc_s[2] += fold(grad)

            by_strips(i, body)

            for cp in [dx_copies(i)] if text else img_copies(i):
                cp.start()

        if not text:
            for i in range(TURNS):
                y_share(i)
        def mixed_grads(part):
            def product(at):
                first = dot_tn(a1_s[part, at], dq_s[part, 0 : 2 * QKV])
                second = dot_tn(drb_s[part, at], o_s[part, :])

                def joined(s):
                    left, right = first[:, s * QKV : (s + 1) * QKV], second[:, s * MIX : (s + 1) * MIX]
                    seam = left[:, MIX * 2 :] + right[:, 0 : QKV - 2 * MIX]
                    return jnp.concatenate([left[:, : MIX * 2], seam, right[:, QKV - 2 * MIX :]], axis=1)

                return joined(0), joined(1)

            return product

        group = d if z_inside else 0

        def early_copy(k):
            return remote(early_s.at[0], eall_s.at[group], K_E, k - 1, adder(k, 0))

        def early_arrival(k):
            place = lax.rem(d + dp_size - k, dp_size)
            return remote(eall_s.at[place], eall_s.at[place], K_E, k - 1, adder(k, 0, True))

        early_sib = remote(early_s.at[1], esib_s, K_S, 1, sib)

        def early_start():
            sums = jnp.sum(acc_s[...], axis=1)
            for j, order in enumerate(((1, 3, 4, 5, 6, 7, 8, 9), (1, 3, 4, 5, 7, 6, 9, 8))):
                for row, src in enumerate(order):
                    early_s[j, row : row + 1, :] = sums[src : src + 1, :]
            early_sib.start()

        def early_next():
            early_sib.wait()
            early_s[0] = early_s[0] + esib_s[...]
            eall_s[group] = early_s[0]
            for k in range(1, groups):
                early_copy(k).start()

        def late_copy(k, j):
            return remote(late_s, lall_s.at[2 * group + core], K_V, 2 * k + j, adder(k, j))

        def late_arrival(k, j):
            place = 2 * (lax.rem(d + dp_size - k, dp_size) if k else group) + (1 - core if j else core)
            return remote(lall_s.at[place], lall_s.at[place], K_V, 2 * k + j, adder(k, j, True))

        def late_start():
            late_s[...] = jnp.zeros_like(late_s)
            for r, src in enumerate((0, 2)):
                row = jnp.sum(acc_s[src], axis=0, keepdims=True)
                for c in range(width // 128):
                    late_s[8 * r + c : 8 * r + c + 1, :] = row[:, c * 128 : (c + 1) * 128]
            for k, j in adders:
                late_copy(k, j).start()
            lall_s[2 * group + core] = late_s[...]

        def vectors_finish():
            for k in range(1, groups):
                early_copy(k).wait_send()
                early_arrival(k).wait_recv()
            for k, j in adders:
                late_copy(k, j).wait_send()
                late_arrival(k, j).wait_recv()
            early, late = eall_s[0], lall_s[0]
            for k in range(1, groups):
                early = early + eall_s[k]
            for k in range(1, 2 * groups):
                late = late + lall_s[k]
            vec_out[...] = jnp.zeros_like(vec_out)
            for row, dst in enumerate((1, 3, 4, 5, 6, 7, 8, 9)):
                vec_out[dst : dst + 1, :] = early[row : row + 1, :]
            for r, dst in enumerate((0, 2)):
                for c in range(width // 128):
                    vec_out[dst : dst + 1, c * 128 : (c + 1) * 128] = late[8 * r + c : 8 * r + c + 1, :]

        if text:

            def backward(i):
                @pl.when(i < CHUNKS)
                def _():
                    attend_back(i)

                @pl.when(i == 2)
                def _():
                    z_middle(2)

                @pl.when(i == 3)
                def _():
                    z_middle(1)

                @pl.when(i > 0)
                def _():
                    send_c(i - 1)

                @pl.when(i == 3)
                def _():
                    grads_part(0, mixed_grads(parts[0]), True)

                @pl.when(i > 2)
                def _():
                    last(i - 3)

            loop(CHUNKS + 1, backward)
        else:

            def backward(i):
                @pl.when(i == 2)
                def _():
                    z_middle(2)

                @pl.when(i == 3)
                def _():
                    z_middle(1)

                attend_back(i)
                send_c(i)

                @pl.when(i == 2)
                def _():
                    grads_part(0, mixed_grads(parts[0]), True)

            loop(CHUNKS, backward)


        if text:
            for i in range(TURNS, CHUNKS):
                hand_on(i)
            loop(CHUNKS, lambda i: y_copies(i)[0].start())
        grads_part(0, mixed_grads(parts[1]), False)
        grads_sum(0)
        z_start(0)
        if z_inside:
            z_near(0, upper).start()
        early_start()
        if text:
            last(CHUNKS - 2)
            last(CHUNKS - 1)
            early_next()
            z_middle(0)
            for i in range(TURNS):
                hand_on(i)
            loop(CHUNKS, own_y)
        else:
            for i in range(TURNS):
                y_sum(i)
            loop(2, last)
            early_next()
            z_middle(0)
            last(CHUNKS - 2)
            last(CHUNKS - 1)

        late_start()
        z_finish(2)
        z_finish(1)
        if text:
            for i in range(CHUNKS):
                image_y(i)
        z_finish(0)
        vectors_finish()

        def finish(i):
            if text:
                dy_to_image(i).wait_send()
                dx_copies(i).wait_send()
                here, there = txt_copies(i)
                here.wait()
                there.wait()
            else:
                x_to_text(i).wait_send()
                if i < TURNS:

                    @pl.when(owned(i))
                    def _():
                        y_copies(i)[0].wait_send()

                    @pl.when(jnp.logical_not(owned(i)))
                    def _():
                        y_side(i).wait_send()

                else:
                    y_copies(i)[0].wait_send()
                dx_copies(i).wait_recv()
                dx_relay(i).start()
            here, there = img_copies(i)
            here.wait()
            there.wait()

        for i in range(CHUNKS):
            finish(i)
        if not text:
            loop(CHUNKS, lambda i: dx_relay(i).wait())
        for a in range(3):
            z_end(a)

    @pl.when(image_here)
    def _():
        one_layer(False)

    @pl.when(jnp.logical_not(image_here))
    def _():
        one_layer(True)


def finish_kernel(
    images, keys_i, rows_i, img_in, txt_in, g_x, g_u, g_d, vec,
    img_out, txt_out, gains, shifts, qkv, bias_qv, proj, outb, up, bias_up, down,
    buf, out_s, gx_s, qkv_s, txt_s, gu_s, gd_s, sem,
):
    plain = [(g_u, gu_s, up), (g_d, gd_s, down), (txt_in, txt_s, txt_out)]
    fetch = [pltpu.make_async_copy(src, mid, sem.at[k]) for k, (src, mid, dst) in enumerate(plain)]
    copies = [pltpu.make_async_copy(mid, dst, sem.at[5 + k]) for k, (src, mid, dst) in enumerate(plain)]
    gx_in = pltpu.make_async_copy(g_x, gx_s, sem.at[3])
    gx_in.start()
    blocks = [(o, min(STEP, rows_i - o)) for o in range(0, rows_i, STEP)]
    loads = [
        pltpu.make_async_copy(img_in.at[:, o : o + n], buf.at[:, o : o + n], sem.at[8 + k])
        for k, (o, n) in enumerate(blocks)
    ]
    for cp in loads:
        cp.start()
    for cp in fetch:
        cp.start()
    gains[...] = vec[0:2, :]
    shifts[...] = vec[2:4, :]
    outb[...] = vec[4:6, :]
    bias_up[...] = vec[6:7, :]
    bias_qv[0:1, :] = vec[8:9, 0:WIDE]
    bias_qv[1:2, :] = vec[8:9, 2 * WIDE : 3 * WIDE]
    gx_in.wait()
    proj[...] = gx_s[:, 3 * WIDE :].T
    for k in range(3):
        qkv_s[k] = gx_s[:, k * WIDE : (k + 1) * WIDE]
    q_out = pltpu.make_async_copy(qkv_s, qkv, sem.at[4])
    q_out.start()
    stores = []
    for k, (o, n) in enumerate(blocks):
        loads[k].wait()
        rows = min(n, keys_i - o)
        value = jnp.swapaxes(buf[:, o : o + n, :].astype(F32), 0, 1)
        out_s[o : o + n] = value.astype(BF16)
        cp = pltpu.make_async_copy(out_s.at[o : o + rows], img_out.at[o : o + rows], sem.at[16 + k])
        cp.start()
        stores.append(cp)
        if k < len(fetch):
            fetch[k].wait()
            copies[k].start()
    for cp in copies + [q_out] + stores:
        cp.wait()


def finish_outputs(images, keys_i, rows_i, img_out, txt_out, g_x, g_u, g_d, vec):
    share, width = g_x.shape
    sds, v = jax.ShapeDtypeStruct, pltpu.VMEM
    any_spec, vmem_spec = pl.BlockSpec(memory_space=pl.ANY), pl.BlockSpec(memory_space=pltpu.VMEM)
    outs = [
        (sds((keys_i, images, width), BF16), any_spec),
        (sds(txt_out.shape, BF16), any_spec),
        (sds((2, width), F32), vmem_spec),
        (sds((2, width), F32), vmem_spec),
        (sds((3, share, WIDE), F32), any_spec),
        (sds((2, WIDE), F32), vmem_spec),
        (sds((WIDE, share), F32), vmem_spec),
        (sds((2, width), F32), vmem_spec),
        (sds((share, width), F32), any_spec),
        (sds((1, width), F32), vmem_spec),
        (sds((share, width), F32), any_spec),
    ]
    img, txt, gains, shifts, qkv, bias_qv, proj, outb, up, bias_up, down = pl.pallas_call(
        partial(finish_kernel, images, keys_i, rows_i),
        out_shape=[o[0] for o in outs],
        in_specs=[any_spec] * 5 + [vmem_spec],
        out_specs=[o[1] for o in outs],
        scratch_shapes=[
            v((images, rows_i, width), BF16), v((rows_i, images, width), BF16), v((share, width), F32),
            v((3, share, WIDE), F32), v(txt_out.shape, BF16), v((share, width), F32), v((share, width), F32),
            pltpu.SemaphoreType.DMA((24,)),
        ],
        compiler_params=pltpu.CompilerParams(vmem_limit_bytes=60 << 20),
    )(img_out.reshape(images, rows_i, width), txt_out, g_x, g_u, g_d, vec)
    return (
        jnp.transpose(img, (1, 0, 2))[None], txt.reshape(2, -1, width)[None], gains[None], shifts[None],
        jnp.transpose(qkv, (1, 0, 2))[None], bias_qv[None], proj[None], outb[None], up[None], bias_up, down.T[None],
    )


def per_device(
    image_side, text_side, caption_lengths, norm_gains, norm_shifts, w_qkv, bias_qv, w_proj, out_bias, w_up, bias_up, w_down,
):
    dp_size = lax.axis_size("dp")
    core = lax.rem(lax.axis_index("tensor"), 2)
    images, keys_i, width = image_side.shape[1:]
    blocks, length = text_side.shape[1:3]
    per_core = images // 2
    rows_i = -(-(per_core // CHUNKS * keys_i) // 16) * 16
    rows_t = length * (blocks // 2) // CHUNKS
    share = width // dp_size
    z_inside = dp_size == 4 and share % 16 == 0

    img = lax.dynamic_slice_in_dim(image_side[0], core * per_core, per_core, 0)
    img = jnp.pad(img, ((0, 0), (0, rows_i - keys_i), (0, 0))).reshape(per_core * rows_i, width)
    wq = jnp.transpose(w_qkv[0], (1, 2, 0)).reshape(3 * WIDE, width)
    n_i, n_t = rows_i * CHUNKS, rows_t * CHUNKS
    columns = (width, width, width)
    sds = jax.ShapeDtypeStruct
    grad_type = (lambda w: sds((share, w), F32)) if z_inside else (lambda w: sds((width, w), BF16))
    outs = [sds((2 * n_i, width), BF16), sds((2 * n_t, width), BF16)]
    outs += [grad_type(w) for w in columns] + [sds((16, width), F32)]
    any_spec, vmem_spec = pl.BlockSpec(memory_space=pl.ANY), pl.BlockSpec(memory_space=pltpu.VMEM)
    v = pltpu.VMEM
    scratch = [
        v((n_i, width), BF16), v((n_i, width), BF16),
        v((2 * QKV, width), BF16), v((2 * MIX, width), BF16), v((width, 2 * width), BF16), v((2 * width, width), BF16),
        v((2, 8, width + QKV), F32), v((8, n_t + 2 * rows_t), jnp.int32),
        v((n_i, width), BF16), v((max(n_i, n_t + 2 * rows_t), 2 * QKV), BF16), v((n_i, 2 * MIX), BF16), v((n_i, width), F32),
        v((n_i, width), BF16), v((n_i, 2 * width), BF16), v((n_i, 2 * width), BF16),
        v((CHUNKS * HEADS, max(-(-rows_i // 128) * rows_i, 3 * rows_t // 128 * rows_t), 128), F32),
        v((n_t + 2 * rows_t, 2 * HEADS * HEAD), F32), v((max(rows_i, rows_t), 2 * MIX), BF16),
        v((n_i, width), BF16), v((n_i, width), BF16), v((n_i, width), BF16), v((n_i, width), BF16),
        v((n_i, width), BF16), v((n_t, width), BF16), v((n_i, width), BF16), v((n_i, width), BF16), v((n_i, width), BF16),
        v((16, 8, width), F32), v((2, 8, width), F32), v((8, width), F32), v((dp_size if z_inside else 1, 8, width), F32),
        v((16, 128), F32), v((2 * dp_size if z_inside else 2, 16, 128), F32),
    ]
    scratch += [v((2, width, width), BF16)]
    scratch += [v((width, w), BF16) for w in columns] + [v((width, w), BF16) for w in columns]
    if z_inside:
        scratch += [v((3, 2, share, width), BF16), v((3, share, width), BF16), v((3, share, width), F32)]
    dma = pltpu.SemaphoreType.DMA
    scratch += [dma((4 * N_KINDS,)), dma((4 * N_KINDS,)), dma((24,))]
    img_out, txt_out, g_x, g_u, g_d, vec = pl.pallas_call(
        partial(layers_kernel, rows_i, rows_t, keys_i, dp_size, z_inside),
        out_shape=outs,
        in_specs=[any_spec] * 6 + [pl.BlockSpec(memory_space=pltpu.SMEM)] + [vmem_spec] * 5,
        out_specs=[any_spec] * 5 + [vmem_spec],
        scratch_shapes=scratch,
        compiler_params=pltpu.CompilerParams(collective_id=0, has_side_effects=True, vmem_limit_bytes=60 << 20),
    )(
        img, text_side[0], wq, w_proj[0], w_up[0], w_down[0], caption_lengths,
        norm_gains[0], norm_shifts[0], out_bias[0], bias_up, bias_qv[0],
    )
    if z_inside:
        return finish_outputs(images, keys_i, rows_i, img_out, txt_out, g_x, g_u, g_d, vec)
    else:
        def scatter(grad):
            return lax.psum_scatter(grad, "dp", scatter_dimension=0, tiled=True).astype(F32)

        g_x, g_u, g_d = (scatter(g) for g in (g_x, g_u, g_d))
        vec = lax.psum(vec, "dp")
    image_result = img_out.reshape(images, rows_i, width)[:, :keys_i][None]
    text_result = txt_out.reshape(blocks, length, width)[None]
    return (
        image_result,
        text_result,
        vec[0:2][None],
        vec[2:4][None],
        g_x[:, : 3 * WIDE].reshape(share, 3, WIDE)[None],
        jnp.stack([vec[8, 0:WIDE], vec[8, 2 * WIDE : 3 * WIDE]])[None],
        g_x[:, 3 * WIDE :].T[None],
        vec[4:6][None],
        g_u[None],
        vec[6][None],
        g_d.T[None],
    )


def solution(mesh):
    placed = (
        P("pipe", "dp", None, None),
        P("pipe", "dp", None, None),
        P("dp", None),
        P("pipe", None, None),
        P("pipe", None, None),
        P("pipe", None, None, "tensor"),
        P("pipe", None, "tensor"),
        P("pipe", "tensor", None),
        P("pipe", None, None),
        P("pipe", None, "tensor"),
        P("pipe", "tensor"),
        P("pipe", "tensor", None),
    )
    return jax.shard_map(
        per_device,
        mesh=mesh,
        in_specs=placed,
        out_specs=(
            P("pipe", "dp", None, None),
            P("pipe", "dp", None, None),
            P("pipe", None, None),
            P("pipe", None, None),
            P("pipe", "dp", None, "tensor"),
            P("pipe", None, "tensor"),
            P("pipe", "tensor", "dp"),
            P("pipe", None, None),
            P("pipe", "dp", "tensor"),
            P("pipe", "tensor"),
            P("pipe", "tensor", "dp"),
        ),
        check_vma=False,
    )
```

```python
from functools import partial

import jax
import jax.numpy as jnp
from jax import lax
from jax.experimental import pallas as pl
from jax.experimental.pallas import tpu as pltpu
from jax.sharding import PartitionSpec as P

F32 = jnp.float32
BF16 = jnp.bfloat16
BY_MESH = pl.DeviceIdType.MESH
HEAD = 64
HALF = 3
HEADS = 2 * HALF
WIDE = HALF * HEAD
EPSILON = 1e-06
MASKED = -1000000000.0
CHUNKS = 4
STRIP = 16
TURNS = 2
G_TILE = 256
STEP = 64
BLOCK = 208
QKV = 640
MIX = 256
PAD = MIX - WIDE
TILE = 256

K_IN, K_A, K_B, K_C, K_Y1, K_Y2, K_YT, K_OI, K_OT, K_T1, K_W, K_S, K_G = range(13)
K_Z = K_G + 3
K_V = K_Z + 3
K_E = K_V + 2
N_KINDS = K_E + 1


def dot(a, b):
    return lax.dot_general(a, b, (((1,), (0,)), ((), ())), preferred_element_type=F32)


def dot_nt(a, b):
    return lax.dot_general(a, b, (((1,), (1,)), ((), ())), preferred_element_type=F32)


def dot_tn(a, b):
    return lax.dot_general(a, b, (((0,), (0,)), ((), ())), preferred_element_type=F32)


def loop(count, body):
    def step(j, carry):
        body(j)
        return carry

    lax.fori_loop(0, count, step, 0)


def unit_of(rows):
    centre = rows - jnp.mean(rows, axis=-1, keepdims=True)
    inverse = lax.rsqrt(jnp.mean(centre * centre, axis=-1, keepdims=True) + EPSILON)
    return centre * inverse, inverse


def norm_back(grad, unit, inverse, gain):
    scaled = grad * gain
    first = jnp.mean(scaled, axis=-1, keepdims=True)
    second = jnp.mean(scaled * unit, axis=-1, keepdims=True)
    return inverse * (scaled - first - unit * second)


def gelu_pair(u):
    cdf = 0.5 * (1.0 + lax.erf(u * (0.5**0.5)))
    pdf = jnp.exp(u * u * -0.5) * 0.3989422804014327
    return u * cdf, cdf + u * pdf


def fold(rows):
    return jnp.sum(rows.reshape(rows.shape[0] // 8, 8, rows.shape[1]), axis=0)


def layers_kernel(
    rows_i, rows_t, keys_i, dp_size, z_inside,
    img_own, txt_all, w_qkv, w_proj, w_up, w_down, lengths, gains, shifts, outb, bias_up, bias_qv,
    img_out, txt_out, g_mix, g_up, g_down, vec_out,
    x_s, dy_s, wq_s, wp_s, wu_s, wd_s, small_s, seg_s, a1_s, qkv_s, o_s, r_s, a2_s, gb_s, du_s, p_s, dkv_s, do_s,
    send_s, ra_s, rb_s, rc_s, ys_s, yt_s, y1_s, y2_s, fin_s, acc_s, early_s, esib_s, eall_s, late_s, lall_s,
    half_s, gs_x, gs_u, gs_d, gr_x, gr_u, gr_d, *rest,
):
    if z_inside:
        z1_s, z2_s, zf_s, ssem, rsem, lsem = rest
    else:
        ssem, rsem, lsem = rest
    width = x_s.shape[1]
    p, d, t = lax.axis_index("pipe"), lax.axis_index("dp"), lax.axis_index("tensor")
    core = lax.rem(t, 2)
    sib_t = t + 1 - 2 * core
    peer_t = lax.rem(t + 2, 4)
    other = 1 - p
    sib, peer = (p, d, sib_t), (p, d, peer_t)
    across = (other, d, t)
    txt_own = txt_all.at[core]
    groups = dp_size if z_inside else 1
    adders = [(k, j) for k in range(groups) for j in range(2) if k + j > 0]

    def adder(k, j, back=False):
        dist = dp_size - k if back else k
        return (p, lax.rem(d + dist, dp_size) if k else d, sib_t if j else t)

    partners = [peer, across] + [adder(k, j) for k, j in adders]

    def remote(src, dst, kind, slot, to):
        at = kind * 4 + slot
        return pltpu.make_async_remote_copy(
            src_ref=src, dst_ref=dst, send_sem=ssem.at[at], recv_sem=rsem.at[at],
            device_id=to, device_id_type=BY_MESH,
        )

    def local(src, dst, slot):
        return pltpu.make_async_copy(src, dst, lsem.at[slot])

    image_here = p == 0
    n_img = rows_i * CHUNKS
    n_txt = rows_t * CHUNKS

    wq_own = local(w_qkv, wq_s.at[0 : 3 * WIDE], 0)
    wp_own = local(w_proj, wp_s.at[PAD:MIX], 1)
    wu_own = local(w_up, wu_s.at[:, 0:width], 2)
    wd_own = local(w_down, wd_s.at[0:width], 3)
    img_in = local(img_own, x_s, 5)
    txt_in = local(txt_own, dy_s.at[0:n_txt], 6)
    wq_own.start()

    @pl.when(image_here)
    def _():
        img_in.start()

    @pl.when(jnp.logical_not(image_here))
    def _():
        txt_in.start()

    wp_own.start()
    wu_own.start()
    wd_own.start()
    zero_rows = jnp.zeros((PAD, width), BF16)
    wp_s[0:PAD, :] = zero_rows
    wp_s[MIX : MIX + PAD, :] = zero_rows
    zero_rows = jnp.zeros((QKV - 3 * WIDE, width), BF16)
    wq_s[3 * WIDE : QKV, :] = zero_rows
    wq_s[QKV + 3 * WIDE :, :] = zero_rows
    acc_s[...] = jnp.zeros_like(acc_s)
    small_s[0] = jnp.zeros_like(small_s[0])
    small_s[0, 0:1, 0:width] = bias_up[...]
    small_s[0, 0:1, width : width + WIDE] = bias_qv[0:1, :]
    small_s[0, 0:1, width + 2 * WIDE : width + 3 * WIDE] = bias_qv[1:2, :]

    barrier = pltpu.get_barrier_semaphore()
    for to in partners:
        pl.semaphore_signal(barrier, inc=1, device_id=to, device_id_type=BY_MESH)

    @pl.when(image_here)
    def _():
        img_in.wait()

        def first_norm(i):
            at = pl.ds(pl.multiple_of(i * rows_i, 16), rows_i)
            unit, _ = unit_of(x_s[at, :].astype(F32))
            a1_s[at, :] = (unit * gains[0:1, :] + shifts[0:1, :]).astype(BF16)

        loop(CHUNKS, first_norm)

    pl.semaphore_wait(barrier, len(partners))

    sm_sib = remote(small_s.at[0], small_s.at[1], K_S, 0, sib)
    wq_sib = remote(w_qkv, wq_s.at[QKV : QKV + 3 * WIDE], K_W, 0, sib)
    wp_sib = remote(w_proj, wp_s.at[MIX + PAD :], K_W, 1, sib)
    wu_sib = remote(w_up, wu_s.at[:, width:], K_W, 2, sib)
    wd_sib = remote(w_down, wd_s.at[width:], K_W, 3, sib)

    def x_to_text(i):
        rows = pl.ds(pl.multiple_of(i * rows_t, 16), rows_t)
        return remote(txt_own.at[rows], x_s.at[rows], K_IN, i, across)

    def dy_to_image(i):
        rows = pl.ds(pl.multiple_of(i * rows_i, 16), rows_i)
        return remote(img_own.at[rows], dy_s.at[rows], K_IN, i, across)

    @pl.when(image_here)
    def _():
        loop(CHUNKS, lambda i: x_to_text(i).start())

    sm_sib.start()
    wq_sib.start()

    @pl.when(jnp.logical_not(image_here))
    def _():
        loop(CHUNKS, lambda i: dy_to_image(i).start())

    wp_sib.start()
    wu_sib.start()
    wd_sib.start()

    own_gain = [gains[0:1, :], gains[1:2, :]]
    own_shift = [shifts[0:1, :], shifts[1:2, :]]

    g_arrays = [(gs_x, gr_x, g_mix), (gs_u, gr_u, g_up), (gs_d, gr_d, g_down)]

    def g_exchange(a, m):
        at = pl.ds(pl.multiple_of(m * G_TILE, G_TILE), G_TILE)
        return remote(half_s.at[a % 2, at], g_arrays[a][1].at[at], K_G + m, a, sib)

    def grads_part(a, product, first, final):
        mine, theirs = g_arrays[a][0], half_s.at[a % 2]

        def both(m):
            at = pl.ds(pl.multiple_of(m * G_TILE, G_TILE), G_TILE)
            for ref, value in zip((mine, theirs), product(at)):
                ref[at, :] = (value if first else value + ref[at, :].astype(F32)).astype(BF16)
            if final:
                g_exchange(a, m).start()

        loop(width // G_TILE, both)

    def grads_sum(a):
        mine, theirs = g_arrays[a][0:2]

        def body(m):
            g_exchange(a, m).wait()
            at = pl.ds(pl.multiple_of(m * G_TILE, G_TILE), G_TILE)
            mine[at, :] = (mine[at, :].astype(F32) + theirs[at, :].astype(F32)).astype(BF16)

        loop(width // G_TILE, body)

    share = width // dp_size
    parity = lax.rem(d, 2)
    upper = d // 2
    near = d + 1 - 2 * parity
    far = d + 2 - 4 * upper if z_inside else d

    def share_rows(at):
        return pl.ds(pl.multiple_of(at * share, 16), share)

    def z_near(a, k):
        src = g_arrays[a][0].at[share_rows(1 - parity + 2 * k)]
        return remote(src, z1_s.at[a, k], K_Z, 3 * k + a, (p, near, t))

    def z_far(a):
        return remote(g_arrays[a][0].at[share_rows(far)], z2_s.at[a], K_Z, 6 + a, (p, far, t))

    def z_start(a):
        if z_inside:
            z_near(a, 1 - upper).start()
        else:
            local(g_arrays[a][0], g_arrays[a][2], 20 + a).start()

    def z_middle(a):
        if z_inside:
            z_near(a, 1 - upper).wait()
            mine = g_arrays[a][0]
            rows = share_rows(far)
            mine[rows, :] = (mine[rows, :].astype(F32) + z1_s[a, 1 - upper].astype(F32)).astype(BF16)
            z_far(a).start()

    def z_finish(a):
        if z_inside:
            z_near(a, upper).wait()
            z_far(a).wait()
            total = g_arrays[a][0][share_rows(d), :].astype(F32) + z1_s[a, upper].astype(F32)
            zf_s[a] = total + z2_s[a].astype(F32)
            local(zf_s.at[a], g_arrays[a][2], 20 + a).start()

    def z_end(a):
        if z_inside:
            local(zf_s.at[a], g_arrays[a][2], 20 + a).wait()
        else:
            local(g_arrays[a][0], g_arrays[a][2], 20 + a).wait()

    def one_layer(text):
        rows = rows_t if text else rows_i
        total = rows * CHUNKS
        cuts = [(o, min(BLOCK, rows - o)) for o in range(0, rows, BLOCK)]
        q_off = rows_t if text else 0

        def at_rows(i):
            return pl.ds(pl.multiple_of(i * rows, 16), rows)

        def q_rows(i):
            return pl.ds(pl.multiple_of(i * rows + q_off, 16), rows)

        def by_strips(i, body):
            for o, size in cuts:
                body(pl.ds(pl.multiple_of(i * rows + o, STRIP), size))

        def swap(i, landing, kind):
            return remote(send_s.at[at_rows(i)], landing.at[at_rows(i)], kind, i, peer)

        incoming = dy_to_image if not text else x_to_text

        def wait_input(i):
            cp = remote(x_s.at[at_rows(i)] if text else dy_s.at[at_rows(i)],
                        x_s.at[at_rows(i)] if text else dy_s.at[at_rows(i)], K_IN, i, across)
            cp.wait_recv()

        wq_own.wait()
        wq_sib.wait()
        sm_sib.wait()
        def caption(places):
            bound = lengths[core, 0]
            segment = (places >= bound).astype(jnp.int32)
            for k in range(1, lengths.shape[1]):
                bound = bound + lengths[core, k]
                segment = segment + (places >= bound).astype(jnp.int32)
            return segment

        if text:
            places = lax.broadcasted_iota(jnp.int32, (8, total + 2 * rows_t), 1) - rows_t
            seg_s[...] = jnp.where(places < 0, -1, caption(places))
            txt_in.wait()
            pad = jnp.zeros((rows_t, 2 * QKV), BF16)
            qkv_s[0:rows_t, :] = pad
            qkv_s[rows_t + total : 2 * rows_t + total, :] = pad
            dkv_s[...] = jnp.zeros_like(dkv_s)
        for s in range(2):
            o_s[0:total, s * MIX : s * MIX + PAD] = jnp.zeros((total, PAD), BF16)

        def project(i):
            if text:
                wait_input(i)

            def first_norm(at):
                unit, _ = unit_of(x_s[at, :].astype(F32))
                a1_s[at, :] = (unit * own_gain[0] + own_shift[0]).astype(BF16)

            if text:
                by_strips(i, first_norm)
            left = a1_s[at_rows(i), :]
            lanes = lax.broadcasted_iota(jnp.int32, (1, QKV), 1)
            factor = jnp.where(lanes < WIDE, HEAD**-0.5, 1.0).astype(F32)
            for s in range(2):
                value = dot_nt(left, wq_s[s * QKV : (s + 1) * QKV, :])
                value = (value + small_s[s, 0:1, width : width + QKV]) * factor
                qkv_s[q_rows(i), s * QKV : (s + 1) * QKV] = value.astype(BF16)

        def head_at(h):
            s, hh = h // HALF, h % HALF
            base = s * QKV + hh * HEAD
            return slice(base, base + HEAD), slice(base + WIDE, base + WIDE + HEAD), slice(base + 2 * WIDE, base + 2 * WIDE + HEAD), slice(s * MIX + PAD + hh * HEAD, s * MIX + PAD + hh * HEAD + HEAD)

        span = 3 * rows_t if text else rows_i
        pieces = [(o, min(128, span - o)) for o in range(0, span, 128)]

        def keep_weights(at, value):
            for k, (o, n) in enumerate(pieces):
                p_s[at, k * rows : (k + 1) * rows, 0:n] = value[:, o : o + n]

        def kept_weights(at):
            parts = [p_s[at, k * rows : (k + 1) * rows, 0:n] for k, (o, n) in enumerate(pieces)]
            return jnp.concatenate(parts, axis=1)

        def key_rows(i):
            return pl.ds(pl.multiple_of(i * rows, 16), span)

        def allowed(i):
            if text:
                mine = caption(lax.broadcasted_iota(jnp.int32, (rows, 1), 0) + i * rows)
                keys = seg_s[0:1, pl.ds(pl.multiple_of(i * rows_t, 128), span)]
                return mine == keys
            return lax.broadcasted_iota(jnp.int32, (1, span), 1) < keys_i

        def attend(i):
            ok = allowed(i)
            for h in range(HEADS):
                qc, kc, vc, oc = head_at(h)
                scores = dot_nt(qkv_s[q_rows(i), qc], qkv_s[key_rows(i), kc])
                scores = jnp.where(ok, scores, MASKED)
                raised = jnp.exp(scores - jnp.max(scores, axis=-1, keepdims=True))
                weights = raised * (1.0 / jnp.sum(raised, axis=-1, keepdims=True))
                keep_weights(i * HEADS + h, weights)
                mixed = dot(weights.astype(BF16), qkv_s[key_rows(i), vc])
                o_s[at_rows(i), oc] = mixed.astype(BF16)

        def send_a(i):
            send_s[at_rows(i), :] = dot(o_s[at_rows(i), :], wp_s[...]).astype(BF16)
            swap(i, ra_s, K_A).start()

        if text:

            def forward(i):
                @pl.when(i < CHUNKS)
                def _():
                    project(i)

                @pl.when(i == 1)
                def _():
                    wp_own.wait()
                    wp_sib.wait()

                @pl.when(i > 0)
                def _():
                    attend(i - 1)
                    send_a(i - 1)

            loop(CHUNKS + 1, forward)
        else:

            def forward(i):
                project(i)
                attend(i)

                @pl.when(i == 0)
                def _():
                    wp_own.wait()
                    wp_sib.wait()

                send_a(i)

            loop(CHUNKS, forward)
        wu_own.wait()
        wu_sib.wait()
        wd_own.wait()
        wd_sib.wait()

        def y_copies(i):
            at = at_rows(i)
            if text:
                return [remote(ys_s.at[at], yt_s.at[at], K_YT, i, peer)]
            return [remote(ys_s.at[at], y1_s.at[at], K_Y1, i, across)]

        def owned(i):
            return lax.rem(i, 2) == t // 2

        def y_side(i):
            at = pl.ds(pl.multiple_of(i * rows_i, 16), rows_i)
            there = y1_s if text and i < TURNS else y2_s
            return remote((y1_s if text else ys_s).at[at], there.at[at], K_Y2, i, peer)

        def y_share(i):
            @pl.when(jnp.logical_not(owned(i)))
            def _():
                y_side(i).start()

        def y_sum(i):
            @pl.when(owned(i))
            def _():
                y_side(i).wait_recv()
                at = at_rows(i)
                ys_s[at, :] = (ys_s[at, :].astype(F32) + y2_s[at, :].astype(F32)).astype(BF16)
                y_copies(i)[0].start()

        def hand_on(i):
            def go():
                at = pl.ds(pl.multiple_of(i * rows_i, 16), rows_i)
                remote(y1_s.at[at], y1_s.at[at], K_Y1, i, across).wait_recv()
                y_side(i).start()

            if i < TURNS:
                pl.when(owned(i))(go)
            else:
                go()

        def middle(i):
            if not text:
                wait_input(i)
            swap(i, ra_s, K_A).wait()

            def second_norm(at):
                r = x_s[at, :].astype(F32) + (send_s[at, :].astype(F32) + ra_s[at, :].astype(F32)) + outb[0:1, :]
                r_s[at, :] = r
                unit, _ = unit_of(r)
                a2_s[at, :] = (unit * own_gain[1] + own_shift[1]).astype(BF16)
                acc_s[5] += fold(dy_s[at, :].astype(F32))

            by_strips(i, second_norm)
            left = a2_s[at_rows(i), :]
            grad = dy_s[at_rows(i), :]
            for n in range(2 * width // TILE):
                cols = slice(n * TILE, (n + 1) * TILE)
                s, inner = (n * TILE) // width, (n * TILE) % width
                u = dot(left, wu_s[:, cols]) + small_s[s, 0:1, inner : inner + TILE]
                g, slope = gelu_pair(u)
                gb_s[at_rows(i), cols] = g.astype(BF16)
                du = (dot_nt(grad, wd_s[cols, :]) * slope).astype(BF16)
                du_s[at_rows(i), cols] = du
                acc_s[6 + s, :, inner : inner + TILE] += fold(du.astype(F32))
            send_s[at_rows(i), :] = dot_nt(du_s[at_rows(i), :], wu_s[...]).astype(BF16)
            swap(i, rb_s, K_B).start()
            lower = dot(gb_s[at_rows(i), :], wd_s[...])
            ys_s[at_rows(i), :] = (lower + 0.5 * (r_s[at_rows(i), :] + outb[1:2, :])).astype(BF16)
            if not text:

                @pl.when(i >= TURNS)
                def _():
                    y_copies(i)[0].start()
        parts = (slice(0, total // 2), slice(0 if text else total // 2, total))

        def halves(left, right, part):
            def product(at):
                value = dot_tn(left[part, at], right[part, :])
                return value[:, :width], value[:, width:]

            return product

        def middle_and_grads(i):
            middle(i)
            if text:
                return

            @pl.when(i == 1)
            def _():
                grads_part(2, halves(dy_s, gb_s, parts[0]), True, False)

            @pl.when(i == 2)
            def _():
                grads_part(1, halves(a2_s, du_s, parts[0]), True, False)

        loop(CHUNKS, middle_and_grads)
        grads_part(2, halves(dy_s, gb_s, parts[1]), text, True)
        grads_part(1, halves(a2_s, du_s, parts[1]), text, True)
        grads_sum(2)
        z_start(2)
        grads_sum(1)
        z_start(1)
        if z_inside:
            z_near(2, upper).start()

        dq_s, drb_s = gb_s, a2_s
        for s in range(2):
            dq_s[0:total, s * QKV + 3 * WIDE : (s + 1) * QKV] = jnp.zeros((total, QKV - 3 * WIDE), BF16)

        def attend_back(i):
            swap(i, rb_s, K_B).wait()

            def back_norm(at):
                grad = send_s[at, :].astype(F32) + rb_s[at, :].astype(F32)
                unit, inverse = unit_of(r_s[at, :])
                dr = dy_s[at, :].astype(F32) + norm_back(grad, unit, inverse, own_gain[1])
                r_s[at, :] = dr
                drb_s[at, :] = dr.astype(BF16)
                acc_s[1] += fold(grad * unit)
                acc_s[3] += fold(grad)
                acc_s[4] += fold(dr)

            by_strips(i, back_norm)
            do_s[0:rows, :] = dot_nt(drb_s[at_rows(i), :], wp_s[...]).astype(BF16)
            for h in range(HEADS):
                qc, kc, vc, oc = head_at(h)
                weights = kept_weights(i * HEADS + h)
                grad_o = do_s[0:rows, oc]
                keys = qkv_s[key_rows(i), kc]
                slope = dot_nt(grad_o, qkv_s[key_rows(i), vc])
                ds = (weights * (slope - jnp.sum(slope * weights, axis=-1, keepdims=True))).astype(BF16)
                dq = dot(ds, keys).astype(BF16) * (HEAD**-0.5)
                dk = dot_tn(ds, qkv_s[q_rows(i), qc])
                dv = dot_tn(weights.astype(BF16), grad_o)
                dq_s[at_rows(i), qc] = dq.astype(BF16)
                if text:
                    hc = slice(h * HEAD, (h + 1) * HEAD)
                    hv = slice((HEADS + h) * HEAD, (HEADS + h + 1) * HEAD)
                    dkv_s[key_rows(i), hc] += dk
                    dkv_s[key_rows(i), hv] += dv
                else:
                    dq_s[at_rows(i), kc] = dk.astype(BF16)
                    dq_s[at_rows(i), vc] = dv.astype(BF16)

        def send_c(i):
            if text:
                for s in range(2):
                    k0 = s * QKV + WIDE
                    dq_s[at_rows(i), k0 : k0 + WIDE] = dkv_s[q_rows(i), s * WIDE : (s + 1) * WIDE].astype(BF16)
                    v0 = 2 * WIDE + s * WIDE
                    dq_s[at_rows(i), k0 + WIDE : k0 + 2 * WIDE] = dkv_s[q_rows(i), v0 : v0 + WIDE].astype(BF16)
            grad = dq_s[at_rows(i), 0 : 2 * QKV]
            send_s[at_rows(i), :] = dot(grad, wq_s[...]).astype(BF16)
            swap(i, rc_s, K_C).start()
            for s in range(2):
                acc_s[8 + s, :, 0:QKV] += fold(grad[:, s * QKV : (s + 1) * QKV].astype(F32))

        def own_img(i):
            return img_out.at[pl.ds(pl.multiple_of(core * n_img + i * rows_i, 16), rows_i)]

        def own_txt(i):
            return txt_out.at[pl.ds(pl.multiple_of(core * n_txt + i * rows_t, 16), rows_t)]

        def img_copies(i):
            src = (y1_s if text else fin_s).at[pl.ds(pl.multiple_of(i * rows_i, 16), rows_i)]
            return local(src, own_img(i), 8 + i), remote(src, own_img(i), K_OI, i, sib)

        def txt_copies(i):
            src = ys_s.at[pl.ds(pl.multiple_of(i * rows_t, 16), rows_t)]
            return local(src, own_txt(i), 12 + i), remote(src, own_txt(i), K_OT, i, sib)

        def dx_copies(i):
            src = rb_s.at[pl.ds(pl.multiple_of(i * rows_t, 16), rows_t)]
            return remote(src, own_txt(i), K_T1, i, across)

        def dx_relay(i):
            return remote(own_txt(i), own_txt(i), K_OT, i, sib)

        if text:

            def own_y(i):
                y_copies(i)[0].wait()
                at = at_rows(i)
                ys_s[at, :] = (ys_s[at, :].astype(F32) + yt_s[at, :].astype(F32)).astype(BF16)
                for cp in txt_copies(i):
                    cp.start()

            def image_y(i):
                at = pl.ds(pl.multiple_of(i * rows_i, 16), rows_i)
                if i < TURNS:

                    @pl.when(owned(i))
                    def _():
                        y_side(i).wait_send()

                    @pl.when(jnp.logical_not(owned(i)))
                    def _():
                        y_side(i).wait_recv()

                else:
                    y_side(i).wait()
                    y1_s[at, :] = (y1_s[at, :].astype(F32) + y2_s[at, :].astype(F32)).astype(BF16)
                for cp in img_copies(i):
                    cp.start()

        def last(i):
            swap(i, rc_s, K_C).wait()

            def body(at):
                grad = send_s[at, :].astype(F32) + rc_s[at, :].astype(F32)
                unit, inverse = unit_of(x_s[at, :].astype(F32))
                dx = (r_s[at, :] + norm_back(grad, unit, inverse, own_gain[0])).astype(BF16)
                if text:
                    rb_s[at, :] = dx
                else:
                    fin_s[at, :] = dx
                acc_s[0] += fold(grad * unit)
                acc_s[2] += fold(grad)

            by_strips(i, body)

            for cp in [dx_copies(i)] if text else img_copies(i):
                cp.start()

        if not text:
            for i in range(TURNS):
                y_share(i)
        def mixed_grads(part):
            def product(at):
                first = dot_tn(a1_s[part, at], dq_s[part, 0 : 2 * QKV])
                second = dot_tn(drb_s[part, at], o_s[part, :])

                def joined(s):
                    left, right = first[:, s * QKV : (s + 1) * QKV], second[:, s * MIX : (s + 1) * MIX]
                    seam = left[:, MIX * 2 :] + right[:, 0 : QKV - 2 * MIX]
                    return jnp.concatenate([left[:, : MIX * 2], seam, right[:, QKV - 2 * MIX :]], axis=1)

                return joined(0), joined(1)

            return product

        group = d if z_inside else 0

        def early_copy(k):
            return remote(early_s.at[0], eall_s.at[group], K_E, k - 1, adder(k, 0))

        def early_arrival(k):
            place = lax.rem(d + dp_size - k, dp_size)
            return remote(eall_s.at[place], eall_s.at[place], K_E, k - 1, adder(k, 0, True))

        early_sib = remote(early_s.at[1], esib_s, K_S, 1, sib)

        def early_start():
            sums = jnp.sum(acc_s[...], axis=1)
            for j, order in enumerate(((1, 3, 4, 5, 6, 7, 8, 9), (1, 3, 4, 5, 7, 6, 9, 8))):
                for row, src in enumerate(order):
                    early_s[j, row : row + 1, :] = sums[src : src + 1, :]
            early_sib.start()

        def early_next():
            early_sib.wait()
            early_s[0] = early_s[0] + esib_s[...]
            eall_s[group] = early_s[0]
            for k in range(1, groups):
                early_copy(k).start()

        def late_copy(k, j):
            return remote(late_s, lall_s.at[2 * group + core], K_V, 2 * k + j, adder(k, j))

        def late_arrival(k, j):
            place = 2 * (lax.rem(d + dp_size - k, dp_size) if k else group) + (1 - core if j else core)
            return remote(lall_s.at[place], lall_s.at[place], K_V, 2 * k + j, adder(k, j, True))

        def late_start():
            late_s[...] = jnp.zeros_like(late_s)
            for r, src in enumerate((0, 2)):
                row = jnp.sum(acc_s[src], axis=0, keepdims=True)
                for c in range(width // 128):
                    late_s[8 * r + c : 8 * r + c + 1, :] = row[:, c * 128 : (c + 1) * 128]
            for k, j in adders:
                late_copy(k, j).start()
            lall_s[2 * group + core] = late_s[...]

        def vectors_finish():
            for k in range(1, groups):
                early_copy(k).wait_send()
                early_arrival(k).wait_recv()
            for k, j in adders:
                late_copy(k, j).wait_send()
                late_arrival(k, j).wait_recv()
            early, late = eall_s[0], lall_s[0]
            for k in range(1, groups):
                early = early + eall_s[k]
            for k in range(1, 2 * groups):
                late = late + lall_s[k]
            vec_out[...] = jnp.zeros_like(vec_out)
            for row, dst in enumerate((1, 3, 4, 5, 6, 7, 8, 9)):
                vec_out[dst : dst + 1, :] = early[row : row + 1, :]
            for r, dst in enumerate((0, 2)):
                for c in range(width // 128):
                    vec_out[dst : dst + 1, c * 128 : (c + 1) * 128] = late[8 * r + c : 8 * r + c + 1, :]

        if text:

            def backward(i):
                @pl.when(i < CHUNKS)
                def _():
                    attend_back(i)

                @pl.when(i == 2)
                def _():
                    z_middle(2)

                @pl.when(i == 3)
                def _():
                    z_middle(1)

                @pl.when(i > 0)
                def _():
                    send_c(i - 1)

                @pl.when(i > 2)
                def _():
                    last(i - 3)

            loop(CHUNKS + 1, backward)
        else:

            def backward(i):
                @pl.when(i == 2)
                def _():
                    z_middle(2)

                @pl.when(i == 3)
                def _():
                    z_middle(1)

                attend_back(i)
                send_c(i)

                @pl.when(i == 2)
                def _():
                    grads_part(0, mixed_grads(parts[0]), True, False)

            loop(CHUNKS, backward)


        if text:
            for i in range(TURNS, CHUNKS):
                hand_on(i)
            loop(CHUNKS, lambda i: y_copies(i)[0].start())
        grads_part(0, mixed_grads(parts[1]), text, True)
        grads_sum(0)
        z_start(0)
        if z_inside:
            z_near(1, upper).start()
            z_near(0, upper).start()
        early_start()
        if text:
            last(CHUNKS - 2)
            last(CHUNKS - 1)
            early_next()
            z_middle(0)
            for i in range(TURNS):
                hand_on(i)
        else:
            for i in range(TURNS):
                y_sum(i)
            loop(2, last)
            early_next()
            z_middle(0)
            last(CHUNKS - 2)
            last(CHUNKS - 1)

        late_start()
        if text:
            loop(CHUNKS, own_y)
        z_finish(2)
        z_finish(1)
        if text:
            for i in range(CHUNKS):
                image_y(i)
        z_finish(0)
        vectors_finish()

        def finish(i):
            if text:
                dy_to_image(i).wait_send()
                dx_copies(i).wait_send()
                here, there = txt_copies(i)
                here.wait()
                there.wait()
            else:
                x_to_text(i).wait_send()
                if i < TURNS:

                    @pl.when(owned(i))
                    def _():
                        y_copies(i)[0].wait_send()

                    @pl.when(jnp.logical_not(owned(i)))
                    def _():
                        y_side(i).wait_send()

                else:
                    y_copies(i)[0].wait_send()
                dx_copies(i).wait_recv()
                dx_relay(i).start()
            here, there = img_copies(i)
            here.wait()
            there.wait()

        for i in range(CHUNKS):
            finish(i)
        if not text:
            loop(CHUNKS, lambda i: dx_relay(i).wait())
        for a in range(3):
            z_end(a)

    @pl.when(image_here)
    def _():
        one_layer(False)

    @pl.when(jnp.logical_not(image_here))
    def _():
        one_layer(True)


def finish_kernel(
    images, keys_i, rows_i, img_in, txt_in, g_x, g_u, g_d, vec,
    img_out, txt_out, gains, shifts, qkv, bias_qv, proj, outb, up, bias_up, down,
    buf, out_s, gx_s, qkv_s, txt_s, gu_s, gd_s, sem,
):
    plain = [(g_u, gu_s, up), (g_d, gd_s, down), (txt_in, txt_s, txt_out)]
    fetch = [pltpu.make_async_copy(src, mid, sem.at[k]) for k, (src, mid, dst) in enumerate(plain)]
    copies = [pltpu.make_async_copy(mid, dst, sem.at[5 + k]) for k, (src, mid, dst) in enumerate(plain)]
    gx_in = pltpu.make_async_copy(g_x, gx_s, sem.at[3])
    gx_in.start()
    blocks = [(o, min(STEP, rows_i - o)) for o in range(0, rows_i, STEP)]
    loads = [
        pltpu.make_async_copy(img_in.at[:, o : o + n], buf.at[:, o : o + n], sem.at[8 + k])
        for k, (o, n) in enumerate(blocks)
    ]
    for cp in loads:
        cp.start()
    for cp in fetch:
        cp.start()
    gains[...] = vec[0:2, :]
    shifts[...] = vec[2:4, :]
    outb[...] = vec[4:6, :]
    bias_up[...] = vec[6:7, :]
    bias_qv[0:1, :] = vec[8:9, 0:WIDE]
    bias_qv[1:2, :] = vec[8:9, 2 * WIDE : 3 * WIDE]
    gx_in.wait()
    proj[...] = gx_s[:, 3 * WIDE :].T
    for k in range(3):
        qkv_s[k] = gx_s[:, k * WIDE : (k + 1) * WIDE]
    q_out = pltpu.make_async_copy(qkv_s, qkv, sem.at[4])
    q_out.start()
    stores = []
    for k, (o, n) in enumerate(blocks):
        loads[k].wait()
        rows = min(n, keys_i - o)
        value = jnp.swapaxes(buf[:, o : o + n, :].astype(F32), 0, 1)
        out_s[o : o + n] = value.astype(BF16)
        cp = pltpu.make_async_copy(out_s.at[o : o + rows], img_out.at[o : o + rows], sem.at[16 + k])
        cp.start()
        stores.append(cp)
        if k < len(fetch):
            fetch[k].wait()
            copies[k].start()
    for cp in copies + [q_out] + stores:
        cp.wait()


def finish_outputs(images, keys_i, rows_i, img_out, txt_out, g_x, g_u, g_d, vec):
    share, width = g_x.shape
    sds, v = jax.ShapeDtypeStruct, pltpu.VMEM
    any_spec, vmem_spec = pl.BlockSpec(memory_space=pl.ANY), pl.BlockSpec(memory_space=pltpu.VMEM)
    outs = [
        (sds((keys_i, images, width), BF16), any_spec),
        (sds(txt_out.shape, BF16), any_spec),
        (sds((2, width), F32), vmem_spec),
        (sds((2, width), F32), vmem_spec),
        (sds((3, share, WIDE), F32), any_spec),
        (sds((2, WIDE), F32), vmem_spec),
        (sds((WIDE, share), F32), vmem_spec),
        (sds((2, width), F32), vmem_spec),
        (sds((share, width), F32), any_spec),
        (sds((1, width), F32), vmem_spec),
        (sds((share, width), F32), any_spec),
    ]
    img, txt, gains, shifts, qkv, bias_qv, proj, outb, up, bias_up, down = pl.pallas_call(
        partial(finish_kernel, images, keys_i, rows_i),
        out_shape=[o[0] for o in outs],
        in_specs=[any_spec] * 5 + [vmem_spec],
        out_specs=[o[1] for o in outs],
        scratch_shapes=[
            v((images, rows_i, width), BF16), v((rows_i, images, width), BF16), v((share, width), F32),
            v((3, share, WIDE), F32), v(txt_out.shape, BF16), v((share, width), F32), v((share, width), F32),
            pltpu.SemaphoreType.DMA((24,)),
        ],
        compiler_params=pltpu.CompilerParams(vmem_limit_bytes=60 << 20),
    )(img_out.reshape(images, rows_i, width), txt_out, g_x, g_u, g_d, vec)
    return (
        jnp.transpose(img, (1, 0, 2))[None], txt.reshape(2, -1, width)[None], gains[None], shifts[None],
        jnp.transpose(qkv, (1, 0, 2))[None], bias_qv[None], proj[None], outb[None], up[None], bias_up, down.T[None],
    )


def per_device(
    image_side, text_side, caption_lengths, norm_gains, norm_shifts, w_qkv, bias_qv, w_proj, out_bias, w_up, bias_up, w_down,
):
    dp_size = lax.axis_size("dp")
    core = lax.rem(lax.axis_index("tensor"), 2)
    images, keys_i, width = image_side.shape[1:]
    blocks, length = text_side.shape[1:3]
    per_core = images // 2
    rows_i = -(-(per_core // CHUNKS * keys_i) // 16) * 16
    rows_t = length * (blocks // 2) // CHUNKS
    share = width // dp_size
    z_inside = dp_size == 4 and share % 16 == 0

    img = lax.dynamic_slice_in_dim(image_side[0], core * per_core, per_core, 0)
    img = jnp.pad(img, ((0, 0), (0, rows_i - keys_i), (0, 0))).reshape(per_core * rows_i, width)
    wq = jnp.transpose(w_qkv[0], (1, 2, 0)).reshape(3 * WIDE, width)
    n_i, n_t = rows_i * CHUNKS, rows_t * CHUNKS
    columns = (width, width, width)
    sds = jax.ShapeDtypeStruct
    grad_type = (lambda w: sds((share, w), F32)) if z_inside else (lambda w: sds((width, w), BF16))
    outs = [sds((2 * n_i, width), BF16), sds((2 * n_t, width), BF16)]
    outs += [grad_type(w) for w in columns] + [sds((16, width), F32)]
    any_spec, vmem_spec = pl.BlockSpec(memory_space=pl.ANY), pl.BlockSpec(memory_space=pltpu.VMEM)
    v = pltpu.VMEM
    scratch = [
        v((n_i, width), BF16), v((n_i, width), BF16),
        v((2 * QKV, width), BF16), v((2 * MIX, width), BF16), v((width, 2 * width), BF16), v((2 * width, width), BF16),
        v((2, 8, width + QKV), F32), v((8, n_t + 2 * rows_t), jnp.int32),
        v((n_i, width), BF16), v((max(n_i, n_t + 2 * rows_t), 2 * QKV), BF16), v((n_i, 2 * MIX), BF16), v((n_i, width), F32),
        v((n_i, width), BF16), v((n_i, 2 * width), BF16), v((n_i, 2 * width), BF16),
        v((CHUNKS * HEADS, max(-(-rows_i // 128) * rows_i, 3 * rows_t // 128 * rows_t), 128), F32),
        v((n_t + 2 * rows_t, 2 * HEADS * HEAD), F32), v((max(rows_i, rows_t), 2 * MIX), BF16),
        v((n_i, width), BF16), v((n_i, width), BF16), v((n_i, width), BF16), v((n_i, width), BF16),
        v((n_i, width), BF16), v((n_t, width), BF16), v((n_i, width), BF16), v((n_i, width), BF16), v((n_i, width), BF16),
        v((16, 8, width), F32), v((2, 8, width), F32), v((8, width), F32), v((dp_size if z_inside else 1, 8, width), F32),
        v((16, 128), F32), v((2 * dp_size if z_inside else 2, 16, 128), F32),
    ]
    scratch += [v((2, width, width), BF16)]
    scratch += [v((width, w), BF16) for w in columns] + [v((width, w), BF16) for w in columns]
    if z_inside:
        scratch += [v((3, 2, share, width), BF16), v((3, share, width), BF16), v((3, share, width), F32)]
    dma = pltpu.SemaphoreType.DMA
    scratch += [dma((4 * N_KINDS,)), dma((4 * N_KINDS,)), dma((24,))]
    img_out, txt_out, g_x, g_u, g_d, vec = pl.pallas_call(
        partial(layers_kernel, rows_i, rows_t, keys_i, dp_size, z_inside),
        out_shape=outs,
        in_specs=[any_spec] * 6 + [pl.BlockSpec(memory_space=pltpu.SMEM)] + [vmem_spec] * 5,
        out_specs=[any_spec] * 5 + [vmem_spec],
        scratch_shapes=scratch,
        compiler_params=pltpu.CompilerParams(collective_id=0, has_side_effects=True, vmem_limit_bytes=60 << 20),
    )(
        img, text_side[0], wq, w_proj[0], w_up[0], w_down[0], caption_lengths,
        norm_gains[0], norm_shifts[0], out_bias[0], bias_up, bias_qv[0],
    )
    if z_inside:
        return finish_outputs(images, keys_i, rows_i, img_out, txt_out, g_x, g_u, g_d, vec)
    else:
        def scatter(grad):
            return lax.psum_scatter(grad, "dp", scatter_dimension=0, tiled=True).astype(F32)

        g_x, g_u, g_d = (scatter(g) for g in (g_x, g_u, g_d))
        vec = lax.psum(vec, "dp")
    image_result = img_out.reshape(images, rows_i, width)[:, :keys_i][None]
    text_result = txt_out.reshape(blocks, length, width)[None]
    return (
        image_result,
        text_result,
        vec[0:2][None],
        vec[2:4][None],
        g_x[:, : 3 * WIDE].reshape(share, 3, WIDE)[None],
        jnp.stack([vec[8, 0:WIDE], vec[8, 2 * WIDE : 3 * WIDE]])[None],
        g_x[:, 3 * WIDE :].T[None],
        vec[4:6][None],
        g_u[None],
        vec[6][None],
        g_d.T[None],
    )


def solution(mesh):
    placed = (
        P("pipe", "dp", None, None),
        P("pipe", "dp", None, None),
        P("dp", None),
        P("pipe", None, None),
        P("pipe", None, None),
        P("pipe", None, None, "tensor"),
        P("pipe", None, "tensor"),
        P("pipe", "tensor", None),
        P("pipe", None, None),
        P("pipe", None, "tensor"),
        P("pipe", "tensor"),
        P("pipe", "tensor", None),
    )
    return jax.shard_map(
        per_device,
        mesh=mesh,
        in_specs=placed,
        out_specs=(
            P("pipe", "dp", None, None),
            P("pipe", "dp", None, None),
            P("pipe", None, None),
            P("pipe", None, None),
            P("pipe", "dp", None, "tensor"),
            P("pipe", None, "tensor"),
            P("pipe", "tensor", "dp"),
            P("pipe", None, None),
            P("pipe", "dp", "tensor"),
            P("pipe", "tensor"),
            P("pipe", "tensor", "dp"),
        ),
        check_vma=False,
    )
```

```python
from functools import partial

import jax
import jax.numpy as jnp
from jax import lax
from jax.experimental import pallas as pl
from jax.experimental.pallas import tpu as pltpu
from jax.sharding import PartitionSpec as P

F32 = jnp.float32
BF16 = jnp.bfloat16
BY_MESH = pl.DeviceIdType.MESH
HEAD = 64
HALF = 3
HEADS = 2 * HALF
WIDE = HALF * HEAD
EPSILON = 1e-06
MASKED = -1000000000.0
CHUNKS = 4
STRIP = 16
TURNS = 2
EARLY = 2
G_TILE = 256
STEP = 64
BLOCK = 208
QKV = 640
MIX = 256
PAD = MIX - WIDE
TILE = 256

K_IN, K_A, K_B, K_C, K_Y1, K_Y2, K_YT, K_OI, K_OT, K_T1, K_W, K_S, K_G = range(13)
K_Z = K_G + 3
K_V = K_Z + 3
K_E = K_V + 2
N_KINDS = K_E + 1


def dot(a, b):
    return lax.dot_general(a, b, (((1,), (0,)), ((), ())), preferred_element_type=F32)


def dot_nt(a, b):
    return lax.dot_general(a, b, (((1,), (1,)), ((), ())), preferred_element_type=F32)


def dot_tn(a, b):
    return lax.dot_general(a, b, (((0,), (0,)), ((), ())), preferred_element_type=F32)


def loop(count, body):
    def step(j, carry):
        body(j)
        return carry

    lax.fori_loop(0, count, step, 0)


def unit_of(rows):
    centre = rows - jnp.mean(rows, axis=-1, keepdims=True)
    inverse = lax.rsqrt(jnp.mean(centre * centre, axis=-1, keepdims=True) + EPSILON)
    return centre * inverse, inverse


def norm_back(grad, unit, inverse, gain):
    scaled = grad * gain
    first = jnp.mean(scaled, axis=-1, keepdims=True)
    second = jnp.mean(scaled * unit, axis=-1, keepdims=True)
    return inverse * (scaled - first - unit * second)


def gelu_pair(u):
    cdf = 0.5 * (1.0 + lax.erf(u * (0.5**0.5)))
    pdf = jnp.exp(u * u * -0.5) * 0.3989422804014327
    return u * cdf, cdf + u * pdf


def fold(rows):
    return jnp.sum(rows.reshape(rows.shape[0] // 8, 8, rows.shape[1]), axis=0)


def layers_kernel(
    rows_i, rows_t, keys_i, dp_size, z_inside,
    img_own, txt_all, w_qkv, w_proj, w_up, w_down, lengths, gains, shifts, outb, bias_up, bias_qv,
    img_out, txt_out, g_mix, g_up, g_down, vec_out,
    x_s, dy_s, wq_s, wp_s, wu_s, wd_s, small_s, seg_s, a1_s, qkv_s, o_s, r_s, a2_s, gb_s, du_s, p_s, dkv_s, do_s,
    send_s, ra_s, rb_s, rc_s, ys_s, yt_s, y1_s, y2_s, fin_s, acc_s, early_s, esib_s, eall_s, late_s, lall_s,
    half_s, gs_x, gs_u, gs_d, gr_x, gr_u, gr_d, *rest,
):
    if z_inside:
        z1_s, z2_s, zf_s, ssem, rsem, lsem = rest
    else:
        ssem, rsem, lsem = rest
    width = x_s.shape[1]
    p, d, t = lax.axis_index("pipe"), lax.axis_index("dp"), lax.axis_index("tensor")
    core = lax.rem(t, 2)
    sib_t = t + 1 - 2 * core
    peer_t = lax.rem(t + 2, 4)
    other = 1 - p
    sib, peer = (p, d, sib_t), (p, d, peer_t)
    across = (other, d, t)
    txt_own = txt_all.at[core]
    groups = dp_size if z_inside else 1
    adders = [(k, j) for k in range(groups) for j in range(2) if k + j > 0]

    def adder(k, j, back=False):
        dist = dp_size - k if back else k
        return (p, lax.rem(d + dist, dp_size) if k else d, sib_t if j else t)

    partners = [peer, across] + [adder(k, j) for k, j in adders]

    def remote(src, dst, kind, slot, to):
        at = kind * 4 + slot
        return pltpu.make_async_remote_copy(
            src_ref=src, dst_ref=dst, send_sem=ssem.at[at], recv_sem=rsem.at[at],
            device_id=to, device_id_type=BY_MESH,
        )

    def local(src, dst, slot):
        return pltpu.make_async_copy(src, dst, lsem.at[slot])

    image_here = p == 0
    n_img = rows_i * CHUNKS
    n_txt = rows_t * CHUNKS

    wq_own = local(w_qkv, wq_s.at[0 : 3 * WIDE], 0)
    wp_own = local(w_proj, wp_s.at[PAD:MIX], 1)
    wu_own = local(w_up, wu_s.at[:, 0:width], 2)
    wd_own = local(w_down, wd_s.at[0:width], 3)
    img_in = local(img_own, x_s, 5)
    txt_in = local(txt_own, dy_s.at[0:n_txt], 6)
    wq_own.start()

    @pl.when(image_here)
    def _():
        img_in.start()

    @pl.when(jnp.logical_not(image_here))
    def _():
        txt_in.start()

    wp_own.start()
    wu_own.start()
    wd_own.start()
    zero_rows = jnp.zeros((PAD, width), BF16)
    wp_s[0:PAD, :] = zero_rows
    wp_s[MIX : MIX + PAD, :] = zero_rows
    zero_rows = jnp.zeros((QKV - 3 * WIDE, width), BF16)
    wq_s[3 * WIDE : QKV, :] = zero_rows
    wq_s[QKV + 3 * WIDE :, :] = zero_rows
    acc_s[...] = jnp.zeros_like(acc_s)
    small_s[0] = jnp.zeros_like(small_s[0])
    small_s[0, 0:1, 0:width] = bias_up[...]
    small_s[0, 0:1, width : width + WIDE] = bias_qv[0:1, :]
    small_s[0, 0:1, width + 2 * WIDE : width + 3 * WIDE] = bias_qv[1:2, :]

    barrier = pltpu.get_barrier_semaphore()
    for to in partners:
        pl.semaphore_signal(barrier, inc=1, device_id=to, device_id_type=BY_MESH)

    @pl.when(image_here)
    def _():
        img_in.wait()

        def first_norm(i):
            at = pl.ds(pl.multiple_of(i * rows_i, 16), rows_i)
            unit, _ = unit_of(x_s[at, :].astype(F32))
            a1_s[at, :] = (unit * gains[0:1, :] + shifts[0:1, :]).astype(BF16)

        loop(CHUNKS, first_norm)

    pl.semaphore_wait(barrier, len(partners))

    sm_sib = remote(small_s.at[0], small_s.at[1], K_S, 0, sib)
    wq_sib = remote(w_qkv, wq_s.at[QKV : QKV + 3 * WIDE], K_W, 0, sib)
    wp_sib = remote(w_proj, wp_s.at[MIX + PAD :], K_W, 1, sib)
    wu_sib = remote(w_up, wu_s.at[:, width:], K_W, 2, sib)
    wd_sib = remote(w_down, wd_s.at[width:], K_W, 3, sib)

    def x_to_text(i):
        rows = pl.ds(pl.multiple_of(i * rows_t, 16), rows_t)
        return remote(txt_own.at[rows], x_s.at[rows], K_IN, i, across)

    def dy_to_image(i):
        rows = pl.ds(pl.multiple_of(i * rows_i, 16), rows_i)
        return remote(img_own.at[rows], dy_s.at[rows], K_IN, i, across)

    @pl.when(image_here)
    def _():
        loop(CHUNKS, lambda i: x_to_text(i).start())

    sm_sib.start()
    wq_sib.start()

    @pl.when(jnp.logical_not(image_here))
    def _():
        loop(CHUNKS, lambda i: dy_to_image(i).start())

    wp_sib.start()
    wu_sib.start()
    wd_sib.start()

    own_gain = [gains[0:1, :], gains[1:2, :]]
    own_shift = [shifts[0:1, :], shifts[1:2, :]]

    g_arrays = [(gs_x, gr_x, g_mix), (gs_u, gr_u, g_up), (gs_d, gr_d, g_down)]

    def g_exchange(a, m):
        at = pl.ds(pl.multiple_of(m * G_TILE, G_TILE), G_TILE)
        return remote(half_s.at[a % 2, at], g_arrays[a][1].at[at], K_G + m, a, sib)

    def grads_part(a, product, first, final):
        mine, theirs = g_arrays[a][0], half_s.at[a % 2]

        def both(m):
            at = pl.ds(pl.multiple_of(m * G_TILE, G_TILE), G_TILE)
            for ref, value in zip((mine, theirs), product(at)):
                ref[at, :] = (value if first else value + ref[at, :].astype(F32)).astype(BF16)
            if final:
                g_exchange(a, m).start()

        loop(width // G_TILE, both)

    def grads_sum(a):
        mine, theirs = g_arrays[a][0:2]

        def body(m):
            g_exchange(a, m).wait()
            at = pl.ds(pl.multiple_of(m * G_TILE, G_TILE), G_TILE)
            mine[at, :] = (mine[at, :].astype(F32) + theirs[at, :].astype(F32)).astype(BF16)

        loop(width // G_TILE, body)

    share = width // dp_size
    parity = lax.rem(d, 2)
    upper = d // 2
    near = d + 1 - 2 * parity
    far = d + 2 - 4 * upper if z_inside else d

    def share_rows(at):
        return pl.ds(pl.multiple_of(at * share, 16), share)

    def z_near(a, k):
        src = g_arrays[a][0].at[share_rows(1 - parity + 2 * k)]
        return remote(src, z1_s.at[a, k], K_Z, 3 * k + a, (p, near, t))

    def z_far(a):
        return remote(g_arrays[a][0].at[share_rows(far)], z2_s.at[a], K_Z, 6 + a, (p, far, t))

    def z_start(a):
        if z_inside:
            z_near(a, 1 - upper).start()
        else:
            local(g_arrays[a][0], g_arrays[a][2], 20 + a).start()

    def z_middle(a):
        if z_inside:
            z_near(a, 1 - upper).wait()
            mine = g_arrays[a][0]
            rows = share_rows(far)
            mine[rows, :] = (mine[rows, :].astype(F32) + z1_s[a, 1 - upper].astype(F32)).astype(BF16)
            z_far(a).start()

    def z_finish(a):
        if z_inside:
            z_near(a, upper).wait()
            z_far(a).wait()
            total = g_arrays[a][0][share_rows(d), :].astype(F32) + z1_s[a, upper].astype(F32)
            zf_s[a] = total + z2_s[a].astype(F32)
            local(zf_s.at[a], g_arrays[a][2], 20 + a).start()

    def z_end(a):
        if z_inside:
            local(zf_s.at[a], g_arrays[a][2], 20 + a).wait()
        else:
            local(g_arrays[a][0], g_arrays[a][2], 20 + a).wait()

    def one_layer(text):
        rows = rows_t if text else rows_i
        total = rows * CHUNKS
        cuts = [(o, min(BLOCK, rows - o)) for o in range(0, rows, BLOCK)]
        q_off = rows_t if text else 0

        def at_rows(i):
            return pl.ds(pl.multiple_of(i * rows, 16), rows)

        def q_rows(i):
            return pl.ds(pl.multiple_of(i * rows + q_off, 16), rows)

        def by_strips(i, body):
            for o, size in cuts:
                body(pl.ds(pl.multiple_of(i * rows + o, STRIP), size))

        def swap(i, landing, kind):
            return remote(send_s.at[at_rows(i)], landing.at[at_rows(i)], kind, i, peer)

        incoming = dy_to_image if not text else x_to_text

        def wait_input(i):
            cp = remote(x_s.at[at_rows(i)] if text else dy_s.at[at_rows(i)],
                        x_s.at[at_rows(i)] if text else dy_s.at[at_rows(i)], K_IN, i, across)
            cp.wait_recv()

        wq_own.wait()
        wq_sib.wait()
        sm_sib.wait()
        def caption(places):
            bound = lengths[core, 0]
            segment = (places >= bound).astype(jnp.int32)
            for k in range(1, lengths.shape[1]):
                bound = bound + lengths[core, k]
                segment = segment + (places >= bound).astype(jnp.int32)
            return segment

        if text:
            places = lax.broadcasted_iota(jnp.int32, (8, total + 2 * rows_t), 1) - rows_t
            seg_s[...] = jnp.where(places < 0, -1, caption(places))
            txt_in.wait()
            pad = jnp.zeros((rows_t, 2 * QKV), BF16)
            qkv_s[0:rows_t, :] = pad
            qkv_s[rows_t + total : 2 * rows_t + total, :] = pad
            dkv_s[...] = jnp.zeros_like(dkv_s)
        for s in range(2):
            o_s[0:total, s * MIX : s * MIX + PAD] = jnp.zeros((total, PAD), BF16)

        def project(i):
            if text:
                wait_input(i)

            def first_norm(at):
                unit, _ = unit_of(x_s[at, :].astype(F32))
                a1_s[at, :] = (unit * own_gain[0] + own_shift[0]).astype(BF16)

            if text:
                by_strips(i, first_norm)
            left = a1_s[at_rows(i), :]
            lanes = lax.broadcasted_iota(jnp.int32, (1, QKV), 1)
            factor = jnp.where(lanes < WIDE, HEAD**-0.5, 1.0).astype(F32)
            for s in range(2):
                value = dot_nt(left, wq_s[s * QKV : (s + 1) * QKV, :])
                value = (value + small_s[s, 0:1, width : width + QKV]) * factor
                qkv_s[q_rows(i), s * QKV : (s + 1) * QKV] = value.astype(BF16)

        def head_at(h):
            s, hh = h // HALF, h % HALF
            base = s * QKV + hh * HEAD
            return slice(base, base + HEAD), slice(base + WIDE, base + WIDE + HEAD), slice(base + 2 * WIDE, base + 2 * WIDE + HEAD), slice(s * MIX + PAD + hh * HEAD, s * MIX + PAD + hh * HEAD + HEAD)

        span = 3 * rows_t if text else rows_i
        pieces = [(o, min(128, span - o)) for o in range(0, span, 128)]

        def keep_weights(at, value):
            for k, (o, n) in enumerate(pieces):
                p_s[at, k * rows : (k + 1) * rows, 0:n] = value[:, o : o + n]

        def kept_weights(at):
            parts = [p_s[at, k * rows : (k + 1) * rows, 0:n] for k, (o, n) in enumerate(pieces)]
            return jnp.concatenate(parts, axis=1)

        def key_rows(i):
            return pl.ds(pl.multiple_of(i * rows, 16), span)

        def allowed(i):
            if text:
                mine = caption(lax.broadcasted_iota(jnp.int32, (rows, 1), 0) + i * rows)
                keys = seg_s[0:1, pl.ds(pl.multiple_of(i * rows_t, 128), span)]
                return mine == keys
            return lax.broadcasted_iota(jnp.int32, (1, span), 1) < keys_i

        def attend(i):
            ok = allowed(i)
            for h in range(HEADS):
                qc, kc, vc, oc = head_at(h)
                scores = dot_nt(qkv_s[q_rows(i), qc], qkv_s[key_rows(i), kc])
                scores = jnp.where(ok, scores, MASKED)
                raised = jnp.exp(scores - jnp.max(scores, axis=-1, keepdims=True))
                weights = raised * (1.0 / jnp.sum(raised, axis=-1, keepdims=True))
                keep_weights(i * HEADS + h, weights)
                mixed = dot(weights.astype(BF16), qkv_s[key_rows(i), vc])
                o_s[at_rows(i), oc] = mixed.astype(BF16)

        def send_a(i):
            send_s[at_rows(i), :] = dot(o_s[at_rows(i), :], wp_s[...]).astype(BF16)
            swap(i, ra_s, K_A).start()

        if text:

            def forward(i):
                @pl.when(i < CHUNKS)
                def _():
                    project(i)

                @pl.when(i == 1)
                def _():
                    wp_own.wait()
                    wp_sib.wait()

                @pl.when(i > 0)
                def _():
                    attend(i - 1)
                    send_a(i - 1)

            loop(CHUNKS + 1, forward)
        else:

            def forward(i):
                project(i)
                attend(i)

                @pl.when(i == 0)
                def _():
                    wp_own.wait()
                    wp_sib.wait()

                send_a(i)

            loop(CHUNKS, forward)
        wu_own.wait()
        wu_sib.wait()
        wd_own.wait()
        wd_sib.wait()

        def y_copies(i):
            at = at_rows(i)
            if text:
                return [remote(ys_s.at[at], yt_s.at[at], K_YT, i, peer)]
            return [remote(ys_s.at[at], y1_s.at[at], K_Y1, i, across)]

        def owned(i):
            return lax.rem(i, 2) == t // 2

        def y_side(i):
            at = pl.ds(pl.multiple_of(i * rows_i, 16), rows_i)
            there = y1_s if text and i < TURNS else y2_s
            return remote((y1_s if text else ys_s).at[at], there.at[at], K_Y2, i, peer)

        def y_share(i):
            @pl.when(jnp.logical_not(owned(i)))
            def _():
                y_side(i).start()

        def y_sum(i):
            @pl.when(owned(i))
            def _():
                y_side(i).wait_recv()
                at = at_rows(i)
                ys_s[at, :] = (ys_s[at, :].astype(F32) + y2_s[at, :].astype(F32)).astype(BF16)
                y_copies(i)[0].start()

        def hand_on(i):
            def go():
                at = pl.ds(pl.multiple_of(i * rows_i, 16), rows_i)
                remote(y1_s.at[at], y1_s.at[at], K_Y1, i, across).wait_recv()
                y_side(i).start()

            if i < TURNS:
                pl.when(owned(i))(go)
            else:
                go()

        def middle(i):
            if not text:
                wait_input(i)
            swap(i, ra_s, K_A).wait()

            def second_norm(at):
                r = x_s[at, :].astype(F32) + (send_s[at, :].astype(F32) + ra_s[at, :].astype(F32)) + outb[0:1, :]
                r_s[at, :] = r
                unit, _ = unit_of(r)
                a2_s[at, :] = (unit * own_gain[1] + own_shift[1]).astype(BF16)
                acc_s[5] += fold(dy_s[at, :].astype(F32))

            by_strips(i, second_norm)
            left = a2_s[at_rows(i), :]
            grad = dy_s[at_rows(i), :]
            for n in range(2 * width // TILE):
                cols = slice(n * TILE, (n + 1) * TILE)
                s, inner = (n * TILE) // width, (n * TILE) % width
                u = dot(left, wu_s[:, cols]) + small_s[s, 0:1, inner : inner + TILE]
                g, slope = gelu_pair(u)
                gb_s[at_rows(i), cols] = g.astype(BF16)
                du = (dot_nt(grad, wd_s[cols, :]) * slope).astype(BF16)
                du_s[at_rows(i), cols] = du
                acc_s[6 + s, :, inner : inner + TILE] += fold(du.astype(F32))
            send_s[at_rows(i), :] = dot_nt(du_s[at_rows(i), :], wu_s[...]).astype(BF16)
            swap(i, rb_s, K_B).start()
            lower = dot(gb_s[at_rows(i), :], wd_s[...])
            ys_s[at_rows(i), :] = (lower + 0.5 * (r_s[at_rows(i), :] + outb[1:2, :])).astype(BF16)
            if not text:

                @pl.when(i >= TURNS)
                def _():
                    y_copies(i)[0].start()
        parts = (slice(0, total // 2), slice(0 if text else total // 2, total))

        def halves(left, right, part):
            def product(at):
                value = dot_tn(left[part, at], right[part, :])
                return value[:, :width], value[:, width:]

            return product

        def middle_and_grads(i):
            middle(i)
            if text:
                return

            @pl.when(i == 1)
            def _():
                grads_part(2, halves(dy_s, gb_s, parts[0]), True, False)

            @pl.when(i == 2)
            def _():
                grads_part(1, halves(a2_s, du_s, parts[0]), True, False)

        loop(CHUNKS, middle_and_grads)
        if text:
            loop(EARLY, lambda i: y_copies(i)[0].start())
        grads_part(2, halves(dy_s, gb_s, parts[1]), text, True)
        grads_part(1, halves(a2_s, du_s, parts[1]), text, True)
        grads_sum(2)
        z_start(2)
        grads_sum(1)
        z_start(1)
        if z_inside:
            z_near(2, upper).start()

        dq_s, drb_s = gb_s, a2_s
        for s in range(2):
            dq_s[0:total, s * QKV + 3 * WIDE : (s + 1) * QKV] = jnp.zeros((total, QKV - 3 * WIDE), BF16)

        def attend_back(i):
            swap(i, rb_s, K_B).wait()

            def back_norm(at):
                grad = send_s[at, :].astype(F32) + rb_s[at, :].astype(F32)
                unit, inverse = unit_of(r_s[at, :])
                dr = dy_s[at, :].astype(F32) + norm_back(grad, unit, inverse, own_gain[1])
                r_s[at, :] = dr
                drb_s[at, :] = dr.astype(BF16)
                acc_s[1] += fold(grad * unit)
                acc_s[3] += fold(grad)
                acc_s[4] += fold(dr)

            by_strips(i, back_norm)
            do_s[0:rows, :] = dot_nt(drb_s[at_rows(i), :], wp_s[...]).astype(BF16)
            for h in range(HEADS):
                qc, kc, vc, oc = head_at(h)
                weights = kept_weights(i * HEADS + h)
                grad_o = do_s[0:rows, oc]
                keys = qkv_s[key_rows(i), kc]
                slope = dot_nt(grad_o, qkv_s[key_rows(i), vc])
                ds = (weights * (slope - jnp.sum(slope * weights, axis=-1, keepdims=True))).astype(BF16)
                dq = dot(ds, keys).astype(BF16) * (HEAD**-0.5)
                dk = dot_tn(ds, qkv_s[q_rows(i), qc])
                dv = dot_tn(weights.astype(BF16), grad_o)
                dq_s[at_rows(i), qc] = dq.astype(BF16)
                if text:
                    hc = slice(h * HEAD, (h + 1) * HEAD)
                    hv = slice((HEADS + h) * HEAD, (HEADS + h + 1) * HEAD)
                    dkv_s[key_rows(i), hc] += dk
                    dkv_s[key_rows(i), hv] += dv
                else:
                    dq_s[at_rows(i), kc] = dk.astype(BF16)
                    dq_s[at_rows(i), vc] = dv.astype(BF16)

        def send_c(i):
            if text:
                for s in range(2):
                    k0 = s * QKV + WIDE
                    dq_s[at_rows(i), k0 : k0 + WIDE] = dkv_s[q_rows(i), s * WIDE : (s + 1) * WIDE].astype(BF16)
                    v0 = 2 * WIDE + s * WIDE
                    dq_s[at_rows(i), k0 + WIDE : k0 + 2 * WIDE] = dkv_s[q_rows(i), v0 : v0 + WIDE].astype(BF16)
            grad = dq_s[at_rows(i), 0 : 2 * QKV]
            send_s[at_rows(i), :] = dot(grad, wq_s[...]).astype(BF16)
            swap(i, rc_s, K_C).start()
            for s in range(2):
                acc_s[8 + s, :, 0:QKV] += fold(grad[:, s * QKV : (s + 1) * QKV].astype(F32))

        def own_img(i):
            return img_out.at[pl.ds(pl.multiple_of(core * n_img + i * rows_i, 16), rows_i)]

        def own_txt(i):
            return txt_out.at[pl.ds(pl.multiple_of(core * n_txt + i * rows_t, 16), rows_t)]

        def img_copies(i):
            src = (y1_s if text else fin_s).at[pl.ds(pl.multiple_of(i * rows_i, 16), rows_i)]
            return local(src, own_img(i), 8 + i), remote(src, own_img(i), K_OI, i, sib)

        def txt_copies(i):
            src = ys_s.at[pl.ds(pl.multiple_of(i * rows_t, 16), rows_t)]
            return local(src, own_txt(i), 12 + i), remote(src, own_txt(i), K_OT, i, sib)

        def dx_copies(i):
            src = rb_s.at[pl.ds(pl.multiple_of(i * rows_t, 16), rows_t)]
            return remote(src, yt_s.at[pl.ds(pl.multiple_of(i * rows_t, 16), rows_t)], K_T1, i, across)

        def dx_relay(i):
            src = yt_s.at[pl.ds(pl.multiple_of(i * rows_t, 16), rows_t)]
            return local(src, own_txt(i), 12 + i), remote(src, own_txt(i), K_OT, i, sib)

        def dx_hand_on(i):
            dx_copies(i).wait_recv()
            for cp in dx_relay(i):
                cp.start()

        if text:

            def own_y(i):
                y_copies(i)[0].wait()
                at = at_rows(i)
                ys_s[at, :] = (ys_s[at, :].astype(F32) + yt_s[at, :].astype(F32)).astype(BF16)
                for cp in txt_copies(i):
                    cp.start()

            def image_y(i):
                at = pl.ds(pl.multiple_of(i * rows_i, 16), rows_i)
                if i < TURNS:

                    @pl.when(owned(i))
                    def _():
                        y_side(i).wait_send()

                    @pl.when(jnp.logical_not(owned(i)))
                    def _():
                        y_side(i).wait_recv()

                else:
                    y_side(i).wait()
                    y1_s[at, :] = (y1_s[at, :].astype(F32) + y2_s[at, :].astype(F32)).astype(BF16)
                for cp in img_copies(i):
                    cp.start()

        def last(i):
            swap(i, rc_s, K_C).wait()

            def body(at):
                grad = send_s[at, :].astype(F32) + rc_s[at, :].astype(F32)
                unit, inverse = unit_of(x_s[at, :].astype(F32))
                dx = (r_s[at, :] + norm_back(grad, unit, inverse, own_gain[0])).astype(BF16)
                if text:
                    rb_s[at, :] = dx
                else:
                    fin_s[at, :] = dx
                acc_s[0] += fold(grad * unit)
                acc_s[2] += fold(grad)

            by_strips(i, body)

            for cp in [dx_copies(i)] if text else img_copies(i):
                cp.start()

        if not text:
            for i in range(TURNS):
                y_share(i)
        def mixed_grads(part):
            def product(at):
                first = dot_tn(a1_s[part, at], dq_s[part, 0 : 2 * QKV])
                second = dot_tn(drb_s[part, at], o_s[part, :])

                def joined(s):
                    left, right = first[:, s * QKV : (s + 1) * QKV], second[:, s * MIX : (s + 1) * MIX]
                    seam = left[:, MIX * 2 :] + right[:, 0 : QKV - 2 * MIX]
                    return jnp.concatenate([left[:, : MIX * 2], seam, right[:, QKV - 2 * MIX :]], axis=1)

                return joined(0), joined(1)

            return product

        group = d if z_inside else 0

        def early_copy(k):
            return remote(early_s.at[0], eall_s.at[group], K_E, k - 1, adder(k, 0))

        def early_arrival(k):
            place = lax.rem(d + dp_size - k, dp_size)
            return remote(eall_s.at[place], eall_s.at[place], K_E, k - 1, adder(k, 0, True))

        early_sib = remote(early_s.at[1], esib_s, K_S, 1, sib)

        def early_start():
            sums = jnp.sum(acc_s[...], axis=1)
            for j, order in enumerate(((1, 3, 4, 5, 6, 7, 8, 9), (1, 3, 4, 5, 7, 6, 9, 8))):
                for row, src in enumerate(order):
                    early_s[j, row : row + 1, :] = sums[src : src + 1, :]
            early_sib.start()

        def early_next():
            early_sib.wait()
            early_s[0] = early_s[0] + esib_s[...]
            eall_s[group] = early_s[0]
            for k in range(1, groups):
                early_copy(k).start()

        def late_copy(k, j):
            return remote(late_s, lall_s.at[2 * group + core], K_V, 2 * k + j, adder(k, j))

        def late_arrival(k, j):
            place = 2 * (lax.rem(d + dp_size - k, dp_size) if k else group) + (1 - core if j else core)
            return remote(lall_s.at[place], lall_s.at[place], K_V, 2 * k + j, adder(k, j, True))

        def late_start():
            late_s[...] = jnp.zeros_like(late_s)
            for r, src in enumerate((0, 2)):
                row = jnp.sum(acc_s[src], axis=0, keepdims=True)
                for c in range(width // 128):
                    late_s[8 * r + c : 8 * r + c + 1, :] = row[:, c * 128 : (c + 1) * 128]
            for k, j in adders:
                late_copy(k, j).start()
            lall_s[2 * group + core] = late_s[...]

        def vectors_finish():
            for k in range(1, groups):
                early_copy(k).wait_send()
                early_arrival(k).wait_recv()
            for k, j in adders:
                late_copy(k, j).wait_send()
                late_arrival(k, j).wait_recv()
            early, late = eall_s[0], lall_s[0]
            for k in range(1, groups):
                early = early + eall_s[k]
            for k in range(1, 2 * groups):
                late = late + lall_s[k]
            vec_out[...] = jnp.zeros_like(vec_out)
            for row, dst in enumerate((1, 3, 4, 5, 6, 7, 8, 9)):
                vec_out[dst : dst + 1, :] = early[row : row + 1, :]
            for r, dst in enumerate((0, 2)):
                for c in range(width // 128):
                    vec_out[dst : dst + 1, c * 128 : (c + 1) * 128] = late[8 * r + c : 8 * r + c + 1, :]

        if text:

            def backward(i):
                @pl.when(i < CHUNKS)
                def _():
                    attend_back(i)

                @pl.when(i == 2)
                def _():
                    z_middle(2)

                @pl.when(i == 3)
                def _():
                    z_middle(1)

                @pl.when(i > 0)
                def _():
                    send_c(i - 1)

                @pl.when(i > 2)
                def _():
                    last(i - 3)

            loop(CHUNKS + 1, backward)
        else:

            def backward(i):
                @pl.when(i == 2)
                def _():
                    z_middle(2)

                @pl.when(i == 3)
                def _():
                    z_middle(1)

                attend_back(i)
                send_c(i)

                @pl.when(i == 2)
                def _():
                    grads_part(0, mixed_grads(parts[0]), True, False)

            loop(CHUNKS, backward)


        if text:
            for i in range(TURNS, CHUNKS):
                hand_on(i)
            for i in range(EARLY, CHUNKS):
                y_copies(i)[0].start()
        grads_part(0, mixed_grads(parts[1]), text, True)
        grads_sum(0)
        z_start(0)
        if z_inside:
            z_near(1, upper).start()
            z_near(0, upper).start()
        early_start()
        if text:
            last(CHUNKS - 2)
            last(CHUNKS - 1)
            early_next()
            z_middle(0)
            for i in range(TURNS):
                hand_on(i)
        else:
            for i in range(TURNS):
                y_sum(i)
            loop(2, last)
            early_next()
            z_middle(0)
            last(CHUNKS - 2)
            loop(CHUNKS, dx_hand_on)
            last(CHUNKS - 1)

        late_start()
        if text:
            loop(CHUNKS, own_y)
        z_finish(2)
        z_finish(1)
        if text:
            for i in range(CHUNKS):
                image_y(i)
        z_finish(0)
        vectors_finish()

        def finish(i):
            if text:
                dy_to_image(i).wait_send()
                dx_copies(i).wait_send()
                here, there = txt_copies(i)
                here.wait()
                there.wait()
            else:
                x_to_text(i).wait_send()
                if i < TURNS:

                    @pl.when(owned(i))
                    def _():
                        y_copies(i)[0].wait_send()

                    @pl.when(jnp.logical_not(owned(i)))
                    def _():
                        y_side(i).wait_send()

                else:
                    y_copies(i)[0].wait_send()
                for cp in dx_relay(i):
                    cp.wait()
            here, there = img_copies(i)
            here.wait()
            there.wait()

        for i in range(CHUNKS):
            finish(i)
        for a in range(3):
            z_end(a)

    @pl.when(image_here)
    def _():
        one_layer(False)

    @pl.when(jnp.logical_not(image_here))
    def _():
        one_layer(True)


def finish_kernel(
    images, keys_i, rows_i, img_in, txt_in, g_x, g_u, g_d, vec,
    img_out, txt_out, gains, shifts, qkv, bias_qv, proj, outb, up, bias_up, down,
    buf, out_s, gx_s, qkv_s, txt_s, gu_s, gd_s, sem,
):
    plain = [(g_u, gu_s, up), (g_d, gd_s, down), (txt_in, txt_s, txt_out)]
    fetch = [pltpu.make_async_copy(src, mid, sem.at[k]) for k, (src, mid, dst) in enumerate(plain)]
    copies = [pltpu.make_async_copy(mid, dst, sem.at[5 + k]) for k, (src, mid, dst) in enumerate(plain)]
    gx_in = pltpu.make_async_copy(g_x, gx_s, sem.at[3])
    gx_in.start()
    blocks = [(o, min(STEP, rows_i - o)) for o in range(0, rows_i, STEP)]
    loads = [
        pltpu.make_async_copy(img_in.at[:, o : o + n], buf.at[:, o : o + n], sem.at[8 + k])
        for k, (o, n) in enumerate(blocks)
    ]
    for cp in loads:
        cp.start()
    for cp in fetch:
        cp.start()
    gains[...] = vec[0:2, :]
    shifts[...] = vec[2:4, :]
    outb[...] = vec[4:6, :]
    bias_up[...] = vec[6:7, :]
    bias_qv[0:1, :] = vec[8:9, 0:WIDE]
    bias_qv[1:2, :] = vec[8:9, 2 * WIDE : 3 * WIDE]
    gx_in.wait()
    proj[...] = gx_s[:, 3 * WIDE :].T
    for k in range(3):
        qkv_s[k] = gx_s[:, k * WIDE : (k + 1) * WIDE]
    q_out = pltpu.make_async_copy(qkv_s, qkv, sem.at[4])
    q_out.start()
    stores = []
    for k, (o, n) in enumerate(blocks):
        loads[k].wait()
        rows = min(n, keys_i - o)
        value = jnp.swapaxes(buf[:, o : o + n, :].astype(F32), 0, 1)
        out_s[o : o + n] = value.astype(BF16)
        cp = pltpu.make_async_copy(out_s.at[o : o + rows], img_out.at[o : o + rows], sem.at[16 + k])
        cp.start()
        stores.append(cp)
        if k < len(fetch):
            fetch[k].wait()
            copies[k].start()
    for cp in copies + [q_out] + stores:
        cp.wait()


def finish_outputs(images, keys_i, rows_i, img_out, txt_out, g_x, g_u, g_d, vec):
    share, width = g_x.shape
    sds, v = jax.ShapeDtypeStruct, pltpu.VMEM
    any_spec, vmem_spec = pl.BlockSpec(memory_space=pl.ANY), pl.BlockSpec(memory_space=pltpu.VMEM)
    outs = [
        (sds((keys_i, images, width), BF16), any_spec),
        (sds(txt_out.shape, BF16), any_spec),
        (sds((2, width), F32), vmem_spec),
        (sds((2, width), F32), vmem_spec),
        (sds((3, share, WIDE), F32), any_spec),
        (sds((2, WIDE), F32), vmem_spec),
        (sds((WIDE, share), F32), vmem_spec),
        (sds((2, width), F32), vmem_spec),
        (sds((share, width), F32), any_spec),
        (sds((1, width), F32), vmem_spec),
        (sds((share, width), F32), any_spec),
    ]
    img, txt, gains, shifts, qkv, bias_qv, proj, outb, up, bias_up, down = pl.pallas_call(
        partial(finish_kernel, images, keys_i, rows_i),
        out_shape=[o[0] for o in outs],
        in_specs=[any_spec] * 5 + [vmem_spec],
        out_specs=[o[1] for o in outs],
        scratch_shapes=[
            v((images, rows_i, width), BF16), v((rows_i, images, width), BF16), v((share, width), F32),
            v((3, share, WIDE), F32), v(txt_out.shape, BF16), v((share, width), F32), v((share, width), F32),
            pltpu.SemaphoreType.DMA((24,)),
        ],
        compiler_params=pltpu.CompilerParams(vmem_limit_bytes=60 << 20),
    )(img_out.reshape(images, rows_i, width), txt_out, g_x, g_u, g_d, vec)
    return (
        jnp.transpose(img, (1, 0, 2))[None], txt.reshape(2, -1, width)[None], gains[None], shifts[None],
        jnp.transpose(qkv, (1, 0, 2))[None], bias_qv[None], proj[None], outb[None], up[None], bias_up, down.T[None],
    )


def per_device(
    image_side, text_side, caption_lengths, norm_gains, norm_shifts, w_qkv, bias_qv, w_proj, out_bias, w_up, bias_up, w_down,
):
    dp_size = lax.axis_size("dp")
    core = lax.rem(lax.axis_index("tensor"), 2)
    images, keys_i, width = image_side.shape[1:]
    blocks, length = text_side.shape[1:3]
    per_core = images // 2
    rows_i = -(-(per_core // CHUNKS * keys_i) // 16) * 16
    rows_t = length * (blocks // 2) // CHUNKS
    share = width // dp_size
    z_inside = dp_size == 4 and share % 16 == 0

    img = lax.dynamic_slice_in_dim(image_side[0], core * per_core, per_core, 0)
    img = jnp.pad(img, ((0, 0), (0, rows_i - keys_i), (0, 0))).reshape(per_core * rows_i, width)
    wq = jnp.transpose(w_qkv[0], (1, 2, 0)).reshape(3 * WIDE, width)
    n_i, n_t = rows_i * CHUNKS, rows_t * CHUNKS
    columns = (width, width, width)
    sds = jax.ShapeDtypeStruct
    grad_type = (lambda w: sds((share, w), F32)) if z_inside else (lambda w: sds((width, w), BF16))
    outs = [sds((2 * n_i, width), BF16), sds((2 * n_t, width), BF16)]
    outs += [grad_type(w) for w in columns] + [sds((16, width), F32)]
    any_spec, vmem_spec = pl.BlockSpec(memory_space=pl.ANY), pl.BlockSpec(memory_space=pltpu.VMEM)
    v = pltpu.VMEM
    scratch = [
        v((n_i, width), BF16), v((n_i, width), BF16),
        v((2 * QKV, width), BF16), v((2 * MIX, width), BF16), v((width, 2 * width), BF16), v((2 * width, width), BF16),
        v((2, 8, width + QKV), F32), v((8, n_t + 2 * rows_t), jnp.int32),
        v((n_i, width), BF16), v((max(n_i, n_t + 2 * rows_t), 2 * QKV), BF16), v((n_i, 2 * MIX), BF16), v((n_i, width), F32),
        v((n_i, width), BF16), v((n_i, 2 * width), BF16), v((n_i, 2 * width), BF16),
        v((CHUNKS * HEADS, max(-(-rows_i // 128) * rows_i, 3 * rows_t // 128 * rows_t), 128), F32),
        v((n_t + 2 * rows_t, 2 * HEADS * HEAD), F32), v((max(rows_i, rows_t), 2 * MIX), BF16),
        v((n_i, width), BF16), v((n_i, width), BF16), v((n_i, width), BF16), v((n_i, width), BF16),
        v((n_i, width), BF16), v((n_t, width), BF16), v((n_i, width), BF16), v((n_i, width), BF16), v((n_i, width), BF16),
        v((16, 8, width), F32), v((2, 8, width), F32), v((8, width), F32), v((dp_size if z_inside else 1, 8, width), F32),
        v((16, 128), F32), v((2 * dp_size if z_inside else 2, 16, 128), F32),
    ]
    scratch += [v((2, width, width), BF16)]
    scratch += [v((width, w), BF16) for w in columns] + [v((width, w), BF16) for w in columns]
    if z_inside:
        scratch += [v((3, 2, share, width), BF16), v((3, share, width), BF16), v((3, share, width), F32)]
    dma = pltpu.SemaphoreType.DMA
    scratch += [dma((4 * N_KINDS,)), dma((4 * N_KINDS,)), dma((24,))]
    img_out, txt_out, g_x, g_u, g_d, vec = pl.pallas_call(
        partial(layers_kernel, rows_i, rows_t, keys_i, dp_size, z_inside),
        out_shape=outs,
        in_specs=[any_spec] * 6 + [pl.BlockSpec(memory_space=pltpu.SMEM)] + [vmem_spec] * 5,
        out_specs=[any_spec] * 5 + [vmem_spec],
        scratch_shapes=scratch,
        compiler_params=pltpu.CompilerParams(collective_id=0, has_side_effects=True, vmem_limit_bytes=60 << 20),
    )(
        img, text_side[0], wq, w_proj[0], w_up[0], w_down[0], caption_lengths,
        norm_gains[0], norm_shifts[0], out_bias[0], bias_up, bias_qv[0],
    )
    if z_inside:
        return finish_outputs(images, keys_i, rows_i, img_out, txt_out, g_x, g_u, g_d, vec)
    else:
        def scatter(grad):
            return lax.psum_scatter(grad, "dp", scatter_dimension=0, tiled=True).astype(F32)

        g_x, g_u, g_d = (scatter(g) for g in (g_x, g_u, g_d))
        vec = lax.psum(vec, "dp")
    image_result = img_out.reshape(images, rows_i, width)[:, :keys_i][None]
    text_result = txt_out.reshape(blocks, length, width)[None]
    return (
        image_result,
        text_result,
        vec[0:2][None],
        vec[2:4][None],
        g_x[:, : 3 * WIDE].reshape(share, 3, WIDE)[None],
        jnp.stack([vec[8, 0:WIDE], vec[8, 2 * WIDE : 3 * WIDE]])[None],
        g_x[:, 3 * WIDE :].T[None],
        vec[4:6][None],
        g_u[None],
        vec[6][None],
        g_d.T[None],
    )


def solution(mesh):
    placed = (
        P("pipe", "dp", None, None),
        P("pipe", "dp", None, None),
        P("dp", None),
        P("pipe", None, None),
        P("pipe", None, None),
        P("pipe", None, None, "tensor"),
        P("pipe", None, "tensor"),
        P("pipe", "tensor", None),
        P("pipe", None, None),
        P("pipe", None, "tensor"),
        P("pipe", "tensor"),
        P("pipe", "tensor", None),
    )
    return jax.shard_map(
        per_device,
        mesh=mesh,
        in_specs=placed,
        out_specs=(
            P("pipe", "dp", None, None),
            P("pipe", "dp", None, None),
            P("pipe", None, None),
            P("pipe", None, None),
            P("pipe", "dp", None, "tensor"),
            P("pipe", None, "tensor"),
            P("pipe", "tensor", "dp"),
            P("pipe", None, None),
            P("pipe", "dp", "tensor"),
            P("pipe", "tensor"),
            P("pipe", "tensor", "dp"),
        ),
        check_vma=False,
    )
```

```python
from functools import partial

import jax
import jax.numpy as jnp
from jax import lax
from jax.experimental import pallas as pl
from jax.experimental.pallas import tpu as pltpu
from jax.sharding import PartitionSpec as P

F32 = jnp.float32
BF16 = jnp.bfloat16
BY_MESH = pl.DeviceIdType.MESH
HEAD = 64
HALF = 3
HEADS = 2 * HALF
WIDE = HALF * HEAD
EPSILON = 1e-06
MASKED = -1000000000.0
CHUNKS = 4
STRIP = 16
TURNS = 2
EARLY = 2
G_TILE = 256
STEP = 64
BLOCK = 208
QKV = 640
MIX = 256
PAD = MIX - WIDE
TILE = 256

K_IN, K_A, K_B, K_C, K_Y1, K_Y2, K_YT, K_OI, K_OT, K_T1, K_W, K_S, K_G = range(13)
K_Z = K_G + 3
K_V = K_Z + 3
K_E = K_V + 2
N_KINDS = K_E + 1


def dot(a, b):
    return lax.dot_general(a, b, (((1,), (0,)), ((), ())), preferred_element_type=F32)


def dot_nt(a, b):
    return lax.dot_general(a, b, (((1,), (1,)), ((), ())), preferred_element_type=F32)


def dot_tn(a, b):
    return lax.dot_general(a, b, (((0,), (0,)), ((), ())), preferred_element_type=F32)


def loop(count, body):
    def step(j, carry):
        body(j)
        return carry

    lax.fori_loop(0, count, step, 0)


def unit_of(rows):
    centre = rows - jnp.mean(rows, axis=-1, keepdims=True)
    inverse = lax.rsqrt(jnp.mean(centre * centre, axis=-1, keepdims=True) + EPSILON)
    return centre * inverse, inverse


def norm_back(grad, unit, inverse, gain):
    scaled = grad * gain
    first = jnp.mean(scaled, axis=-1, keepdims=True)
    second = jnp.mean(scaled * unit, axis=-1, keepdims=True)
    return inverse * (scaled - first - unit * second)


def gelu_pair(u):
    cdf = 0.5 * (1.0 + lax.erf(u * (0.5**0.5)))
    pdf = jnp.exp(u * u * -0.5) * 0.3989422804014327
    return u * cdf, cdf + u * pdf


def fold(rows):
    return jnp.sum(rows.reshape(rows.shape[0] // 8, 8, rows.shape[1]), axis=0)


def layers_kernel(
    rows_i, rows_t, keys_i, dp_size, z_inside,
    img_own, txt_all, w_qkv, w_proj, w_up, w_down, lengths, gains, shifts, outb, bias_up, bias_qv,
    img_out, txt_out, g_mix, g_up, g_down, vec_out,
    x_s, dy_s, wq_s, wp_s, wu_s, wd_s, small_s, seg_s, a1_s, qkv_s, o_s, r_s, a2_s, gb_s, du_s, p_s, dkv_s, do_s,
    send_s, ra_s, rb_s, rc_s, ys_s, yt_s, y1_s, y2_s, fin_s, acc_s, early_s, esib_s, eall_s, late_s, lall_s,
    half_s, gs_x, gs_u, gs_d, gr_x, gr_u, gr_d, *rest,
):
    if z_inside:
        z1_s, z2_s, zf_s, ssem, rsem, lsem = rest
    else:
        ssem, rsem, lsem = rest
    width = x_s.shape[1]
    p, d, t = lax.axis_index("pipe"), lax.axis_index("dp"), lax.axis_index("tensor")
    core = lax.rem(t, 2)
    sib_t = t + 1 - 2 * core
    peer_t = lax.rem(t + 2, 4)
    other = 1 - p
    sib, peer = (p, d, sib_t), (p, d, peer_t)
    across = (other, d, t)
    txt_own = txt_all.at[core]
    groups = dp_size if z_inside else 1
    adders = [(k, j) for k in range(groups) for j in range(2) if k + j > 0]

    def adder(k, j, back=False):
        dist = dp_size - k if back else k
        return (p, lax.rem(d + dist, dp_size) if k else d, sib_t if j else t)

    partners = [peer, across] + [adder(k, j) for k, j in adders]

    def remote(src, dst, kind, slot, to):
        at = kind * 4 + slot
        return pltpu.make_async_remote_copy(
            src_ref=src, dst_ref=dst, send_sem=ssem.at[at], recv_sem=rsem.at[at],
            device_id=to, device_id_type=BY_MESH,
        )

    def local(src, dst, slot):
        return pltpu.make_async_copy(src, dst, lsem.at[slot])

    image_here = p == 0
    n_img = rows_i * CHUNKS
    n_txt = rows_t * CHUNKS

    wq_own = local(w_qkv, wq_s.at[0 : 3 * WIDE], 0)
    wp_own = local(w_proj, wp_s.at[PAD:MIX], 1)
    wu_own = local(w_up, wu_s.at[:, 0:width], 2)
    wd_own = local(w_down, wd_s.at[0:width], 3)
    img_in = local(img_own, x_s, 5)
    txt_in = local(txt_own, dy_s.at[0:n_txt], 6)
    wq_own.start()

    @pl.when(image_here)
    def _():
        img_in.start()

    @pl.when(jnp.logical_not(image_here))
    def _():
        txt_in.start()

    wp_own.start()
    wu_own.start()
    wd_own.start()
    zero_rows = jnp.zeros((PAD, width), BF16)
    wp_s[0:PAD, :] = zero_rows
    wp_s[MIX : MIX + PAD, :] = zero_rows
    zero_rows = jnp.zeros((QKV - 3 * WIDE, width), BF16)
    wq_s[3 * WIDE : QKV, :] = zero_rows
    wq_s[QKV + 3 * WIDE :, :] = zero_rows
    acc_s[...] = jnp.zeros_like(acc_s)
    small_s[0] = jnp.zeros_like(small_s[0])
    small_s[0, 0:1, 0:width] = bias_up[...]
    small_s[0, 0:1, width : width + WIDE] = bias_qv[0:1, :]
    small_s[0, 0:1, width + 2 * WIDE : width + 3 * WIDE] = bias_qv[1:2, :]

    barrier = pltpu.get_barrier_semaphore()
    for to in partners:
        pl.semaphore_signal(barrier, inc=1, device_id=to, device_id_type=BY_MESH)

    @pl.when(image_here)
    def _():
        img_in.wait()

        def first_norm(i):
            at = pl.ds(pl.multiple_of(i * rows_i, 16), rows_i)
            unit, _ = unit_of(x_s[at, :].astype(F32))
            a1_s[at, :] = (unit * gains[0:1, :] + shifts[0:1, :]).astype(BF16)

        first_norm(0)

    pl.semaphore_wait(barrier, len(partners))

    sm_sib = remote(small_s.at[0], small_s.at[1], K_S, 0, sib)
    wq_sib = remote(w_qkv, wq_s.at[QKV : QKV + 3 * WIDE], K_W, 0, sib)
    wp_sib = remote(w_proj, wp_s.at[MIX + PAD :], K_W, 1, sib)
    wu_sib = remote(w_up, wu_s.at[:, width:], K_W, 2, sib)
    wd_sib = remote(w_down, wd_s.at[width:], K_W, 3, sib)

    def x_to_text(i):
        rows = pl.ds(pl.multiple_of(i * rows_t, 16), rows_t)
        return remote(txt_own.at[rows], x_s.at[rows], K_IN, i, across)

    def dy_to_image(i):
        rows = pl.ds(pl.multiple_of(i * rows_i, 16), rows_i)
        return remote(img_own.at[rows], dy_s.at[rows], K_IN, i, across)

    @pl.when(image_here)
    def _():
        loop(CHUNKS, lambda i: x_to_text(i).start())

    sm_sib.start()
    wq_sib.start()

    @pl.when(jnp.logical_not(image_here))
    def _():
        loop(CHUNKS, lambda i: dy_to_image(i).start())

    wp_sib.start()
    wu_sib.start()
    wd_sib.start()

    own_gain = [gains[0:1, :], gains[1:2, :]]
    own_shift = [shifts[0:1, :], shifts[1:2, :]]

    g_arrays = [(gs_x, gr_x, g_mix), (gs_u, gr_u, g_up), (gs_d, gr_d, g_down)]

    def g_exchange(a, m):
        at = pl.ds(pl.multiple_of(m * G_TILE, G_TILE), G_TILE)
        return remote(half_s.at[a % 2, at], g_arrays[a][1].at[at], K_G + m, a, sib)

    def grads_part(a, product, first, final):
        mine, theirs = g_arrays[a][0], half_s.at[a % 2]

        def both(m):
            at = pl.ds(pl.multiple_of(m * G_TILE, G_TILE), G_TILE)
            for ref, value in zip((mine, theirs), product(at)):
                ref[at, :] = (value if first else value + ref[at, :].astype(F32)).astype(BF16)
            if final:
                g_exchange(a, m).start()

        loop(width // G_TILE, both)

    def grads_sum(a):
        mine, theirs = g_arrays[a][0:2]

        def body(m):
            g_exchange(a, m).wait()
            at = pl.ds(pl.multiple_of(m * G_TILE, G_TILE), G_TILE)
            mine[at, :] = (mine[at, :].astype(F32) + theirs[at, :].astype(F32)).astype(BF16)

        loop(width // G_TILE, body)

    share = width // dp_size
    parity = lax.rem(d, 2)
    upper = d // 2
    near = d + 1 - 2 * parity
    far = d + 2 - 4 * upper if z_inside else d

    def share_rows(at):
        return pl.ds(pl.multiple_of(at * share, 16), share)

    def z_near(a, k):
        src = g_arrays[a][0].at[share_rows(1 - parity + 2 * k)]
        return remote(src, z1_s.at[a, k], K_Z, 3 * k + a, (p, near, t))

    def z_far(a):
        return remote(g_arrays[a][0].at[share_rows(far)], z2_s.at[a], K_Z, 6 + a, (p, far, t))

    def z_start(a):
        if z_inside:
            z_near(a, 1 - upper).start()
        else:
            local(g_arrays[a][0], g_arrays[a][2], 20 + a).start()

    def z_middle(a):
        if z_inside:
            z_near(a, 1 - upper).wait()
            mine = g_arrays[a][0]
            rows = share_rows(far)
            mine[rows, :] = (mine[rows, :].astype(F32) + z1_s[a, 1 - upper].astype(F32)).astype(BF16)
            z_far(a).start()

    def z_finish(a):
        if z_inside:
            z_near(a, upper).wait()
            z_far(a).wait()
            total = g_arrays[a][0][share_rows(d), :].astype(F32) + z1_s[a, upper].astype(F32)
            zf_s[a] = total + z2_s[a].astype(F32)
            local(zf_s.at[a], g_arrays[a][2], 20 + a).start()

    def z_end(a):
        if z_inside:
            local(zf_s.at[a], g_arrays[a][2], 20 + a).wait()
        else:
            local(g_arrays[a][0], g_arrays[a][2], 20 + a).wait()

    def one_layer(text):
        rows = rows_t if text else rows_i
        total = rows * CHUNKS
        cuts = [(o, min(BLOCK, rows - o)) for o in range(0, rows, BLOCK)]
        q_off = rows_t if text else 0

        def at_rows(i):
            return pl.ds(pl.multiple_of(i * rows, 16), rows)

        def q_rows(i):
            return pl.ds(pl.multiple_of(i * rows + q_off, 16), rows)

        def by_strips(i, body):
            for o, size in cuts:
                body(pl.ds(pl.multiple_of(i * rows + o, STRIP), size))

        def swap(i, landing, kind):
            return remote(send_s.at[at_rows(i)], landing.at[at_rows(i)], kind, i, peer)

        incoming = dy_to_image if not text else x_to_text

        def wait_input(i):
            cp = remote(x_s.at[at_rows(i)] if text else dy_s.at[at_rows(i)],
                        x_s.at[at_rows(i)] if text else dy_s.at[at_rows(i)], K_IN, i, across)
            cp.wait_recv()

        wq_own.wait()
        wq_sib.wait()
        sm_sib.wait()
        def caption(places):
            bound = lengths[core, 0]
            segment = (places >= bound).astype(jnp.int32)
            for k in range(1, lengths.shape[1]):
                bound = bound + lengths[core, k]
                segment = segment + (places >= bound).astype(jnp.int32)
            return segment

        if text:
            places = lax.broadcasted_iota(jnp.int32, (8, total + 2 * rows_t), 1) - rows_t
            seg_s[...] = jnp.where(places < 0, -1, caption(places))
            txt_in.wait()
            pad = jnp.zeros((rows_t, 2 * QKV), BF16)
            qkv_s[0:rows_t, :] = pad
            qkv_s[rows_t + total : 2 * rows_t + total, :] = pad
            dkv_s[...] = jnp.zeros_like(dkv_s)
        for s in range(2):
            o_s[0:total, s * MIX : s * MIX + PAD] = jnp.zeros((total, PAD), BF16)

        def project(i):
            if text:
                wait_input(i)

            def first_norm(at):
                unit, _ = unit_of(x_s[at, :].astype(F32))
                a1_s[at, :] = (unit * own_gain[0] + own_shift[0]).astype(BF16)

            if text:
                by_strips(i, first_norm)
            else:
                pl.when(i > 0)(lambda: by_strips(i, first_norm))
            left = a1_s[at_rows(i), :]
            lanes = lax.broadcasted_iota(jnp.int32, (1, QKV), 1)
            factor = jnp.where(lanes < WIDE, HEAD**-0.5, 1.0).astype(F32)
            for s in range(2):
                value = dot_nt(left, wq_s[s * QKV : (s + 1) * QKV, :])
                value = (value + small_s[s, 0:1, width : width + QKV]) * factor
                qkv_s[q_rows(i), s * QKV : (s + 1) * QKV] = value.astype(BF16)

        def head_at(h):
            s, hh = h // HALF, h % HALF
            base = s * QKV + hh * HEAD
            return slice(base, base + HEAD), slice(base + WIDE, base + WIDE + HEAD), slice(base + 2 * WIDE, base + 2 * WIDE + HEAD), slice(s * MIX + PAD + hh * HEAD, s * MIX + PAD + hh * HEAD + HEAD)

        span = 3 * rows_t if text else rows_i
        pieces = [(o, min(128, span - o)) for o in range(0, span, 128)]

        def keep_weights(at, value):
            for k, (o, n) in enumerate(pieces):
                p_s[at, k * rows : (k + 1) * rows, 0:n] = value[:, o : o + n]

        def kept_weights(at):
            parts = [p_s[at, k * rows : (k + 1) * rows, 0:n] for k, (o, n) in enumerate(pieces)]
            return jnp.concatenate(parts, axis=1)

        def key_rows(i):
            return pl.ds(pl.multiple_of(i * rows, 16), span)

        def allowed(i):
            if text:
                mine = caption(lax.broadcasted_iota(jnp.int32, (rows, 1), 0) + i * rows)
                keys = seg_s[0:1, pl.ds(pl.multiple_of(i * rows_t, 128), span)]
                return mine == keys
            return lax.broadcasted_iota(jnp.int32, (1, span), 1) < keys_i

        def attend(i):
            ok = allowed(i)
            for h in range(HEADS):
                qc, kc, vc, oc = head_at(h)
                scores = dot_nt(qkv_s[q_rows(i), qc], qkv_s[key_rows(i), kc])
                scores = jnp.where(ok, scores, MASKED)
                raised = jnp.exp(scores - jnp.max(scores, axis=-1, keepdims=True))
                weights = raised * (1.0 / jnp.sum(raised, axis=-1, keepdims=True))
                keep_weights(i * HEADS + h, weights)
                mixed = dot(weights.astype(BF16), qkv_s[key_rows(i), vc])
                o_s[at_rows(i), oc] = mixed.astype(BF16)

        def send_a(i):
            send_s[at_rows(i), :] = dot(o_s[at_rows(i), :], wp_s[...]).astype(BF16)
            swap(i, ra_s, K_A).start()

        if text:

            def forward(i):
                @pl.when(i < CHUNKS)
                def _():
                    project(i)

                @pl.when(i == 1)
                def _():
                    wp_own.wait()
                    wp_sib.wait()

                @pl.when(i > 0)
                def _():
                    attend(i - 1)
                    send_a(i - 1)

            loop(CHUNKS + 1, forward)
        else:

            def forward(i):
                project(i)
                attend(i)

                @pl.when(i == 0)
                def _():
                    wp_own.wait()
                    wp_sib.wait()

                send_a(i)

            loop(CHUNKS, forward)
        wu_own.wait()
        wu_sib.wait()
        wd_own.wait()
        wd_sib.wait()

        def y_copies(i):
            at = at_rows(i)
            if text:
                return [remote(ys_s.at[at], yt_s.at[at], K_YT, i, peer)]
            return [remote(ys_s.at[at], y1_s.at[at], K_Y1, i, across)]

        def owned(i):
            return lax.rem(i, 2) == t // 2

        def y_side(i):
            at = pl.ds(pl.multiple_of(i * rows_i, 16), rows_i)
            there = y1_s if text and i < TURNS else y2_s
            return remote((y1_s if text else ys_s).at[at], there.at[at], K_Y2, i, peer)

        def y_share(i):
            @pl.when(jnp.logical_not(owned(i)))
            def _():
                y_side(i).start()

        def y_sum(i):
            @pl.when(owned(i))
            def _():
                y_side(i).wait_recv()
                at = at_rows(i)
                ys_s[at, :] = (ys_s[at, :].astype(F32) + y2_s[at, :].astype(F32)).astype(BF16)
                y_copies(i)[0].start()

        def hand_on(i):
            def go():
                at = pl.ds(pl.multiple_of(i * rows_i, 16), rows_i)
                remote(y1_s.at[at], y1_s.at[at], K_Y1, i, across).wait_recv()
                y_side(i).start()

            if i < TURNS:
                pl.when(owned(i))(go)
            else:
                go()

        def middle(i):
            if not text:
                wait_input(i)
            swap(i, ra_s, K_A).wait()

            def second_norm(at):
                r = x_s[at, :].astype(F32) + (send_s[at, :].astype(F32) + ra_s[at, :].astype(F32)) + outb[0:1, :]
                r_s[at, :] = r
                unit, _ = unit_of(r)
                a2_s[at, :] = (unit * own_gain[1] + own_shift[1]).astype(BF16)
                acc_s[5] += fold(dy_s[at, :].astype(F32))

            by_strips(i, second_norm)
            left = a2_s[at_rows(i), :]
            grad = dy_s[at_rows(i), :]
            for n in range(2 * width // TILE):
                cols = slice(n * TILE, (n + 1) * TILE)
                s, inner = (n * TILE) // width, (n * TILE) % width
                u = dot(left, wu_s[:, cols]) + small_s[s, 0:1, inner : inner + TILE]
                g, slope = gelu_pair(u)
                gb_s[at_rows(i), cols] = g.astype(BF16)
                du = (dot_nt(grad, wd_s[cols, :]) * slope).astype(BF16)
                du_s[at_rows(i), cols] = du
                acc_s[6 + s, :, inner : inner + TILE] += fold(du.astype(F32))
            send_s[at_rows(i), :] = dot_nt(du_s[at_rows(i), :], wu_s[...]).astype(BF16)
            swap(i, rb_s, K_B).start()
            lower = dot(gb_s[at_rows(i), :], wd_s[...])
            ys_s[at_rows(i), :] = (lower + 0.5 * (r_s[at_rows(i), :] + outb[1:2, :])).astype(BF16)
            if not text:

                @pl.when(i >= TURNS)
                def _():
                    y_copies(i)[0].start()
        parts = (slice(0, total // 2), slice(0 if text else total // 2, total))

        def halves(left, right, part):
            def product(at):
                value = dot_tn(left[part, at], right[part, :])
                return value[:, :width], value[:, width:]

            return product

        def middle_and_grads(i):
            middle(i)
            if text:
                return

            @pl.when(i == 1)
            def _():
                grads_part(2, halves(dy_s, gb_s, parts[0]), True, False)

            @pl.when(i == 2)
            def _():
                grads_part(1, halves(a2_s, du_s, parts[0]), True, False)

        loop(CHUNKS, middle_and_grads)
        if text:
            loop(EARLY, lambda i: y_copies(i)[0].start())
        grads_part(2, halves(dy_s, gb_s, parts[1]), text, True)
        grads_part(1, halves(a2_s, du_s, parts[1]), text, True)
        grads_sum(2)
        z_start(2)
        grads_sum(1)
        z_start(1)
        if z_inside:
            z_near(2, upper).start()

        dq_s, drb_s = gb_s, a2_s
        for s in range(2):
            dq_s[0:total, s * QKV + 3 * WIDE : (s + 1) * QKV] = jnp.zeros((total, QKV - 3 * WIDE), BF16)

        def attend_back(i):
            swap(i, rb_s, K_B).wait()

            def back_norm(at):
                grad = send_s[at, :].astype(F32) + rb_s[at, :].astype(F32)
                unit, inverse = unit_of(r_s[at, :])
                dr = dy_s[at, :].astype(F32) + norm_back(grad, unit, inverse, own_gain[1])
                r_s[at, :] = dr
                drb_s[at, :] = dr.astype(BF16)
                acc_s[1] += fold(grad * unit)
                acc_s[3] += fold(grad)
                acc_s[4] += fold(dr)

            by_strips(i, back_norm)
            do_s[0:rows, :] = dot_nt(drb_s[at_rows(i), :], wp_s[...]).astype(BF16)
            for h in range(HEADS):
                qc, kc, vc, oc = head_at(h)
                weights = kept_weights(i * HEADS + h)
                grad_o = do_s[0:rows, oc]
                keys = qkv_s[key_rows(i), kc]
                slope = dot_nt(grad_o, qkv_s[key_rows(i), vc])
                ds = (weights * (slope - jnp.sum(slope * weights, axis=-1, keepdims=True))).astype(BF16)
                dq = dot(ds, keys).astype(BF16) * (HEAD**-0.5)
                dk = dot_tn(ds, qkv_s[q_rows(i), qc])
                dv = dot_tn(weights.astype(BF16), grad_o)
                dq_s[at_rows(i), qc] = dq.astype(BF16)
                if text:
                    hc = slice(h * HEAD, (h + 1) * HEAD)
                    hv = slice((HEADS + h) * HEAD, (HEADS + h + 1) * HEAD)
                    dkv_s[key_rows(i), hc] += dk
                    dkv_s[key_rows(i), hv] += dv
                else:
                    dq_s[at_rows(i), kc] = dk.astype(BF16)
                    dq_s[at_rows(i), vc] = dv.astype(BF16)

        def send_c(i):
            if text:
                for s in range(2):
                    k0 = s * QKV + WIDE
                    dq_s[at_rows(i), k0 : k0 + WIDE] = dkv_s[q_rows(i), s * WIDE : (s + 1) * WIDE].astype(BF16)
                    v0 = 2 * WIDE + s * WIDE
                    dq_s[at_rows(i), k0 + WIDE : k0 + 2 * WIDE] = dkv_s[q_rows(i), v0 : v0 + WIDE].astype(BF16)
            grad = dq_s[at_rows(i), 0 : 2 * QKV]
            send_s[at_rows(i), :] = dot(grad, wq_s[...]).astype(BF16)
            swap(i, rc_s, K_C).start()
            for s in range(2):
                acc_s[8 + s, :, 0:QKV] += fold(grad[:, s * QKV : (s + 1) * QKV].astype(F32))

        def own_img(i):
            return img_out.at[pl.ds(pl.multiple_of(core * n_img + i * rows_i, 16), rows_i)]

        def own_txt(i):
            return txt_out.at[pl.ds(pl.multiple_of(core * n_txt + i * rows_t, 16), rows_t)]

        def img_copies(i):
            src = (y1_s if text else fin_s).at[pl.ds(pl.multiple_of(i * rows_i, 16), rows_i)]
            return local(src, own_img(i), 8 + i), remote(src, own_img(i), K_OI, i, sib)

        def txt_copies(i):
            src = ys_s.at[pl.ds(pl.multiple_of(i * rows_t, 16), rows_t)]
            return local(src, own_txt(i), 12 + i), remote(src, own_txt(i), K_OT, i, sib)

        def dx_copies(i):
            src = rb_s.at[pl.ds(pl.multiple_of(i * rows_t, 16), rows_t)]
            return remote(src, yt_s.at[pl.ds(pl.multiple_of(i * rows_t, 16), rows_t)], K_T1, i, across)

        def dx_relay(i):
            src = yt_s.at[pl.ds(pl.multiple_of(i * rows_t, 16), rows_t)]
            return local(src, own_txt(i), 12 + i), remote(src, own_txt(i), K_OT, i, sib)

        def dx_hand_on(i):
            dx_copies(i).wait_recv()
            for cp in dx_relay(i):
                cp.start()

        if text:

            def own_y(i):
                y_copies(i)[0].wait()
                at = at_rows(i)
                ys_s[at, :] = (ys_s[at, :].astype(F32) + yt_s[at, :].astype(F32)).astype(BF16)
                for cp in txt_copies(i):
                    cp.start()

            def image_y(i):
                at = pl.ds(pl.multiple_of(i * rows_i, 16), rows_i)
                if i < TURNS:

                    @pl.when(owned(i))
                    def _():
                        y_side(i).wait_send()

                    @pl.when(jnp.logical_not(owned(i)))
                    def _():
                        y_side(i).wait_recv()

                else:
                    y_side(i).wait()
                    y1_s[at, :] = (y1_s[at, :].astype(F32) + y2_s[at, :].astype(F32)).astype(BF16)
                for cp in img_copies(i):
                    cp.start()

        def last(i):
            swap(i, rc_s, K_C).wait()

            def body(at):
                grad = send_s[at, :].astype(F32) + rc_s[at, :].astype(F32)
                unit, inverse = unit_of(x_s[at, :].astype(F32))
                dx = (r_s[at, :] + norm_back(grad, unit, inverse, own_gain[0])).astype(BF16)
                if text:
                    rb_s[at, :] = dx
                else:
                    fin_s[at, :] = dx
                acc_s[0] += fold(grad * unit)
                acc_s[2] += fold(grad)

            by_strips(i, body)

            for cp in [dx_copies(i)] if text else img_copies(i):
                cp.start()

        if not text:
            for i in range(TURNS):
                y_share(i)
        def mixed_grads(part):
            def product(at):
                first = dot_tn(a1_s[part, at], dq_s[part, 0 : 2 * QKV])
                second = dot_tn(drb_s[part, at], o_s[part, :])

                def joined(s):
                    left, right = first[:, s * QKV : (s + 1) * QKV], second[:, s * MIX : (s + 1) * MIX]
                    seam = left[:, MIX * 2 :] + right[:, 0 : QKV - 2 * MIX]
                    return jnp.concatenate([left[:, : MIX * 2], seam, right[:, QKV - 2 * MIX :]], axis=1)

                return joined(0), joined(1)

            return product

        group = d if z_inside else 0

        def early_copy(k):
            return remote(early_s.at[0], eall_s.at[group], K_E, k - 1, adder(k, 0))

        def early_arrival(k):
            place = lax.rem(d + dp_size - k, dp_size)
            return remote(eall_s.at[place], eall_s.at[place], K_E, k - 1, adder(k, 0, True))

        early_sib = remote(early_s.at[1], esib_s, K_S, 1, sib)

        def early_start():
            sums = jnp.sum(acc_s[...], axis=1)
            for j, order in enumerate(((1, 3, 4, 5, 6, 7, 8, 9), (1, 3, 4, 5, 7, 6, 9, 8))):
                for row, src in enumerate(order):
                    early_s[j, row : row + 1, :] = sums[src : src + 1, :]
            early_sib.start()

        def early_next():
            early_sib.wait()
            early_s[0] = early_s[0] + esib_s[...]
            eall_s[group] = early_s[0]
            for k in range(1, groups):
                early_copy(k).start()

        def late_copy(k, j):
            return remote(late_s, lall_s.at[2 * group + core], K_V, 2 * k + j, adder(k, j))

        def late_arrival(k, j):
            place = 2 * (lax.rem(d + dp_size - k, dp_size) if k else group) + (1 - core if j else core)
            return remote(lall_s.at[place], lall_s.at[place], K_V, 2 * k + j, adder(k, j, True))

        def late_start():
            late_s[...] = jnp.zeros_like(late_s)
            for r, src in enumerate((0, 2)):
                row = jnp.sum(acc_s[src], axis=0, keepdims=True)
                for c in range(width // 128):
                    late_s[8 * r + c : 8 * r + c + 1, :] = row[:, c * 128 : (c + 1) * 128]
            for k, j in adders:
                late_copy(k, j).start()
            lall_s[2 * group + core] = late_s[...]

        def vectors_finish():
            for k in range(1, groups):
                early_copy(k).wait_send()
                early_arrival(k).wait_recv()
            for k, j in adders:
                late_copy(k, j).wait_send()
                late_arrival(k, j).wait_recv()
            early, late = eall_s[0], lall_s[0]
            for k in range(1, groups):
                early = early + eall_s[k]
            for k in range(1, 2 * groups):
                late = late + lall_s[k]
            vec_out[...] = jnp.zeros_like(vec_out)
            for row, dst in enumerate((1, 3, 4, 5, 6, 7, 8, 9)):
                vec_out[dst : dst + 1, :] = early[row : row + 1, :]
            for r, dst in enumerate((0, 2)):
                for c in range(width // 128):
                    vec_out[dst : dst + 1, c * 128 : (c + 1) * 128] = late[8 * r + c : 8 * r + c + 1, :]

        if text:

            def backward(i):
                @pl.when(i < CHUNKS)
                def _():
                    attend_back(i)

                @pl.when(i == 2)
                def _():
                    z_middle(2)

                @pl.when(i == 3)
                def _():
                    z_middle(1)

                @pl.when(i > 0)
                def _():
                    send_c(i - 1)

                @pl.when(i > 2)
                def _():
                    last(i - 3)

            loop(CHUNKS + 1, backward)
        else:

            def backward(i):
                @pl.when(i == 2)
                def _():
                    z_middle(2)

                @pl.when(i == 3)
                def _():
                    z_middle(1)

                attend_back(i)
                send_c(i)

                @pl.when(i == 2)
                def _():
                    grads_part(0, mixed_grads(parts[0]), True, False)

            loop(CHUNKS, backward)


        if text:
            for i in range(TURNS, CHUNKS):
                hand_on(i)
            for i in range(EARLY, CHUNKS):
                y_copies(i)[0].start()
        grads_part(0, mixed_grads(parts[1]), text, True)
        grads_sum(0)
        z_start(0)
        if z_inside:
            z_near(1, upper).start()
            z_near(0, upper).start()
        early_start()
        if text:
            last(CHUNKS - 2)
            last(CHUNKS - 1)
            early_next()
            z_middle(0)
            for i in range(TURNS):
                hand_on(i)
        else:
            for i in range(TURNS):
                y_sum(i)
            loop(2, last)
            early_next()
            z_middle(0)
            last(CHUNKS - 2)
            loop(CHUNKS, dx_hand_on)
            last(CHUNKS - 1)

        late_start()
        if text:
            loop(CHUNKS, own_y)
        z_finish(2)
        z_finish(1)
        if text:
            for i in range(CHUNKS):
                image_y(i)
        z_finish(0)
        vectors_finish()

        def finish(i):
            if text:
                dy_to_image(i).wait_send()
                dx_copies(i).wait_send()
                here, there = txt_copies(i)
                here.wait()
                there.wait()
            else:
                x_to_text(i).wait_send()
                if i < TURNS:

                    @pl.when(owned(i))
                    def _():
                        y_copies(i)[0].wait_send()

                    @pl.when(jnp.logical_not(owned(i)))
                    def _():
                        y_side(i).wait_send()

                else:
                    y_copies(i)[0].wait_send()
                for cp in dx_relay(i):
                    cp.wait()
            here, there = img_copies(i)
            here.wait()
            there.wait()

        for i in range(CHUNKS):
            finish(i)
        for a in range(3):
            z_end(a)

    @pl.when(image_here)
    def _():
        one_layer(False)

    @pl.when(jnp.logical_not(image_here))
    def _():
        one_layer(True)


def finish_kernel(
    images, keys_i, rows_i, img_in, txt_in, g_x, g_u, g_d, vec,
    img_out, txt_out, gains, shifts, qkv, bias_qv, proj, outb, up, bias_up, down,
    buf, out_s, gx_s, qkv_s, txt_s, gu_s, gd_s, sem,
):
    plain = [(g_u, gu_s, up), (g_d, gd_s, down), (txt_in, txt_s, txt_out)]
    fetch = [pltpu.make_async_copy(src, mid, sem.at[k]) for k, (src, mid, dst) in enumerate(plain)]
    copies = [pltpu.make_async_copy(mid, dst, sem.at[5 + k]) for k, (src, mid, dst) in enumerate(plain)]
    gx_in = pltpu.make_async_copy(g_x, gx_s, sem.at[3])
    gx_in.start()
    blocks = [(o, min(STEP, rows_i - o)) for o in range(0, rows_i, STEP)]
    loads = [
        pltpu.make_async_copy(img_in.at[:, o : o + n], buf.at[:, o : o + n], sem.at[8 + k])
        for k, (o, n) in enumerate(blocks)
    ]
    for cp in loads:
        cp.start()
    for cp in fetch:
        cp.start()
    gains[...] = vec[0:2, :]
    shifts[...] = vec[2:4, :]
    outb[...] = vec[4:6, :]
    bias_up[...] = vec[6:7, :]
    bias_qv[0:1, :] = vec[8:9, 0:WIDE]
    bias_qv[1:2, :] = vec[8:9, 2 * WIDE : 3 * WIDE]
    gx_in.wait()
    proj[...] = gx_s[:, 3 * WIDE :].T
    for k in range(3):
        qkv_s[k] = gx_s[:, k * WIDE : (k + 1) * WIDE]
    q_out = pltpu.make_async_copy(qkv_s, qkv, sem.at[4])
    q_out.start()
    stores = []
    for k, (o, n) in enumerate(blocks):
        loads[k].wait()
        rows = min(n, keys_i - o)
        value = jnp.swapaxes(buf[:, o : o + n, :].astype(F32), 0, 1)
        out_s[o : o + n] = value.astype(BF16)
        cp = pltpu.make_async_copy(out_s.at[o : o + rows], img_out.at[o : o + rows], sem.at[16 + k])
        cp.start()
        stores.append(cp)
        if k < len(fetch):
            fetch[k].wait()
            copies[k].start()
    for cp in copies + [q_out] + stores:
        cp.wait()


def finish_outputs(images, keys_i, rows_i, img_out, txt_out, g_x, g_u, g_d, vec):
    share, width = g_x.shape
    sds, v = jax.ShapeDtypeStruct, pltpu.VMEM
    any_spec, vmem_spec = pl.BlockSpec(memory_space=pl.ANY), pl.BlockSpec(memory_space=pltpu.VMEM)
    outs = [
        (sds((keys_i, images, width), BF16), any_spec),
        (sds(txt_out.shape, BF16), any_spec),
        (sds((2, width), F32), vmem_spec),
        (sds((2, width), F32), vmem_spec),
        (sds((3, share, WIDE), F32), any_spec),
        (sds((2, WIDE), F32), vmem_spec),
        (sds((WIDE, share), F32), vmem_spec),
        (sds((2, width), F32), vmem_spec),
        (sds((share, width), F32), any_spec),
        (sds((1, width), F32), vmem_spec),
        (sds((share, width), F32), any_spec),
    ]
    img, txt, gains, shifts, qkv, bias_qv, proj, outb, up, bias_up, down = pl.pallas_call(
        partial(finish_kernel, images, keys_i, rows_i),
        out_shape=[o[0] for o in outs],
        in_specs=[any_spec] * 5 + [vmem_spec],
        out_specs=[o[1] for o in outs],
        scratch_shapes=[
            v((images, rows_i, width), BF16), v((rows_i, images, width), BF16), v((share, width), F32),
            v((3, share, WIDE), F32), v(txt_out.shape, BF16), v((share, width), F32), v((share, width), F32),
            pltpu.SemaphoreType.DMA((24,)),
        ],
        compiler_params=pltpu.CompilerParams(vmem_limit_bytes=60 << 20),
    )(img_out.reshape(images, rows_i, width), txt_out, g_x, g_u, g_d, vec)
    return (
        jnp.transpose(img, (1, 0, 2))[None], txt.reshape(2, -1, width)[None], gains[None], shifts[None],
        jnp.transpose(qkv, (1, 0, 2))[None], bias_qv[None], proj[None], outb[None], up[None], bias_up, down.T[None],
    )


def per_device(
    image_side, text_side, caption_lengths, norm_gains, norm_shifts, w_qkv, bias_qv, w_proj, out_bias, w_up, bias_up, w_down,
):
    dp_size = lax.axis_size("dp")
    core = lax.rem(lax.axis_index("tensor"), 2)
    images, keys_i, width = image_side.shape[1:]
    blocks, length = text_side.shape[1:3]
    per_core = images // 2
    rows_i = -(-(per_core // CHUNKS * keys_i) // 16) * 16
    rows_t = length * (blocks // 2) // CHUNKS
    share = width // dp_size
    z_inside = dp_size == 4 and share % 16 == 0

    img = lax.dynamic_slice_in_dim(image_side[0], core * per_core, per_core, 0)
    img = jnp.pad(img, ((0, 0), (0, rows_i - keys_i), (0, 0))).reshape(per_core * rows_i, width)
    wq = jnp.transpose(w_qkv[0], (1, 2, 0)).reshape(3 * WIDE, width)
    n_i, n_t = rows_i * CHUNKS, rows_t * CHUNKS
    columns = (width, width, width)
    sds = jax.ShapeDtypeStruct
    grad_type = (lambda w: sds((share, w), F32)) if z_inside else (lambda w: sds((width, w), BF16))
    outs = [sds((2 * n_i, width), BF16), sds((2 * n_t, width), BF16)]
    outs += [grad_type(w) for w in columns] + [sds((16, width), F32)]
    any_spec, vmem_spec = pl.BlockSpec(memory_space=pl.ANY), pl.BlockSpec(memory_space=pltpu.VMEM)
    v = pltpu.VMEM
    scratch = [
        v((n_i, width), BF16), v((n_i, width), BF16),
        v((2 * QKV, width), BF16), v((2 * MIX, width), BF16), v((width, 2 * width), BF16), v((2 * width, width), BF16),
        v((2, 8, width + QKV), F32), v((8, n_t + 2 * rows_t), jnp.int32),
        v((n_i, width), BF16), v((max(n_i, n_t + 2 * rows_t), 2 * QKV), BF16), v((n_i, 2 * MIX), BF16), v((n_i, width), F32),
        v((n_i, width), BF16), v((n_i, 2 * width), BF16), v((n_i, 2 * width), BF16),
        v((CHUNKS * HEADS, max(-(-rows_i // 128) * rows_i, 3 * rows_t // 128 * rows_t), 128), F32),
        v((n_t + 2 * rows_t, 2 * HEADS * HEAD), F32), v((max(rows_i, rows_t), 2 * MIX), BF16),
        v((n_i, width), BF16), v((n_i, width), BF16), v((n_i, width), BF16), v((n_i, width), BF16),
        v((n_i, width), BF16), v((n_t, width), BF16), v((n_i, width), BF16), v((n_i, width), BF16), v((n_i, width), BF16),
        v((16, 8, width), F32), v((2, 8, width), F32), v((8, width), F32), v((dp_size if z_inside else 1, 8, width), F32),
        v((16, 128), F32), v((2 * dp_size if z_inside else 2, 16, 128), F32),
    ]
    scratch += [v((2, width, width), BF16)]
    scratch += [v((width, w), BF16) for w in columns] + [v((width, w), BF16) for w in columns]
    if z_inside:
        scratch += [v((3, 2, share, width), BF16), v((3, share, width), BF16), v((3, share, width), F32)]
    dma = pltpu.SemaphoreType.DMA
    scratch += [dma((4 * N_KINDS,)), dma((4 * N_KINDS,)), dma((24,))]
    img_out, txt_out, g_x, g_u, g_d, vec = pl.pallas_call(
        partial(layers_kernel, rows_i, rows_t, keys_i, dp_size, z_inside),
        out_shape=outs,
        in_specs=[any_spec] * 6 + [pl.BlockSpec(memory_space=pltpu.SMEM)] + [vmem_spec] * 5,
        out_specs=[any_spec] * 5 + [vmem_spec],
        scratch_shapes=scratch,
        compiler_params=pltpu.CompilerParams(collective_id=0, has_side_effects=True, vmem_limit_bytes=60 << 20),
    )(
        img, text_side[0], wq, w_proj[0], w_up[0], w_down[0], caption_lengths,
        norm_gains[0], norm_shifts[0], out_bias[0], bias_up, bias_qv[0],
    )
    if z_inside:
        return finish_outputs(images, keys_i, rows_i, img_out, txt_out, g_x, g_u, g_d, vec)
    else:
        def scatter(grad):
            return lax.psum_scatter(grad, "dp", scatter_dimension=0, tiled=True).astype(F32)

        g_x, g_u, g_d = (scatter(g) for g in (g_x, g_u, g_d))
        vec = lax.psum(vec, "dp")
    image_result = img_out.reshape(images, rows_i, width)[:, :keys_i][None]
    text_result = txt_out.reshape(blocks, length, width)[None]
    return (
        image_result,
        text_result,
        vec[0:2][None],
        vec[2:4][None],
        g_x[:, : 3 * WIDE].reshape(share, 3, WIDE)[None],
        jnp.stack([vec[8, 0:WIDE], vec[8, 2 * WIDE : 3 * WIDE]])[None],
        g_x[:, 3 * WIDE :].T[None],
        vec[4:6][None],
        g_u[None],
        vec[6][None],
        g_d.T[None],
    )


def solution(mesh):
    placed = (
        P("pipe", "dp", None, None),
        P("pipe", "dp", None, None),
        P("dp", None),
        P("pipe", None, None),
        P("pipe", None, None),
        P("pipe", None, None, "tensor"),
        P("pipe", None, "tensor"),
        P("pipe", "tensor", None),
        P("pipe", None, None),
        P("pipe", None, "tensor"),
        P("pipe", "tensor"),
        P("pipe", "tensor", None),
    )
    return jax.shard_map(
        per_device,
        mesh=mesh,
        in_specs=placed,
        out_specs=(
            P("pipe", "dp", None, None),
            P("pipe", "dp", None, None),
            P("pipe", None, None),
            P("pipe", None, None),
            P("pipe", "dp", None, "tensor"),
            P("pipe", None, "tensor"),
            P("pipe", "tensor", "dp"),
            P("pipe", None, None),
            P("pipe", "dp", "tensor"),
            P("pipe", "tensor"),
            P("pipe", "tensor", "dp"),
        ),
        check_vma=False,
    )
```
